32 devices in a mesh: dp: 4 (over z), blk: 4 (over y, core), uly: 2 (over x).
Axes of the slice: x: 2, y: 2, z: 4, core: 2. Of those that a mesh axis runs over, the one named last changes fastest.
Arguments:
- layer_input: bfloat16 [4096, 2048], P(('dp', 'blk', 'uly')), may hold values from -16 to 16
- span_order: int32 [4, 8], P('dp'), may hold values from 0 to 7, each once within a row
- qkv_weight: bfloat16 [2048, 4096], P(('dp', 'blk', 'uly')), may hold values from -0.125 to 0.125
- out_weight: bfloat16 [2048, 2048], P(('dp', 'blk', 'uly')), may hold values from -1.5 to 1.5
- gate_up_weight: bfloat16 [2048, 2, 8192], P(('dp', 'blk'), None, 'uly'), may hold values from -0.125 to 0.125
- down_weight: bfloat16 [2048, 8192], P(('dp', 'blk'), 'uly'), may hold values from -0.0625 to 0.0625
- attn_gain: bfloat16 [2048], P(('dp', 'blk', 'uly')), may hold values from 0.099609375 to 1.8984375
- mlp_gain: bfloat16 [2048], P(('dp', 'blk', 'uly')), may hold values from 0.099609375 to 1.8984375
- output_cotangent: bfloat16 [4096, 2048], P(('dp', 'blk', 'uly')), may hold values from -6 to 6
Outputs:
- layer_output: bfloat16 [4096, 2048], P(('dp', 'blk', 'uly'))
- input_grad: float32 [4096, 2048], P(('dp', 'blk', 'uly'))
- qkv_grad: float32 [2048, 4096], P(('dp', 'blk', 'uly'))
- out_weight_grad: float32 [2048, 2048], P(('dp', 'blk', 'uly'))
- gate_up_grad: float32 [2048, 2, 8192], P(('dp', 'blk'), None, 'uly')
- down_grad: float32 [2048, 8192], P(('dp', 'blk'), 'uly')
- attn_gain_grad: float32 [2048], P(('dp', 'blk', 'uly'))
- mlp_gain_grad: float32 [2048], P(('dp', 'blk', 'uly'))
- rms_values: float32 [5], replicated
The draws below stay inside these ranges and needn't reach their ends.
Inputs may be any that keep to these rules, and one draw needn't show every extreme that they name: `span_order`: each row names each of the 8 position blocks of its sequence once.
All inputs are finite; a program needn't handle non-finite values.
Results may differ from the reference program's by a relative error of at most 0.023.
Values may be sent and summed in bfloat16 or wider, within the bound.
No kernel may reach another device: no remote copies, remote signals or barrier semaphores. Data moves between devices by JAX's collectives and lax.ppermute only.
A program may use at most 384 MiB of HBM per device.

```python
import math
from functools import partial
import jax
import jax.numpy as jnp
from jax import lax

D = 2048
H = 16
KV = 8
HD = 128
FF = 8192
SEQS = 4
LEN = 1024
SPANS = 8
SPAN = 128
TOKENS = 4096


def draw_layer_input(key, part):
    key = jax.random.fold_in(key, 11)
    first_key = jax.random.fold_in(key, 0)
    row_place = (jnp.arange(TOKENS, dtype=jnp.float32) / TOKENS)[:, None]
    growth = 0.4 * jnp.exp(row_place * jnp.log(6.0))
    base_draw = jax.random.truncated_normal(first_key, -6.0, 6.0, (TOKENS, D), jnp.float32)
    return (base_draw * growth).astype(jnp.bfloat16)


def block_scale(stream_key, extent, cuts, smallest, high):
    level, own = 1.0, jax.random.fold_in(stream_key, 6)
    for axis_at, blocks in cuts:
        heights = jnp.exp(jax.random.uniform(jax.random.fold_in(own, axis_at), (blocks,), jnp.float32, smallest / len(cuts), high / len(cuts)))
        level = level * jnp.repeat(heights, extent[axis_at] // blocks).reshape([-1 if axis == axis_at else 1 for axis in range(len(extent))])
    return level


def scatter_about(key, shape, deviation, reach, pieces=(), kind=jnp.bfloat16):
    level = block_scale(key, shape, pieces, -0.22, 0.18) if pieces else 1.0
    drawn = jax.random.normal(key, shape, jnp.float32) * deviation * level
    return jnp.minimum(jnp.maximum(drawn, -reach), reach).astype(kind)


def setup_inputs(seed: int = 0) -> dict:
    key_list = jax.random.split(jax.random.key(seed), 10)
    layer_input = draw_layer_input(jax.random.fold_in(key_list[9], 71), 0)
    span_order = jax.vmap(lambda own: jax.random.permutation(own, SPANS))(jax.random.split(key_list[1], SEQS)).reshape((SEQS, SPANS)).astype(jnp.int32)
    qkv_weight = scatter_about(key_list[2], (D, (H + 2 * KV) * HD), D ** -0.5, 0.125, ((0, 32),))
    out_weight = scatter_about(key_list[3], (D, H * HD), (max(1, D // 128)) ** -0.5, 1.5, ((0, 32),))
    gate_up_weight = scatter_about(key_list[4], (D, 2, FF), D ** -0.5, 0.125, ((0, 16), (2, 2)))
    down_weight = scatter_about(key_list[5], (D, FF), FF ** -0.5, 0.0625, ((0, 16), (1, 2)))
    attn_gain = jnp.clip(1.0 + 0.18 * jax.random.normal(key_list[6], (D,), jnp.float32), 0.099609375, 1.8984375).astype(jnp.bfloat16)
    mlp_gain = jnp.clip(1.0 + 0.18 * jax.random.normal(key_list[7], (D,), jnp.float32), 0.099609375, 1.8984375).astype(jnp.bfloat16)
    output_cotangent = scatter_about(key_list[8], (TOKENS, D), 1.0, 6.0, ((0, 32),))
    return {"layer_input": layer_input, "span_order": span_order, "qkv_weight": qkv_weight, "out_weight": out_weight, "gate_up_weight": gate_up_weight, "down_weight": down_weight, "attn_gain": attn_gain, "mlp_gain": mlp_gain, "output_cotangent": output_cotangent}


EPSILON = 1e-06
ROPE_BASE = 1000000.0
MASKED = -1e+30

@jax.custom_vjp
def low(v):
    return lax.optimization_barrier(v.astype(jnp.bfloat16)).astype(jnp.float32)

@jax.custom_vjp
def low_back(v):
    return v

def low_keep(v):
    return (low(v), None)

def low_pass(kept, grad):
    return (grad,)

def back_keep(v):
    return (v, None)

def back_low(kept, grad):
    return (low(grad),)
low.defvjp(low_keep, low_pass)
low_back.defvjp(back_keep, back_low)

def rms_scale(values, gain):
    return values * lax.rsqrt(lax.optimization_barrier(jnp.mean(values * values, axis=-1, keepdims=True)) + EPSILON) * gain

def rope_angles(positions):
    freq_index = jnp.arange(HD // 2, dtype=jnp.float32)
    inverse_freq = ROPE_BASE ** (-2.0 * freq_index / HD)
    return positions.astype(jnp.float32)[:, None] * inverse_freq[None, :]

def rotate_pairs(values, angles):
    half_size = values.shape[-1] // 2
    first_half = values[..., :half_size]
    second_half = values[..., half_size:]
    cosine = jnp.cos(angles)[:, None, :]
    sine = jnp.sin(angles)[:, None, :]
    return jnp.concatenate([first_half * cosine - second_half * sine, second_half * cosine + first_half * sine], axis=-1)

def sequence_positions(row_index, span_size, order_row):
    block_index = row_index // span_size
    picks = block_index[:, None] == jnp.arange(order_row.shape[0], dtype=jnp.int32)[None, :]
    chosen = lax.optimization_barrier(jnp.sum(jnp.where(picks, order_row[None, :], 0), axis=1)).astype(jnp.int32)
    return chosen * span_size + row_index % span_size

def sequence_attention(block_inputs):
    query_rows, key_rows, value_rows, positions = block_inputs
    group_size = H // KV
    key_wide = jnp.repeat(key_rows, group_size, axis=1)
    value_wide = jnp.repeat(value_rows, group_size, axis=1)
    block_rows = math.gcd(LEN, 512)
    block_count = LEN // block_rows
    query_blocks = query_rows.reshape(block_count, block_rows, H, HD)
    pos_blocks = positions.reshape(block_count, block_rows)

    def one_block(pair):
        query_block, pos_block = pair
        scores = jnp.einsum('rhd,phd->hrp', query_block, key_wide, precision=lax.Precision.HIGHEST) * HD ** (-0.5)
        scores = low_back(scores)
        allowed = (positions[None, :] <= pos_block[:, None])[None]
        scores = jnp.where(allowed, scores, MASKED)
        row_top = lax.optimization_barrier(jnp.max(scores, axis=-1, keepdims=True))
        weights = jnp.where(allowed, jnp.exp(scores - row_top), 0.0)
        row_total = lax.optimization_barrier(jnp.sum(weights, axis=-1, keepdims=True))
        soft_probs = low(weights / row_total)
        return jnp.einsum('hrp,phd->rhd', soft_probs, value_wide, precision=lax.Precision.HIGHEST)
    head_blocks = lax.map(jax.checkpoint(one_block), (query_blocks, pos_blocks))
    return head_blocks.reshape(LEN, H, HD)

def layer_forward(positions, layer_in, qkv_w, out_w, gate_up_w, down_w, attn_g, mlp_g):
    normed_attn = low(rms_scale(layer_in, attn_g))
    qkv_all = low_back(jnp.dot(normed_attn, qkv_w, precision=lax.Precision.HIGHEST))
    angles = rope_angles(positions)
    query_all = low_back(low(rotate_pairs(qkv_all[:, :H * HD].reshape(TOKENS, H, HD), angles)))
    key_all = low_back(low(rotate_pairs(qkv_all[:, H * HD:(H + KV) * HD].reshape(TOKENS, KV, HD), angles)))
    value_all = low_back(low(qkv_all[:, (H + KV) * HD:].reshape(TOKENS, KV, HD)))
    head_rows = lax.map(sequence_attention, (query_all.reshape(SEQS, LEN, H, HD), key_all.reshape(SEQS, LEN, KV, HD), value_all.reshape(SEQS, LEN, KV, HD), positions.reshape(SEQS, LEN)))
    head_rows = low_back(low(head_rows.reshape(TOKENS, H * HD)))
    attn_out = low_back(jnp.dot(head_rows, out_w.T, precision=lax.Precision.HIGHEST))
    middle = layer_in + attn_out
    normed_mlp = low(rms_scale(middle, mlp_g))
    gate_up = low_back(jnp.dot(normed_mlp, gate_up_w.reshape(D, 2 * FF), precision=lax.Precision.HIGHEST))
    hidden = low(jax.nn.silu(gate_up[:, :FF]) * gate_up[:, FF:])
    mlp_out = low_back(jnp.dot(hidden, down_w.T, precision=lax.Precision.HIGHEST))
    final_stream = middle + mlp_out
    squares = jnp.stack([jnp.sum(layer_in * layer_in), jnp.sum(attn_out * attn_out), jnp.sum(middle * middle), jnp.sum(mlp_out * mlp_out), jnp.sum(final_stream * final_stream)])
    return (final_stream, squares)

def reference(layer_input, span_order, qkv_weight, out_weight, gate_up_weight, down_weight, attn_gain, mlp_gain, output_cotangent):
    row_index = jnp.arange(LEN, dtype=jnp.int32)
    positions = jax.vmap(partial(sequence_positions, row_index, SPAN))(span_order).reshape(TOKENS)
    final_stream, pull_back, squares = jax.vjp(partial(layer_forward, positions), layer_input.astype(jnp.float32), qkv_weight.astype(jnp.float32), out_weight.astype(jnp.float32), gate_up_weight.astype(jnp.float32), down_weight.astype(jnp.float32), attn_gain.astype(jnp.float32), mlp_gain.astype(jnp.float32), has_aux=True)
    input_grad, qkv_grad, out_weight_grad, gate_up_grad, down_grad, attn_gain_grad, mlp_gain_grad = pull_back(output_cotangent.astype(jnp.float32))
    rms_values = jnp.sqrt(squares / (TOKENS * D))
    return (final_stream.astype(jnp.bfloat16), input_grad, qkv_grad, out_weight_grad, gate_up_grad, down_grad, attn_gain_grad, mlp_gain_grad, rms_values)
```

```python
import jax
import jax.numpy as jnp
from jax import lax
from jax.sharding import Mesh
from jax.sharding import PartitionSpec as P

D = 2048
H = 16
KV = 8
HD = 128


EPSILON = 1e-06
ROPE_BASE = 1000000.0
MASKED = -1e30


def rms_scale(values, gain):
    return values * lax.rsqrt(jnp.mean(values * values, axis=-1, keepdims=True) + EPSILON) * gain


def rope_angles(positions):
    freq_index = jnp.arange(HD // 2, dtype=jnp.float32)
    inverse_freq = ROPE_BASE ** (-2.0 * freq_index / HD)
    return positions.astype(jnp.float32)[:, None] * inverse_freq[None, :]


def rotate_pairs(values, angles):
    half_size = values.shape[-1] // 2
    first_half = values[..., :half_size]
    second_half = values[..., half_size:]
    cosine = jnp.cos(angles)[:, None, :]
    sine = jnp.sin(angles)[:, None, :]
    return jnp.concatenate(
        [first_half * cosine - second_half * sine, second_half * cosine + first_half * sine],
        axis=-1,
    )


def sequence_positions(row_index, span_size, order_row):
    block_index = row_index // span_size
    picks = block_index[:, None] == jnp.arange(order_row.shape[0], dtype=jnp.int32)[None, :]
    chosen = jnp.sum(jnp.where(picks, order_row[None, :], 0), axis=1)
    return chosen * span_size + row_index % span_size


def contract_rows(left_side, right_side):
    return lax.dot_general(
        left_side, right_side, (((0,), (0,)), ((), ())), preferred_element_type=jnp.float32
    )


def contract_cols(left_side, right_side):
    return lax.dot_general(
        left_side, right_side, (((1,), (1,)), ((), ())), preferred_element_type=jnp.float32
    )


def general_plan(
    layer_input,
    span_order,
    qkv_weight,
    out_weight,
    gate_up_weight,
    down_weight,
    attn_gain,
    mlp_gain,
    output_cotangent,
):
    tok_rows = layer_input.shape[0]
    uly_size = lax.axis_size("uly")
    blk_size = lax.axis_size("blk")
    group_rows = tok_rows * uly_size
    seq_rows = group_rows * blk_size
    span_size = group_rows // 2
    order_row = span_order[0]
    local_kv = KV // uly_size
    local_heads = H // uly_size
    group_size = H // KV
    ff_local = down_weight.shape[1]
    score_scale = HD ** (-0.5)
    token_start = (lax.axis_index("blk") * uly_size + lax.axis_index("uly")) * tok_rows
    token_pos = sequence_positions(
        token_start + jnp.arange(tok_rows, dtype=jnp.int32), span_size, order_row
    )
    token_angles = rope_angles(token_pos)
    query_pos = sequence_positions(
        lax.axis_index("blk") * group_rows + jnp.arange(group_rows, dtype=jnp.int32),
        span_size,
        order_row,
    )
    stream_in = layer_input.astype(jnp.float32)
    qkv_full, out_full, attn_gain_full, mlp_gain_full = (
        lax.all_gather(qkv_weight, ("dp", "blk", "uly"), axis=0, tiled=True),
        lax.all_gather(out_weight, ("dp", "blk", "uly"), axis=0, tiled=True),
        lax.all_gather(attn_gain, ("dp", "blk", "uly"), axis=0, tiled=True),
        lax.all_gather(mlp_gain, ("dp", "blk", "uly"), axis=0, tiled=True),
    )
    gate_up_cols, down_cols = (
        lax.all_gather(gate_up_weight, ("dp", "blk"), axis=0, tiled=True),
        lax.all_gather(down_weight, ("dp", "blk"), axis=0, tiled=True),
    )
    attn_gain_wide = attn_gain_full.astype(jnp.float32)
    mlp_gain_wide = mlp_gain_full.astype(jnp.float32)
    normed_attn = rms_scale(stream_in, attn_gain_wide).astype(jnp.bfloat16)
    qkv_all = jnp.dot(normed_attn, qkv_full, preferred_element_type=jnp.float32)
    query_tok = (
        rotate_pairs(qkv_all[:, : H * HD].reshape(tok_rows, H, HD), token_angles)
        .reshape(tok_rows, H * HD)
        .astype(jnp.bfloat16)
    )
    key_tok = (
        rotate_pairs(qkv_all[:, H * HD : (H + KV) * HD].reshape(tok_rows, KV, HD), token_angles)
        .reshape(tok_rows, KV * HD)
        .astype(jnp.bfloat16)
    )
    value_tok = qkv_all[:, (H + KV) * HD :].astype(jnp.bfloat16)
    query_grp, key_grp, value_grp = (
        lax.all_to_all(query_tok, "uly", split_axis=1, concat_axis=0, tiled=True),
        lax.all_to_all(key_tok, "uly", split_axis=1, concat_axis=0, tiled=True),
        lax.all_to_all(value_tok, "uly", split_axis=1, concat_axis=0, tiled=True),
    )
    query_four = query_grp.reshape(group_rows, local_kv, group_size, HD)
    key_whole, value_whole = (
        lax.all_gather(key_grp, "blk", axis=0, tiled=True),
        lax.all_gather(value_grp, "blk", axis=0, tiled=True),
    )
    block_count = seq_rows // group_rows

    def take_block(block_index):
        offset = block_index * group_rows
        key_block = lax.dynamic_slice_in_dim(key_whole, offset, group_rows, 0).reshape(
            group_rows, local_kv, HD
        )
        value_block = lax.dynamic_slice_in_dim(value_whole, offset, group_rows, 0).reshape(
            group_rows, local_kv, HD
        )
        key_pos = sequence_positions(
            offset + jnp.arange(group_rows, dtype=jnp.int32), span_size, order_row
        )
        return (offset, key_block, value_block, key_pos)

    def attend_step(block_index, running):
        top_run, total_run, acc_run = running
        offset, key_block, value_block, key_pos = take_block(block_index)
        scores = (
            jnp.einsum("rkgd,pkd->kgrp", query_four, key_block, preferred_element_type=jnp.float32)
            * score_scale
        )
        allowed = key_pos[None, :] <= query_pos[:, None]
        scores = jnp.where(allowed, scores, MASKED)
        top_new = jnp.maximum(top_run, jnp.max(scores, axis=-1))
        weights = jnp.where(allowed, jnp.exp(scores - top_new[..., None]), 0.0)
        shrink_factor = jnp.exp(top_run - top_new)
        total_new = total_run * shrink_factor + jnp.sum(weights, axis=-1)
        acc_new = acc_run * shrink_factor[..., None] + jnp.einsum(
            "kgrp,pkd->kgrd",
            weights.astype(jnp.bfloat16),
            value_block,
            preferred_element_type=jnp.float32,
        )
        return (top_new, total_new, acc_new)

    start_state = (
        jnp.full((local_kv, group_size, group_rows), MASKED, jnp.float32),
        jnp.zeros((local_kv, group_size, group_rows), jnp.float32),
        jnp.zeros((local_kv, group_size, group_rows, HD), jnp.float32),
    )
    top_end, total_end, acc_end = lax.fori_loop(0, block_count, attend_step, start_state)
    log_total = top_end + jnp.log(total_end)
    head_rows = jnp.transpose(acc_end / total_end[..., None], (2, 0, 1, 3))
    heads_group = head_rows.reshape(group_rows, local_heads * HD).astype(jnp.bfloat16)
    heads_tok = lax.all_to_all(heads_group, "uly", split_axis=0, concat_axis=1, tiled=True)
    attn_out = contract_cols(heads_tok, out_full)
    middle = stream_in + attn_out
    normed_mlp = rms_scale(middle, mlp_gain_wide).astype(jnp.bfloat16)
    normed_grp, cotangent_grp = (
        lax.all_gather(normed_mlp, "uly", axis=0, tiled=True),
        lax.all_gather(output_cotangent, "uly", axis=0, tiled=True),
    )
    gate_up = jnp.einsum(
        "rd,dcf->rcf", normed_grp, gate_up_cols, preferred_element_type=jnp.float32
    )
    gate_part = gate_up[:, 0, :]
    up_part = gate_up[:, 1, :]
    hidden = (jax.nn.silu(gate_part) * up_part).astype(jnp.bfloat16)
    mlp_part = contract_cols(hidden, down_cols)
    mlp_out = lax.psum_scatter(
        mlp_part.astype(jnp.bfloat16), "uly", scatter_dimension=0, tiled=True
    ).astype(jnp.float32)
    final_stream = middle + mlp_out
    local_squares = jnp.stack(
        [
            jnp.sum(stream_in * stream_in),
            jnp.sum(attn_out * attn_out),
            jnp.sum(middle * middle),
            jnp.sum(mlp_out * mlp_out),
            jnp.sum(final_stream * final_stream),
        ]
    )
    total_squares = lax.psum(local_squares, ("dp", "blk", "uly"))
    entry_count = tok_rows * lax.axis_size("dp") * blk_size * uly_size * D
    rms_values = jnp.sqrt(total_squares / entry_count)
    grad_hidden = jnp.dot(cotangent_grp, down_cols, preferred_element_type=jnp.float32)
    sigmoid_gate = jax.nn.sigmoid(gate_part)
    grad_gate = grad_hidden * up_part * sigmoid_gate * (1.0 + gate_part * (1.0 - sigmoid_gate))
    grad_up = grad_hidden * gate_part * sigmoid_gate
    grad_gate_up = jnp.stack([grad_gate, grad_up], axis=1).astype(jnp.bfloat16)
    grad_normed_part = jnp.einsum(
        "rcf,dcf->rd", grad_gate_up, gate_up_cols, preferred_element_type=jnp.float32
    )
    grad_normed_mlp = lax.psum_scatter(
        grad_normed_part.astype(jnp.bfloat16), "uly", scatter_dimension=0, tiled=True
    ).astype(jnp.float32)
    gate_term = jnp.einsum(
        "rd,rcf->dcf", normed_grp, grad_gate_up, preferred_element_type=jnp.float32
    ).reshape(lax.axis_size(("dp", "blk")) * gate_up_weight.shape[0], 2 * ff_local)
    mlp_grads = lax.psum_scatter(
        jnp.concatenate([gate_term, contract_rows(cotangent_grp, hidden)], axis=1).astype(
            jnp.bfloat16
        ),
        ("dp", "blk"),
        scatter_dimension=0,
        tiled=True,
    ).astype(jnp.float32)
    gate_up_grad = mlp_grads[:, : 2 * ff_local].reshape(mlp_grads.shape[0], 2, ff_local)
    down_grad = mlp_grads[:, 2 * ff_local :]
    mlp_value, mlp_pull = jax.vjp(rms_scale, middle, mlp_gain_wide)
    grad_middle_norm, mlp_gain_grad_full = mlp_pull(grad_normed_mlp)
    grad_middle = output_cotangent.astype(jnp.float32) + grad_middle_norm
    grad_attn_out = grad_middle.astype(jnp.bfloat16)
    grad_heads_tok = jnp.dot(grad_attn_out, out_full, preferred_element_type=jnp.float32).astype(
        jnp.bfloat16
    )
    out_weight_term = contract_rows(grad_attn_out, heads_tok)
    grad_heads = lax.all_to_all(grad_heads_tok, "uly", split_axis=1, concat_axis=0, tiled=True)
    grad_four = grad_heads.reshape(group_rows, local_kv, group_size, HD)
    row_delta = jnp.transpose(
        jnp.sum(grad_four.astype(jnp.float32) * head_rows, axis=-1), (1, 2, 0)
    )

    def backward_step(block_index, running):
        grad_query_run, grad_key_all, grad_value_all = running
        offset, key_block, value_block, key_pos = take_block(block_index)
        scores = (
            jnp.einsum("rkgd,pkd->kgrp", query_four, key_block, preferred_element_type=jnp.float32)
            * score_scale
        )
        allowed = key_pos[None, :] <= query_pos[:, None]
        soft_probs = jnp.where(
            allowed, jnp.exp(jnp.where(allowed, scores, MASKED) - log_total[..., None]), 0.0
        )
        grad_probs = jnp.einsum(
            "rkgd,pkd->kgrp", grad_four, value_block, preferred_element_type=jnp.float32
        )
        grad_scores = (soft_probs * (grad_probs - row_delta[..., None])).astype(jnp.bfloat16)
        grad_query_run = (
            grad_query_run
            + jnp.einsum(
                "kgrp,pkd->kgrd", grad_scores, key_block, preferred_element_type=jnp.float32
            )
            * score_scale
        )
        grad_key_block = (
            jnp.einsum(
                "kgrp,rkgd->pkd", grad_scores, query_four, preferred_element_type=jnp.float32
            )
            * score_scale
        ).reshape(group_rows, local_kv * HD)
        grad_value_block = jnp.einsum(
            "kgrp,rkgd->pkd",
            soft_probs.astype(jnp.bfloat16),
            grad_four,
            preferred_element_type=jnp.float32,
        ).reshape(group_rows, local_kv * HD)
        grad_key_all = lax.dynamic_update_slice_in_dim(grad_key_all, grad_key_block, offset, 0)
        grad_value_all = lax.dynamic_update_slice_in_dim(
            grad_value_all, grad_value_block, offset, 0
        )
        return (grad_query_run, grad_key_all, grad_value_all)

    back_state = (
        jnp.zeros((local_kv, group_size, group_rows, HD), jnp.float32),
        jnp.zeros((seq_rows, local_kv * HD), jnp.float32),
        jnp.zeros((seq_rows, local_kv * HD), jnp.float32),
    )
    grad_query_end, grad_key_whole, grad_value_whole = lax.fori_loop(
        0, block_count, backward_step, back_state
    )
    grad_key_own, grad_value_own = (
        lax.psum_scatter(
            grad_key_whole.astype(jnp.bfloat16), "blk", scatter_dimension=0, tiled=True
        ).astype(jnp.float32),
        lax.psum_scatter(
            grad_value_whole.astype(jnp.bfloat16), "blk", scatter_dimension=0, tiled=True
        ).astype(jnp.float32),
    )
    grad_query_rows = (
        jnp.transpose(grad_query_end, (2, 0, 1, 3))
        .reshape(group_rows, local_heads * HD)
        .astype(jnp.bfloat16)
    )
    grad_query_tok, grad_key_tok, grad_value_tok = (
        lax.all_to_all(grad_query_rows, "uly", split_axis=0, concat_axis=1, tiled=True),
        lax.all_to_all(
            grad_key_own.astype(jnp.bfloat16), "uly", split_axis=0, concat_axis=1, tiled=True
        ),
        lax.all_to_all(
            grad_value_own.astype(jnp.bfloat16), "uly", split_axis=0, concat_axis=1, tiled=True
        ),
    )
    back_angles = rope_angles(-token_pos)
    grad_query_plain = rotate_pairs(
        grad_query_tok.astype(jnp.float32).reshape(tok_rows, H, HD), back_angles
    ).reshape(tok_rows, H * HD)
    grad_key_plain = rotate_pairs(
        grad_key_tok.astype(jnp.float32).reshape(tok_rows, KV, HD), back_angles
    ).reshape(tok_rows, KV * HD)
    grad_qkv = jnp.concatenate(
        [grad_query_plain, grad_key_plain, grad_value_tok.astype(jnp.float32)], axis=1
    ).astype(jnp.bfloat16)
    grad_normed_attn = contract_cols(grad_qkv, qkv_full)
    qkv_term = contract_rows(normed_attn, grad_qkv)
    attn_value, attn_pull = jax.vjp(rms_scale, stream_in, attn_gain_wide)
    grad_input_norm, attn_gain_grad_full = attn_pull(grad_normed_attn)
    input_grad = grad_middle + grad_input_norm
    qkv_grad, out_weight_grad, attn_gain_grad, mlp_gain_grad = (
        lax.psum_scatter(qkv_term, ("dp", "blk", "uly"), scatter_dimension=0, tiled=True),
        lax.psum_scatter(out_weight_term, ("dp", "blk", "uly"), scatter_dimension=0, tiled=True),
        lax.psum_scatter(
            attn_gain_grad_full, ("dp", "blk", "uly"), scatter_dimension=0, tiled=True
        ),
        lax.psum_scatter(mlp_gain_grad_full, ("dp", "blk", "uly"), scatter_dimension=0, tiled=True),
    )
    return (
        final_stream.astype(jnp.bfloat16),
        input_grad,
        qkv_grad,
        out_weight_grad,
        gate_up_grad,
        down_grad,
        attn_gain_grad,
        mlp_gain_grad,
        rms_values,
    )


ALL_AXES = ("dp", "yy", "cc", "uly")
SIDE_AXES = ("yy", "uly")
SWAP = [(0, 1), (1, 0)]


def unit_scale(values):
    return lax.rsqrt(jnp.mean(values * values, axis=-1, keepdims=True) + EPSILON)


def norm_pull(values, scale, grad_scaled):
    return scale * grad_scaled - values * scale**3 * jnp.mean(
        grad_scaled * values, axis=-1, keepdims=True
    )


def exchange(values, axes):
    return lax.all_to_all(values, axes, split_axis=0, concat_axis=0, tiled=True)


def gather_rows(rows, axis_names):
    group = lax.axis_size(axis_names)
    copies = jnp.broadcast_to(rows[None], (group, *rows.shape)).reshape(-1, rows.shape[1])
    own = exchange(copies, axis_names)
    other = lax.ppermute(own, "cc", SWAP)
    return jnp.concatenate([own, other], axis=0)


def scatter_sum(partial, axis_names):
    group = lax.axis_size(axis_names)
    half = partial.shape[0] // 2
    arrived = lax.ppermute(partial[half:].astype(jnp.bfloat16), "cc", SWAP)
    mine = (partial[:half].astype(jnp.float32) + arrived.astype(jnp.float32)).astype(jnp.bfloat16)
    parts = exchange(mine, axis_names).reshape(group, half // group, -1)
    return jnp.sum(parts.astype(jnp.float32), axis=0)


def plane_plan(
    layer_input,
    span_order,
    qkv_weight,
    out_weight,
    gate_up_weight,
    down_weight,
    attn_gain,
    mlp_gain,
    output_cotangent,
):
    tok = layer_input.shape[0]
    nz = lax.axis_size("dp")
    ndev = lax.axis_size(ALL_AXES)
    plane = ndev // nz
    seq_rows = tok * plane
    span_size = seq_rows // span_order.shape[1]
    y_at, c_at, x_at = lax.axis_index("yy"), lax.axis_index("cc"), lax.axis_index("uly")
    group = H // KV
    q_cols, kv_cols = H * HD // plane, KV * HD // plane
    own_cols = q_cols + 2 * kv_cols
    d_rows = qkv_weight.shape[0]
    score_scale = HD ** (-0.5)

    gain_a = attn_gain.astype(jnp.float32)[:, None]
    folded = (qkv_weight.astype(jnp.float32) * gain_a).astype(jnp.bfloat16)
    cuts = [H * HD, (H + KV) * HD]
    by_group = jnp.concatenate(
        [part.reshape(d_rows, plane, -1) for part in jnp.split(folded, cuts, axis=1)], axis=2
    ).transpose(1, 0, 2)
    wq = exchange(
        jnp.broadcast_to(by_group[None], (nz, plane, d_rows, own_cols)).reshape(-1, own_cols),
        ALL_AXES,
    )
    out_by_group = out_weight.reshape(d_rows, plane, q_cols).transpose(1, 0, 2)
    wo = exchange(
        jnp.broadcast_to(out_by_group[None], (nz, plane, d_rows, q_cols)).reshape(-1, q_cols),
        ALL_AXES,
    )

    stream_in = layer_input.astype(jnp.float32)
    scale_a = unit_scale(stream_in)
    normed_all = gather_rows((stream_in * scale_a).astype(jnp.bfloat16), SIDE_AXES)

    mlp_rows, ff_local = down_weight.shape
    hgroups = nz * lax.axis_size("cc")
    hchunk = ff_local // hgroups
    gain_own = mlp_gain.astype(jnp.float32)[None, :]
    gain_peer = lax.ppermute(mlp_gain[None, :], "uly", SWAP).astype(jnp.float32)
    gain_m = jnp.where(
        x_at == 0,
        jnp.concatenate([gain_own, gain_peer], axis=1),
        jnp.concatenate([gain_peer, gain_own], axis=1),
    ).reshape(mlp_rows, 1)
    folded_gu = (gate_up_weight.astype(jnp.float32) * gain_m[:, :, None]).astype(jnp.bfloat16)
    mlp_w = jnp.concatenate([folded_gu, down_weight[:, None, :]], axis=1)
    mlp_w = mlp_w.reshape(mlp_rows, 3, hgroups, hchunk).transpose(2, 0, 1, 3)
    mlp_w = exchange(mlp_w.reshape(hgroups * mlp_rows, 3 * hchunk), ("dp", "cc"))
    mlp_w = lax.all_gather(mlp_w, SIDE_AXES, axis=0, tiled=True)
    half_d = hgroups * mlp_rows
    mlp_w = mlp_w.reshape(2, 2, half_d, 3, hchunk).transpose(3, 0, 2, 1, 4)
    mlp_w = mlp_w.reshape(3, 2 * half_d, 2 * hchunk)

    def to_split(rows):
        return rows.reshape(tok, nz, 2, 2, mlp_rows).transpose(0, 2, 1, 3, 4).reshape(tok, D)

    def from_split(rows):
        return rows.reshape(tok, 2, nz, 2, mlp_rows).transpose(0, 2, 1, 3, 4).reshape(tok, D)

    cot_all = gather_rows(to_split(output_cotangent), ("dp",))

    block = jnp.arange(plane, dtype=jnp.int32)
    core_of, y_of, x_of = (block // 4) ^ c_at, (block // 2) % 2, block % 2
    stored = (y_of * 2 + core_of) * 2 + x_of
    row_at = (stored[:, None] * tok + jnp.arange(tok, dtype=jnp.int32)[None, :]).reshape(-1)
    positions = sequence_positions(row_at, span_size, span_order[0])
    angles = rope_angles(positions)
    allowed = (positions[None, :] <= positions[:, None])[None]

    qkv = jnp.dot(normed_all, wq, preferred_element_type=jnp.float32)
    query = rotate_pairs(qkv[:, :q_cols].reshape(seq_rows, group, HD), angles).astype(jnp.bfloat16)
    key = rotate_pairs(qkv[:, None, q_cols : q_cols + kv_cols], angles)[:, 0].astype(jnp.bfloat16)
    value = qkv[:, q_cols + kv_cols :].astype(jnp.bfloat16)

    scores = jnp.einsum("rgd,pd->grp", query, key, preferred_element_type=jnp.float32) * score_scale
    scores = jnp.where(allowed, scores, MASKED)
    top = jnp.max(scores, axis=-1, keepdims=True)
    weights = jnp.where(allowed, jnp.exp(scores - top), 0.0)
    total = jnp.sum(weights, axis=-1, keepdims=True)
    probs = weights / total
    probs_low = probs.astype(jnp.bfloat16)
    heads_f = jnp.einsum("grp,pd->rgd", probs_low, value, preferred_element_type=jnp.float32)
    heads = heads_f.reshape(seq_rows, q_cols).astype(jnp.bfloat16)
    attn_out = scatter_sum(contract_cols(heads, wo), SIDE_AXES)

    middle = stream_in + attn_out
    scale_m = unit_scale(middle)
    zhat_all = gather_rows(to_split((middle * scale_m).astype(jnp.bfloat16)), ("dp",))
    gate = jnp.dot(zhat_all, mlp_w[0], preferred_element_type=jnp.float32)
    up = jnp.dot(zhat_all, mlp_w[1], preferred_element_type=jnp.float32)
    grad_hidden = jnp.dot(cot_all, mlp_w[2], preferred_element_type=jnp.float32)
    sig = jax.nn.sigmoid(gate)
    hidden = (gate * sig * up).astype(jnp.bfloat16)
    grad_gate = (grad_hidden * up * sig * (1.0 + gate * (1.0 - sig))).astype(jnp.bfloat16)
    grad_up = (grad_hidden * gate * sig).astype(jnp.bfloat16)
    grad_zhat = from_split(
        scatter_sum(contract_cols(grad_gate, mlp_w[0]) + contract_cols(grad_up, mlp_w[1]), ("dp",))
    )
    mlp_out = from_split(scatter_sum(contract_cols(hidden, mlp_w[2]), ("dp",)))
    final_stream = middle + mlp_out

    terms = jnp.stack(
        [
            contract_rows(zhat_all, grad_gate),
            contract_rows(zhat_all, grad_up),
            contract_rows(cot_all, hidden),
        ]
    ).astype(jnp.bfloat16)
    terms = terms.reshape(3, 2, half_d, 2, hchunk).transpose(1, 3, 2, 0, 4)
    terms = exchange(terms.reshape(4 * half_d, 3 * hchunk), SIDE_AXES)
    terms = jnp.sum(terms.reshape(4, half_d, 3 * hchunk).astype(jnp.float32), axis=0)
    terms = exchange(terms.astype(jnp.bfloat16), ("dp", "cc"))
    terms = terms.reshape(hgroups, mlp_rows, 3, hchunk).transpose(1, 2, 0, 3).astype(jnp.float32)
    terms = terms.reshape(mlp_rows, 3, ff_local)
    gate_up_grad = terms[:, :2] * gain_m[:, :, None]
    down_grad = terms[:, 2]
    gain_sum = jnp.sum(terms[:, :2] * gate_up_weight.astype(jnp.float32), axis=(1, 2))
    gain_halves = gain_sum.reshape(2, -1)
    gain_keep = jnp.where(x_at == 0, gain_halves[0], gain_halves[1])
    gain_send = jnp.where(x_at == 0, gain_halves[1], gain_halves[0])
    mlp_gain_grad = gain_keep + lax.ppermute(gain_send[None, :], "uly", SWAP)[0]

    cot = output_cotangent.astype(jnp.float32)
    grad_middle = cot + norm_pull(middle, scale_m, grad_zhat)
    grad_out_all = gather_rows(grad_middle.astype(jnp.bfloat16), SIDE_AXES)
    grad_heads = jnp.dot(grad_out_all, wo, preferred_element_type=jnp.float32).astype(jnp.bfloat16)
    out_term = contract_rows(grad_out_all, heads)
    grad_four = grad_heads.reshape(seq_rows, group, HD)
    row_delta = jnp.sum(grad_four.astype(jnp.float32) * heads_f, axis=-1).T
    grad_probs = jnp.einsum("rgd,pd->grp", grad_four, value, preferred_element_type=jnp.float32)
    grad_scores = (probs * (grad_probs - row_delta[..., None])).astype(jnp.bfloat16)
    grad_query = (
        jnp.einsum("grp,pd->rgd", grad_scores, key, preferred_element_type=jnp.float32)
        * score_scale
    )
    grad_key = (
        jnp.einsum("grp,rgd->pd", grad_scores, query, preferred_element_type=jnp.float32)
        * score_scale
    )
    grad_value = jnp.einsum("grp,rgd->pd", probs_low, grad_four, preferred_element_type=jnp.float32)
    grad_query, grad_key = (v.astype(jnp.bfloat16).astype(jnp.float32) for v in (grad_query, grad_key))
    grad_qkv = jnp.concatenate(
        [
            rotate_pairs(grad_query, -angles).reshape(seq_rows, q_cols),
            rotate_pairs(grad_key[:, None], -angles)[:, 0],
            grad_value,
        ],
        axis=1,
    ).astype(jnp.bfloat16)
    grad_xhat = scatter_sum(contract_cols(grad_qkv, wq), SIDE_AXES)
    input_grad = grad_middle + norm_pull(stream_in, scale_a, grad_xhat)
    qkv_term = contract_rows(normed_all, grad_qkv)

    qkv_sum = exchange(qkv_term.astype(jnp.bfloat16), ALL_AXES)
    qkv_sum = jnp.sum(qkv_sum.reshape(nz, plane, d_rows, own_cols).astype(jnp.float32), axis=0)
    qkv_sum = qkv_sum.transpose(1, 0, 2)
    qkv_sum = jnp.concatenate(
        [
            qkv_sum[:, :, :q_cols].reshape(d_rows, -1),
            qkv_sum[:, :, q_cols : q_cols + kv_cols].reshape(d_rows, -1),
            qkv_sum[:, :, q_cols + kv_cols :].reshape(d_rows, -1),
        ],
        axis=1,
    )
    qkv_grad = qkv_sum * gain_a
    attn_gain_grad = jnp.sum(qkv_sum * qkv_weight.astype(jnp.float32), axis=1)
    out_sum = exchange(out_term.astype(jnp.bfloat16), ALL_AXES)
    out_sum = jnp.sum(out_sum.reshape(nz, plane, d_rows, q_cols).astype(jnp.float32), axis=0)
    out_weight_grad = out_sum.transpose(1, 0, 2).reshape(d_rows, -1)

    squares = jnp.stack(
        [jnp.sum(v * v) for v in (stream_in, attn_out, middle, mlp_out, final_stream)]
    )
    lanes = jnp.zeros((1, 128), jnp.float32).at[0, :5].set(squares)
    gathered = exchange(jnp.broadcast_to(lanes, (ndev, 128)), ALL_AXES)
    rms_values = jnp.sqrt(jnp.sum(gathered, axis=0)[:5] / (tok * ndev * D))
    return (
        final_stream.astype(jnp.bfloat16),
        input_grad,
        qkv_grad,
        out_weight_grad,
        gate_up_grad,
        down_grad,
        attn_gain_grad,
        mlp_gain_grad,
        rms_values,
    )


def solution(mesh):
    sizes = dict(mesh.shape)
    if sizes["blk"] == 4 and sizes["uly"] == 2:
        mesh = Mesh(mesh.devices.reshape(sizes["dp"], 2, 2, 2), ALL_AXES)
        body, blk = plane_plan, ("yy", "cc")
    else:
        body, blk = general_plan, ("blk",)
    every = ("dp", *blk, "uly")
    rows = ("dp", *blk)
    return jax.shard_map(
        body,
        mesh=mesh,
        in_specs=(
            P(every, None),
            P("dp", None),
            P(every, None),
            P(every, None),
            P(rows, None, "uly"),
            P(rows, "uly"),
            P(every),
            P(every),
            P(every, None),
        ),
        out_specs=(
            P(every, None),
            P(every, None),
            P(every, None),
            P(every, None),
            P(rows, None, "uly"),
            P(rows, "uly"),
            P(every),
            P(every),
            P(),
        ),
        check_vma=False,
    )
```

```python
import functools

import jax
import jax.numpy as jnp
from jax import lax
from jax.experimental import pallas as pl
from jax.experimental.pallas import tpu as pltpu
from jax.sharding import Mesh
from jax.sharding import PartitionSpec as P

D = 2048
H = 16
KV = 8
HD = 128


EPSILON = 1e-06
ROPE_BASE = 1000000.0
MASKED = -1e30


def rms_scale(values, gain):
    return values * lax.rsqrt(jnp.mean(values * values, axis=-1, keepdims=True) + EPSILON) * gain


def rope_angles(positions):
    freq_index = jnp.arange(HD // 2, dtype=jnp.float32)
    inverse_freq = ROPE_BASE ** (-2.0 * freq_index / HD)
    return positions.astype(jnp.float32)[:, None] * inverse_freq[None, :]


def rotate_pairs(values, angles):
    half_size = values.shape[-1] // 2
    first_half = values[..., :half_size]
    second_half = values[..., half_size:]
    cosine = jnp.cos(angles)[:, None, :]
    sine = jnp.sin(angles)[:, None, :]
    return jnp.concatenate(
        [first_half * cosine - second_half * sine, second_half * cosine + first_half * sine],
        axis=-1,
    )


def sequence_positions(row_index, span_size, order_row):
    block_index = row_index // span_size
    picks = block_index[:, None] == jnp.arange(order_row.shape[0], dtype=jnp.int32)[None, :]
    chosen = jnp.sum(jnp.where(picks, order_row[None, :], 0), axis=1)
    return chosen * span_size + row_index % span_size


def contract_rows(left_side, right_side):
    return lax.dot_general(
        left_side, right_side, (((0,), (0,)), ((), ())), preferred_element_type=jnp.float32
    )


def contract_cols(left_side, right_side):
    return lax.dot_general(
        left_side, right_side, (((1,), (1,)), ((), ())), preferred_element_type=jnp.float32
    )


def general_plan(
    layer_input,
    span_order,
    qkv_weight,
    out_weight,
    gate_up_weight,
    down_weight,
    attn_gain,
    mlp_gain,
    output_cotangent,
):
    tok_rows = layer_input.shape[0]
    uly_size = lax.axis_size("uly")
    blk_size = lax.axis_size("blk")
    group_rows = tok_rows * uly_size
    seq_rows = group_rows * blk_size
    span_size = group_rows // 2
    order_row = span_order[0]
    local_kv = KV // uly_size
    local_heads = H // uly_size
    group_size = H // KV
    ff_local = down_weight.shape[1]
    score_scale = HD ** (-0.5)
    token_start = (lax.axis_index("blk") * uly_size + lax.axis_index("uly")) * tok_rows
    token_pos = sequence_positions(
        token_start + jnp.arange(tok_rows, dtype=jnp.int32), span_size, order_row
    )
    token_angles = rope_angles(token_pos)
    query_pos = sequence_positions(
        lax.axis_index("blk") * group_rows + jnp.arange(group_rows, dtype=jnp.int32),
        span_size,
        order_row,
    )
    stream_in = layer_input.astype(jnp.float32)
    qkv_full, out_full, attn_gain_full, mlp_gain_full = (
        lax.all_gather(qkv_weight, ("dp", "blk", "uly"), axis=0, tiled=True),
        lax.all_gather(out_weight, ("dp", "blk", "uly"), axis=0, tiled=True),
        lax.all_gather(attn_gain, ("dp", "blk", "uly"), axis=0, tiled=True),
        lax.all_gather(mlp_gain, ("dp", "blk", "uly"), axis=0, tiled=True),
    )
    gate_up_cols, down_cols = (
        lax.all_gather(gate_up_weight, ("dp", "blk"), axis=0, tiled=True),
        lax.all_gather(down_weight, ("dp", "blk"), axis=0, tiled=True),
    )
    attn_gain_wide = attn_gain_full.astype(jnp.float32)
    mlp_gain_wide = mlp_gain_full.astype(jnp.float32)
    normed_attn = rms_scale(stream_in, attn_gain_wide).astype(jnp.bfloat16)
    qkv_all = jnp.dot(normed_attn, qkv_full, preferred_element_type=jnp.float32)
    query_tok = (
        rotate_pairs(qkv_all[:, : H * HD].reshape(tok_rows, H, HD), token_angles)
        .reshape(tok_rows, H * HD)
        .astype(jnp.bfloat16)
    )
    key_tok = (
        rotate_pairs(qkv_all[:, H * HD : (H + KV) * HD].reshape(tok_rows, KV, HD), token_angles)
        .reshape(tok_rows, KV * HD)
        .astype(jnp.bfloat16)
    )
    value_tok = qkv_all[:, (H + KV) * HD :].astype(jnp.bfloat16)
    query_grp, key_grp, value_grp = (
        lax.all_to_all(query_tok, "uly", split_axis=1, concat_axis=0, tiled=True),
        lax.all_to_all(key_tok, "uly", split_axis=1, concat_axis=0, tiled=True),
        lax.all_to_all(value_tok, "uly", split_axis=1, concat_axis=0, tiled=True),
    )
    query_four = query_grp.reshape(group_rows, local_kv, group_size, HD)
    key_whole, value_whole = (
        lax.all_gather(key_grp, "blk", axis=0, tiled=True),
        lax.all_gather(value_grp, "blk", axis=0, tiled=True),
    )
    block_count = seq_rows // group_rows

    def take_block(block_index):
        offset = block_index * group_rows
        key_block = lax.dynamic_slice_in_dim(key_whole, offset, group_rows, 0).reshape(
            group_rows, local_kv, HD
        )
        value_block = lax.dynamic_slice_in_dim(value_whole, offset, group_rows, 0).reshape(
            group_rows, local_kv, HD
        )
        key_pos = sequence_positions(
            offset + jnp.arange(group_rows, dtype=jnp.int32), span_size, order_row
        )
        return (offset, key_block, value_block, key_pos)

    def attend_step(block_index, running):
        top_run, total_run, acc_run = running
        offset, key_block, value_block, key_pos = take_block(block_index)
        scores = (
            jnp.einsum("rkgd,pkd->kgrp", query_four, key_block, preferred_element_type=jnp.float32)
            * score_scale
        )
        allowed = key_pos[None, :] <= query_pos[:, None]
        scores = jnp.where(allowed, scores, MASKED)
        top_new = jnp.maximum(top_run, jnp.max(scores, axis=-1))
        weights = jnp.where(allowed, jnp.exp(scores - top_new[..., None]), 0.0)
        shrink_factor = jnp.exp(top_run - top_new)
        total_new = total_run * shrink_factor + jnp.sum(weights, axis=-1)
        acc_new = acc_run * shrink_factor[..., None] + jnp.einsum(
            "kgrp,pkd->kgrd",
            weights.astype(jnp.bfloat16),
            value_block,
            preferred_element_type=jnp.float32,
        )
        return (top_new, total_new, acc_new)

    start_state = (
        jnp.full((local_kv, group_size, group_rows), MASKED, jnp.float32),
        jnp.zeros((local_kv, group_size, group_rows), jnp.float32),
        jnp.zeros((local_kv, group_size, group_rows, HD), jnp.float32),
    )
    top_end, total_end, acc_end = lax.fori_loop(0, block_count, attend_step, start_state)
    log_total = top_end + jnp.log(total_end)
    head_rows = jnp.transpose(acc_end / total_end[..., None], (2, 0, 1, 3))
    heads_group = head_rows.reshape(group_rows, local_heads * HD).astype(jnp.bfloat16)
    heads_tok = lax.all_to_all(heads_group, "uly", split_axis=0, concat_axis=1, tiled=True)
    attn_out = contract_cols(heads_tok, out_full)
    middle = stream_in + attn_out
    normed_mlp = rms_scale(middle, mlp_gain_wide).astype(jnp.bfloat16)
    normed_grp, cotangent_grp = (
        lax.all_gather(normed_mlp, "uly", axis=0, tiled=True),
        lax.all_gather(output_cotangent, "uly", axis=0, tiled=True),
    )
    gate_up = jnp.einsum(
        "rd,dcf->rcf", normed_grp, gate_up_cols, preferred_element_type=jnp.float32
    )
    gate_part = gate_up[:, 0, :]
    up_part = gate_up[:, 1, :]
    hidden = (jax.nn.silu(gate_part) * up_part).astype(jnp.bfloat16)
    mlp_part = contract_cols(hidden, down_cols)
    mlp_out = lax.psum_scatter(
        mlp_part.astype(jnp.bfloat16), "uly", scatter_dimension=0, tiled=True
    ).astype(jnp.float32)
    final_stream = middle + mlp_out
    local_squares = jnp.stack(
        [
            jnp.sum(stream_in * stream_in),
            jnp.sum(attn_out * attn_out),
            jnp.sum(middle * middle),
            jnp.sum(mlp_out * mlp_out),
            jnp.sum(final_stream * final_stream),
        ]
    )
    total_squares = lax.psum(local_squares, ("dp", "blk", "uly"))
    entry_count = tok_rows * lax.axis_size("dp") * blk_size * uly_size * D
    rms_values = jnp.sqrt(total_squares / entry_count)
    grad_hidden = jnp.dot(cotangent_grp, down_cols, preferred_element_type=jnp.float32)
    sigmoid_gate = jax.nn.sigmoid(gate_part)
    grad_gate = grad_hidden * up_part * sigmoid_gate * (1.0 + gate_part * (1.0 - sigmoid_gate))
    grad_up = grad_hidden * gate_part * sigmoid_gate
    grad_gate_up = jnp.stack([grad_gate, grad_up], axis=1).astype(jnp.bfloat16)
    grad_normed_part = jnp.einsum(
        "rcf,dcf->rd", grad_gate_up, gate_up_cols, preferred_element_type=jnp.float32
    )
    grad_normed_mlp = lax.psum_scatter(
        grad_normed_part.astype(jnp.bfloat16), "uly", scatter_dimension=0, tiled=True
    ).astype(jnp.float32)
    gate_term = jnp.einsum(
        "rd,rcf->dcf", normed_grp, grad_gate_up, preferred_element_type=jnp.float32
    ).reshape(lax.axis_size(("dp", "blk")) * gate_up_weight.shape[0], 2 * ff_local)
    mlp_grads = lax.psum_scatter(
        jnp.concatenate([gate_term, contract_rows(cotangent_grp, hidden)], axis=1).astype(
            jnp.bfloat16
        ),
        ("dp", "blk"),
        scatter_dimension=0,
        tiled=True,
    ).astype(jnp.float32)
    gate_up_grad = mlp_grads[:, : 2 * ff_local].reshape(mlp_grads.shape[0], 2, ff_local)
    down_grad = mlp_grads[:, 2 * ff_local :]
    mlp_value, mlp_pull = jax.vjp(rms_scale, middle, mlp_gain_wide)
    grad_middle_norm, mlp_gain_grad_full = mlp_pull(grad_normed_mlp)
    grad_middle = output_cotangent.astype(jnp.float32) + grad_middle_norm
    grad_attn_out = grad_middle.astype(jnp.bfloat16)
    grad_heads_tok = jnp.dot(grad_attn_out, out_full, preferred_element_type=jnp.float32).astype(
        jnp.bfloat16
    )
    out_weight_term = contract_rows(grad_attn_out, heads_tok)
    grad_heads = lax.all_to_all(grad_heads_tok, "uly", split_axis=1, concat_axis=0, tiled=True)
    grad_four = grad_heads.reshape(group_rows, local_kv, group_size, HD)
    row_delta = jnp.transpose(
        jnp.sum(grad_four.astype(jnp.float32) * head_rows, axis=-1), (1, 2, 0)
    )

    def backward_step(block_index, running):
        grad_query_run, grad_key_all, grad_value_all = running
        offset, key_block, value_block, key_pos = take_block(block_index)
        scores = (
            jnp.einsum("rkgd,pkd->kgrp", query_four, key_block, preferred_element_type=jnp.float32)
            * score_scale
        )
        allowed = key_pos[None, :] <= query_pos[:, None]
        soft_probs = jnp.where(
            allowed, jnp.exp(jnp.where(allowed, scores, MASKED) - log_total[..., None]), 0.0
        )
        grad_probs = jnp.einsum(
            "rkgd,pkd->kgrp", grad_four, value_block, preferred_element_type=jnp.float32
        )
        grad_scores = (soft_probs * (grad_probs - row_delta[..., None])).astype(jnp.bfloat16)
        grad_query_run = (
            grad_query_run
            + jnp.einsum(
                "kgrp,pkd->kgrd", grad_scores, key_block, preferred_element_type=jnp.float32
            )
            * score_scale
        )
        grad_key_block = (
            jnp.einsum(
                "kgrp,rkgd->pkd", grad_scores, query_four, preferred_element_type=jnp.float32
            )
            * score_scale
        ).reshape(group_rows, local_kv * HD)
        grad_value_block = jnp.einsum(
            "kgrp,rkgd->pkd",
            soft_probs.astype(jnp.bfloat16),
            grad_four,
            preferred_element_type=jnp.float32,
        ).reshape(group_rows, local_kv * HD)
        grad_key_all = lax.dynamic_update_slice_in_dim(grad_key_all, grad_key_block, offset, 0)
        grad_value_all = lax.dynamic_update_slice_in_dim(
            grad_value_all, grad_value_block, offset, 0
        )
        return (grad_query_run, grad_key_all, grad_value_all)

    back_state = (
        jnp.zeros((local_kv, group_size, group_rows, HD), jnp.float32),
        jnp.zeros((seq_rows, local_kv * HD), jnp.float32),
        jnp.zeros((seq_rows, local_kv * HD), jnp.float32),
    )
    grad_query_end, grad_key_whole, grad_value_whole = lax.fori_loop(
        0, block_count, backward_step, back_state
    )
    grad_key_own, grad_value_own = (
        lax.psum_scatter(
            grad_key_whole.astype(jnp.bfloat16), "blk", scatter_dimension=0, tiled=True
        ).astype(jnp.float32),
        lax.psum_scatter(
            grad_value_whole.astype(jnp.bfloat16), "blk", scatter_dimension=0, tiled=True
        ).astype(jnp.float32),
    )
    grad_query_rows = (
        jnp.transpose(grad_query_end, (2, 0, 1, 3))
        .reshape(group_rows, local_heads * HD)
        .astype(jnp.bfloat16)
    )
    grad_query_tok, grad_key_tok, grad_value_tok = (
        lax.all_to_all(grad_query_rows, "uly", split_axis=0, concat_axis=1, tiled=True),
        lax.all_to_all(
            grad_key_own.astype(jnp.bfloat16), "uly", split_axis=0, concat_axis=1, tiled=True
        ),
        lax.all_to_all(
            grad_value_own.astype(jnp.bfloat16), "uly", split_axis=0, concat_axis=1, tiled=True
        ),
    )
    back_angles = rope_angles(-token_pos)
    grad_query_plain = rotate_pairs(
        grad_query_tok.astype(jnp.float32).reshape(tok_rows, H, HD), back_angles
    ).reshape(tok_rows, H * HD)
    grad_key_plain = rotate_pairs(
        grad_key_tok.astype(jnp.float32).reshape(tok_rows, KV, HD), back_angles
    ).reshape(tok_rows, KV * HD)
    grad_qkv = jnp.concatenate(
        [grad_query_plain, grad_key_plain, grad_value_tok.astype(jnp.float32)], axis=1
    ).astype(jnp.bfloat16)
    grad_normed_attn = contract_cols(grad_qkv, qkv_full)
    qkv_term = contract_rows(normed_attn, grad_qkv)
    attn_value, attn_pull = jax.vjp(rms_scale, stream_in, attn_gain_wide)
    grad_input_norm, attn_gain_grad_full = attn_pull(grad_normed_attn)
    input_grad = grad_middle + grad_input_norm
    qkv_grad, out_weight_grad, attn_gain_grad, mlp_gain_grad = (
        lax.psum_scatter(qkv_term, ("dp", "blk", "uly"), scatter_dimension=0, tiled=True),
        lax.psum_scatter(out_weight_term, ("dp", "blk", "uly"), scatter_dimension=0, tiled=True),
        lax.psum_scatter(
            attn_gain_grad_full, ("dp", "blk", "uly"), scatter_dimension=0, tiled=True
        ),
        lax.psum_scatter(mlp_gain_grad_full, ("dp", "blk", "uly"), scatter_dimension=0, tiled=True),
    )
    return (
        final_stream.astype(jnp.bfloat16),
        input_grad,
        qkv_grad,
        out_weight_grad,
        gate_up_grad,
        down_grad,
        attn_gain_grad,
        mlp_gain_grad,
        rms_values,
    )


ALL_AXES = ("dp", "yy", "cc", "uly")
SIDE_AXES = ("yy", "uly")
PLANE_AXES = ("yy", "cc", "uly")
GROUP_AXES = ("dp", "cc")
SWAP = [(0, 1), (1, 0)]
DIAGONAL = [(0, 3), (1, 2), (2, 1), (3, 0)]
VMEM_SPEC = pl.BlockSpec(memory_space=pltpu.VMEM)
KERNEL = dict(
    compiler_params=pltpu.CompilerParams(vmem_limit_bytes=58 * 1024 * 1024),
    cost_estimate=pl.CostEstimate(flops=1000, bytes_accessed=1000, transcendentals=0),
)
ROWS = 256
BY_ROWS = (((0,), (0,)), ((), ()))
BY_COLS = (((1,), (1,)), ((), ()))
PLAIN = (((1,), (0,)), ((), ()))


def wide(values):
    return values.astype(jnp.float32)


def low(values):
    return values.astype(jnp.bfloat16)


def dot32(left, right, dims=PLAIN):
    return lax.dot_general(left, right, dims, preferred_element_type=jnp.float32)


def low_shape(rows, cols):
    return jax.ShapeDtypeStruct((rows, cols), jnp.bfloat16)


def wide_shape(rows, cols):
    return jax.ShapeDtypeStruct((rows, cols), jnp.float32)


def once(shape):
    return pl.BlockSpec(shape, lambda *i: (0,) * len(shape), pipeline_mode=pl.Buffered(1))


def row_block(step):
    return pl.ds(pl.multiple_of(step * ROWS, ROWS), ROWS)


def head_cut(head):
    return slice(head * HD, (head + 1) * HD)


def join_rows(pieces, out):
    rows = pieces[0].shape[0]
    for number, piece in enumerate(pieces):
        out[number * rows : (number + 1) * rows, :] = piece[...]


def turn(values, cosine, sine):
    return values * cosine + pltpu.roll(values, HD // 2, 1) * sine


def softmax_rows(query, key, key_pos, query_pos):
    scores = dot32(query, key, BY_COLS) * HD ** (-0.5)
    allowed = key_pos <= query_pos
    scores = jnp.where(allowed, scores, MASKED)
    top = jnp.max(scores, axis=1, keepdims=True)
    weights = jnp.where(allowed, jnp.exp(scores - top), 0.0)
    return weights / jnp.sum(weights, axis=1, keepdims=True)


def attention_forward_body(group, weight, cosine, sine, pos_col, pos_row, *refs):
    pieces, (query_out, key_out, value_out, heads_out, normed) = refs[:-5], refs[-5:]
    join_rows(pieces, normed)
    steps = normed.shape[0] // ROWS

    def project(step, carry):
        at = row_block(step)
        qkv = dot32(normed[at, :], weight[...])
        for head in range(group):
            turned = turn(qkv[:, head_cut(head)], cosine[at, :], sine[at, :])
            query_out[at, head_cut(head)] = low(turned)
        key_out[at, :] = low(turn(qkv[:, head_cut(group)], cosine[at, :], sine[at, :]))
        value_out[at, :] = low(qkv[:, head_cut(group + 1)])
        return carry

    def attend(step, carry):
        at = row_block(step)
        for head in range(group):
            probs = softmax_rows(
                query_out[at, head_cut(head)], key_out[...], pos_row[...], pos_col[at, :]
            )
            heads_out[at, head_cut(head)] = low(dot32(low(probs), value_out[...]))
        return carry

    lax.fori_loop(0, steps, project, 0)
    lax.fori_loop(0, steps, attend, 0)


def attention_forward(pieces, weight, cosine, sine, positions):
    rows, group = positions.shape[0], weight.shape[1] // HD - 2
    return pl.pallas_call(
        functools.partial(attention_forward_body, group),
        out_shape=(
            low_shape(rows, group * HD),
            low_shape(rows, HD),
            low_shape(rows, HD),
            low_shape(rows, group * HD),
        ),
        in_specs=[VMEM_SPEC] * (5 + len(pieces)),
        out_specs=(VMEM_SPEC,) * 4,
        scratch_shapes=[pltpu.VMEM((rows, weight.shape[0]), jnp.bfloat16)],
        name="attention_forward",
        **KERNEL,
    )(weight, cosine, sine, positions[:, None], positions[None, :], *pieces)


def attention_backward_body(group, weight, query, key, value, cosine, sine, pos_col, pos_row, *refs):
    pieces, (grad_qkv, grad_out, key_sum, value_sum) = refs[:-4], refs[-4:]
    join_rows(pieces, grad_out)
    steps = query.shape[0] // ROWS
    key_sum[...] = jnp.zeros_like(key_sum)
    value_sum[...] = jnp.zeros_like(value_sum)

    def block(step, carry):
        at = row_block(step)
        grad_heads = low(dot32(grad_out[at, :], weight[...]))
        for head in range(group):
            cut = head_cut(head)
            probs = softmax_rows(query[at, cut], key[...], pos_row[...], pos_col[at, :])
            grad_probs = dot32(grad_heads[:, cut], value[...], BY_COLS)
            delta = jnp.sum(probs * grad_probs, axis=1, keepdims=True)
            grad_scores = low(probs * (grad_probs - delta))
            grad_query = wide(low(dot32(grad_scores, key[...]) * HD ** (-0.5)))
            grad_qkv[at, cut] = low(turn(grad_query, cosine[at, :], -sine[at, :]))
            key_sum[...] += dot32(grad_scores, query[at, cut], BY_ROWS)
            value_sum[...] += dot32(low(probs), grad_heads[:, cut], BY_ROWS)
        return carry

    def finish(step, carry):
        at = row_block(step)
        grad_key = wide(low(key_sum[at, :] * HD ** (-0.5)))
        grad_qkv[at, head_cut(group)] = low(turn(grad_key, cosine[at, :], -sine[at, :]))
        grad_qkv[at, head_cut(group + 1)] = low(value_sum[at, :])
        return carry

    lax.fori_loop(0, steps, block, 0)
    lax.fori_loop(0, steps, finish, 0)


def attention_backward(pieces, weight, query, key, value, cosine, sine, positions):
    rows, group = query.shape[0], query.shape[1] // HD
    return pl.pallas_call(
        functools.partial(attention_backward_body, group),
        out_shape=low_shape(rows, (group + 2) * HD),
        in_specs=[VMEM_SPEC] * (8 + len(pieces)),
        out_specs=VMEM_SPEC,
        scratch_shapes=[pltpu.VMEM((rows, weight.shape[0]), jnp.bfloat16)]
        + [pltpu.VMEM((rows, HD), jnp.float32)] * 2,
        name="attention_backward",
        **KERNEL,
    )(weight, query, key, value, cosine, sine, positions[:, None], positions[None, :], *pieces)


def halves_specs(steps, rows, cols):
    half = steps // 2
    return (
        pl.BlockSpec((rows, cols), lambda i: (jnp.minimum(i, half - 1), 0)),
        pl.BlockSpec((rows, cols), lambda i: (jnp.maximum(i - half, 0), 0)),
    )


def store_half(first, second, values):
    step, half = pl.program_id(0), pl.num_programs(0) // 2

    @pl.when(step < half)
    def _():
        first[...] = values

    @pl.when(step >= half)
    def _():
        second[...] = values


def by_cols_body(parts, rows, weight, first, second):
    depth, chunk = weight.shape[0] // parts**2, weight.shape[1]
    out = []
    for y in range(parts):
        total = 0.0
        for x in range(parts):
            at = (y * parts + x) * depth
            cut = slice(x * chunk, (x + 1) * chunk)
            total += dot32(rows[:, cut], weight[at : at + depth, :], BY_COLS)
        out.append(low(total))
    store_half(first, second, out[0] if parts == 1 else jnp.concatenate(out, axis=1))


def by_cols_pass(rows, weight, parts, name):
    count, width = rows.shape[0], weight.shape[0] // parts
    steps = count // ROWS
    return pl.pallas_call(
        functools.partial(by_cols_body, parts),
        grid=(steps,),
        out_shape=(low_shape(count // 2, width),) * 2,
        in_specs=[pl.BlockSpec((ROWS, rows.shape[1]), lambda i: (i, 0)), once(weight.shape)],
        out_specs=halves_specs(steps, ROWS, width),
        name=name,
        **KERNEL,
    )(rows, weight)


def square_dot(rows, weight):
    depth = weight.shape[0] // 4
    near, far = rows[:, :depth], rows[:, depth:]
    out = [
        dot32(near, weight[x * depth : (x + 1) * depth, :])
        + dot32(far, weight[(2 + x) * depth : (3 + x) * depth, :])
        for x in (0, 1)
    ]
    return jnp.concatenate(out, axis=1)


def hidden_body(gate_w, up_w, *refs):
    normed_p, (hidden_out, gate_slope, up_slope, normed) = refs[:-4], refs[-4:]

    @pl.when(pl.program_id(0) == 0)
    def _():
        join_rows(normed_p, normed)

    rows = normed[row_block(pl.program_id(0)), :]
    gate, up = square_dot(rows, gate_w), square_dot(rows, up_w)
    sig = jax.nn.sigmoid(gate)
    hidden_out[...] = low(gate * sig * up)
    gate_slope[...] = low(up * sig * (1.0 + gate * (1.0 - sig)))
    up_slope[...] = low(gate * sig)


def hidden_pass(normed_p, gate_w, up_w):
    rows, width = len(normed_p) * normed_p[0].shape[0], normed_p[0].shape[1]
    units = 2 * gate_w.shape[1]
    by_rows = pl.BlockSpec((ROWS, units), lambda i: (i, 0))
    return pl.pallas_call(
        hidden_body,
        grid=(rows // ROWS,),
        out_shape=(low_shape(rows, units),) * 3,
        in_specs=[once(v.shape) for v in (gate_w, up_w, *normed_p)],
        out_specs=(by_rows,) * 3,
        scratch_shapes=[pltpu.VMEM((rows, width), jnp.bfloat16)],
        name="hidden_pass",
        **KERNEL,
    )(gate_w, up_w, *normed_p)


def grad_hidden_body(gate_w, up_w, down_w, gate_slope, up_slope, *refs):
    cot_p, (grad_gate, grad_up, first, second, cot) = refs[:-5], refs[-5:]

    @pl.when(pl.program_id(0) == 0)
    def _():
        join_rows(cot_p, cot)

    grad_hidden = square_dot(cot[row_block(pl.program_id(0)), :], down_w)
    grad_gate[...] = low(grad_hidden * wide(gate_slope[...]))
    grad_up[...] = low(grad_hidden * wide(up_slope[...]))
    depth, chunk = gate_w.shape[0] // 4, gate_w.shape[1]
    out = []
    for y in (0, 1):
        total = 0.0
        for x in (0, 1):
            at, cut = (2 * y + x) * depth, slice(x * chunk, (x + 1) * chunk)
            total += dot32(grad_gate[:, cut], gate_w[at : at + depth, :], BY_COLS)
            total += dot32(grad_up[:, cut], up_w[at : at + depth, :], BY_COLS)
        out.append(low(total))
    store_half(first, second, jnp.concatenate(out, axis=1))


def grad_hidden_pass(cot_p, gate_slope, up_slope, gate_w, up_w, down_w):
    rows, width = len(cot_p) * cot_p[0].shape[0], cot_p[0].shape[1]
    units = 2 * gate_w.shape[1]
    by_rows = pl.BlockSpec((ROWS, units), lambda i: (i, 0))
    steps = rows // ROWS
    return pl.pallas_call(
        grad_hidden_body,
        grid=(steps,),
        out_shape=(low_shape(rows, units),) * 2 + (low_shape(rows // 2, width),) * 2,
        in_specs=[once(v.shape) for v in (gate_w, up_w, down_w)]
        + [by_rows] * 2
        + [once(v.shape) for v in cot_p],
        out_specs=(by_rows,) * 2 + halves_specs(steps, ROWS, width),
        scratch_shapes=[pltpu.VMEM((rows, width), jnp.bfloat16)],
        name="grad_hidden_pass",
        **KERNEL,
    )(gate_w, up_w, down_w, gate_slope, up_slope, *cot_p)


def term_body(*refs):
    pieces, columns, out = refs[:-2], refs[-2], refs[-1]
    rows = jnp.concatenate([piece[...] for piece in pieces], axis=0)
    out[...] = low(dot32(rows, columns[...], BY_ROWS))


def term_pass(pieces, columns, row_parts, col_parts):
    tokens, width = pieces[0].shape
    depth, chunk = width // row_parts, columns.shape[1] // col_parts
    return pl.pallas_call(
        term_body,
        grid=(row_parts, col_parts),
        out_shape=low_shape(width * col_parts, chunk),
        in_specs=[pl.BlockSpec((tokens, depth), lambda y, x: (0, y))] * len(pieces)
        + [pl.BlockSpec((columns.shape[0], chunk), lambda y, x: (0, x))],
        out_specs=pl.BlockSpec((depth, chunk), lambda y, x: (y * col_parts + x, 0)),
        name="term_pass",
        **KERNEL,
    )(*pieces, columns)


def unit_scale(values):
    return lax.rsqrt(jnp.mean(values * values, axis=-1, keepdims=True) + EPSILON)


def norm_pull(values, grad_scaled):
    scale = unit_scale(values)
    mean = jnp.mean(grad_scaled * values, axis=-1, keepdims=True)
    return scale * grad_scaled - values * (scale * scale * scale) * mean


def pick(bit, near, far):
    return jnp.where(bit == 0, near, far)


def to_split(values):
    step = values.shape[1] // 8
    cuts = [values[:, at * step : (at + 1) * step] for at in range(8)]
    return jnp.concatenate(cuts[0::2] + cuts[1::2], axis=1)


def from_split(values):
    step = values.shape[1] // 8
    cuts = [values[:, at * step : (at + 1) * step] for at in range(8)]
    return jnp.concatenate([cut for pair in zip(cuts[:4], cuts[4:]) for cut in pair], axis=1)


def column_sums(*arrays):
    return jnp.concatenate([jnp.sum(v * v, axis=0, keepdims=True) for v in arrays], axis=0)


def summed(parts):
    total = wide(parts[0][...])
    for part in parts[1:]:
        total += wide(part[...])
    return total


def middle_body(stream_in, *refs):
    parts, (middle_out, normed_out, squares_out) = refs[:-3], refs[-3:]
    attn_out, rows = summed(parts), wide(stream_in[...])
    middle = rows + attn_out
    middle_out[...] = middle
    normed_out[...] = to_split(low(middle * unit_scale(middle)))
    squares_out[...] = column_sums(rows, attn_out, middle)


def middle_pass(stream_in, parts):
    rows, width = stream_in.shape
    return pl.pallas_call(
        middle_body,
        out_shape=(wide_shape(rows, width), low_shape(rows, width), wide_shape(3, width)),
        in_specs=[VMEM_SPEC] * (1 + len(parts)),
        out_specs=(VMEM_SPEC,) * 3,
        name="middle_pass",
        **KERNEL,
    )(stream_in, *parts)


def final_body(middle, *refs):
    parts, (layer_out, squares_out) = refs[:-2], refs[-2:]
    mlp_out = from_split(summed(parts))
    final = middle[...] + mlp_out
    layer_out[...] = low(final)
    squares_out[...] = column_sums(mlp_out, final)


def final_pass(middle, parts):
    rows, width = middle.shape
    return pl.pallas_call(
        final_body,
        out_shape=(low_shape(rows, width), wide_shape(2, width)),
        in_specs=[VMEM_SPEC] * (1 + len(parts)),
        out_specs=(VMEM_SPEC,) * 2,
        name="final_pass",
        **KERNEL,
    )(middle, *parts)


def grad_middle_body(middle, cot, *refs):
    parts, (grad_out, low_out) = refs[:-2], refs[-2:]
    grad_normed = from_split(summed(parts))
    grad = wide(cot[...]) + norm_pull(middle[...], grad_normed)
    grad_out[...] = grad
    low_out[...] = low(grad)


def grad_middle_pass(middle, cot, parts):
    rows, width = middle.shape
    return pl.pallas_call(
        grad_middle_body,
        out_shape=(wide_shape(rows, width), low_shape(rows, width)),
        in_specs=[VMEM_SPEC] * (2 + len(parts)),
        out_specs=(VMEM_SPEC,) * 2,
        name="grad_middle_pass",
        **KERNEL,
    )(middle, cot, *parts)


def input_grad_body(stream_in, grad_middle, *refs):
    parts, out = refs[:-1], refs[-1]
    out[...] = grad_middle[...] + norm_pull(wide(stream_in[...]), summed(parts))


def input_grad_pass(stream_in, grad_middle, parts):
    return pl.pallas_call(
        input_grad_body,
        out_shape=wide_shape(*stream_in.shape),
        in_specs=[VMEM_SPEC] * (2 + len(parts)),
        out_specs=VMEM_SPEC,
        name="input_grad_pass",
        **KERNEL,
    )(stream_in, grad_middle, *parts)


def pack_body(gain, gate_up, down, gate_out, up_out, down_out):
    gate_out[...] = low(wide(gate_up[:, 0, :]) * gain[...])
    up_out[...] = low(wide(gate_up[:, 1, :]) * gain[...])
    down_out[...] = down[...]


def pack_pass(gain, gate_up, down, groups):
    rows, chunk = down.shape[0], down.shape[1] // groups
    out = pl.BlockSpec((rows, chunk), lambda g: (g, 0))
    return pl.pallas_call(
        pack_body,
        grid=(groups,),
        out_shape=(low_shape(groups * rows, chunk),) * 3,
        in_specs=[
            pl.BlockSpec((rows, 1), lambda g: (0, 0)),
            pl.BlockSpec((rows, 2, chunk), lambda g: (0, 0, g)),
            pl.BlockSpec((rows, chunk), lambda g: (0, g)),
        ],
        out_specs=(out,) * 3,
        name="pack_pass",
        **KERNEL,
    )(gain, gate_up, down)


def unpack_body(gain, weight, gate, up, out, gain_sum):
    gate_term, up_term = wide(gate[...]), wide(up[...])
    out[:, 0, :] = gate_term * gain[...]
    out[:, 1, :] = up_term * gain[...]
    products = gate_term * wide(weight[:, 0, :]) + up_term * wide(weight[:, 1, :])
    total = jnp.sum(products, axis=1, keepdims=True)

    @pl.when(pl.program_id(0) == 0)
    def _():
        gain_sum[...] = total

    @pl.when(pl.program_id(0) > 0)
    def _():
        gain_sum[...] += total


def unpack_pass(gain, weight, gate, up, groups):
    rows, chunk = weight.shape[0], weight.shape[2] // groups
    column = pl.BlockSpec((rows, 1), lambda g: (0, 0))
    pair = pl.BlockSpec((rows, 2, chunk), lambda g: (0, 0, g))
    by_group = pl.BlockSpec((rows, chunk), lambda g: (g, 0))
    return pl.pallas_call(
        unpack_body,
        grid=(groups,),
        out_shape=(jax.ShapeDtypeStruct(weight.shape, jnp.float32), wide_shape(rows, 1)),
        in_specs=[column, pair, by_group, by_group],
        out_specs=(pair, column),
        name="unpack_pass",
        **KERNEL,
    )(gain, weight, gate, up)


def exchange(values, axes):
    return lax.all_to_all(values, axes, split_axis=0, concat_axis=0, tiled=True)


def after(values, *earlier):
    return lax.optimization_barrier((values, *earlier))[0]


def together(*values):
    return lax.optimization_barrier(values)


def swap(values, *axes):
    pairs = SWAP if len(axes) == 1 else DIAGONAL
    return lax.ppermute(values, axes if len(axes) > 1 else axes[0], pairs)


def plane_hop(rows):
    return (rows, swap(rows, "uly"), swap(rows, "yy"), swap(rows, "yy", "uly"))


def plane_back(parts):
    return (parts[0], swap(parts[1], "uly"), swap(parts[2], "yy"), swap(parts[3], "yy", "uly"))


def shift(values, by):
    count = lax.axis_size("dp")
    return lax.ppermute(values, "dp", [(i, (i + by) % count) for i in range(count)])


def column_hop(rows):
    return (rows, *(shift(rows, by) for by in range(1, lax.axis_size("dp"))))


def column_back(parts):
    return (parts[0], *(shift(v, -by) for by, v in enumerate(parts[1:], 1)))


def core_hop(pieces):
    return (*pieces, *(swap(v, "cc") for v in pieces))


def chip_parts(first, arrived, count):
    return tuple(jnp.split(low(wide(first) + wide(arrived)), count, axis=0))


def plane_plan(
    layer_input,
    span_order,
    qkv_weight,
    out_weight,
    gate_up_weight,
    down_weight,
    attn_gain,
    mlp_gain,
    output_cotangent,
):
    tok = layer_input.shape[0]
    nz = lax.axis_size("dp")
    ndev = lax.axis_size(ALL_AXES)
    plane = ndev // nz
    span_size = tok * plane // span_order.shape[1]
    y_at, c_at, x_at = lax.axis_index("yy"), lax.axis_index("cc"), lax.axis_index("uly")
    q_cols, kv_cols = H * HD // plane, KV * HD // plane
    own_cols = q_cols + 2 * kv_cols
    d_rows = qkv_weight.shape[0]
    mlp_rows, ff_local = down_weight.shape
    hgroups = lax.axis_size(GROUP_AXES)
    hchunk = ff_local // hgroups

    gain_a = wide(attn_gain)[:, None]
    folded = low(wide(qkv_weight) * gain_a)
    by_group = jnp.concatenate(
        [
            part.reshape(d_rows, plane, -1)
            for part in jnp.split(folded, [H * HD, (H + KV) * HD], axis=1)
        ],
        axis=2,
    ).transpose(1, 0, 2)

    def to_planes(rows):
        return jnp.broadcast_to(rows[None], (nz, *rows.shape)).reshape(-1, rows.shape[2])

    qkv_rows = to_planes(by_group)
    out_rows = out_weight.reshape(d_rows, plane, q_cols).transpose(1, 0, 2).reshape(-1, q_cols)
    out_here = exchange(out_rows, PLANE_AXES)

    gain_peer = swap(mlp_gain[None, :], "uly")
    stream_in = wide(layer_input)
    normed = low(stream_in * unit_scale(stream_in))
    normed, gain_peer, out_here, qkv_rows = together(normed, gain_peer, out_here, qkv_rows)

    gain_own, gain_peer = wide(mlp_gain)[None, :], wide(gain_peer)
    gain_m = pick(
        x_at,
        jnp.concatenate([gain_own, gain_peer], axis=1),
        jnp.concatenate([gain_peer, gain_own], axis=1),
    ).reshape(mlp_rows, 1)
    gate_rows, up_rows, down_rows = pack_pass(gain_m, gate_up_weight, down_weight, hgroups)

    cot_split = to_split(output_cotangent)

    block = jnp.arange(plane, dtype=jnp.int32)
    core_of, y_of, x_of = (block // 4) ^ c_at, (block // 2) % 2 ^ y_at, block % 2 ^ x_at
    stored = (y_of * 2 + core_of) * 2 + x_of
    row_at = (stored[:, None] * tok + jnp.arange(tok, dtype=jnp.int32)[None, :]).reshape(-1)
    positions = sequence_positions(row_at, span_size, span_order[0])
    angles = rope_angles(positions)
    cosine = jnp.concatenate([jnp.cos(angles)] * 2, axis=1)
    sine = jnp.concatenate([-jnp.sin(angles), jnp.sin(angles)], axis=1)

    wo = lax.all_gather(out_here, "dp", axis=0, tiled=True)
    gate_here = exchange(gate_rows, GROUP_AXES)
    normed_p = plane_hop(normed)
    gate_here, normed_p, qkv_rows, up_rows, down_rows, cosine, sine, cot_split = together(
        gate_here, normed_p, qkv_rows, up_rows, down_rows, cosine, sine, cot_split
    )

    def spread(here):
        return lax.all_gather(here, SIDE_AXES, axis=0, tiled=True)

    gate_w = spread(gate_here)
    wq = exchange(qkv_rows, ALL_AXES)
    normed_p = core_hop(normed_p)
    cot_1 = shift(cot_split, 1)
    wq, normed_p, cot_1, up_rows, cot_split = together(wq, normed_p, cot_1, up_rows, cot_split)

    up_here = exchange(up_rows, GROUP_AXES)
    query, key, value, heads = attention_forward(normed_p, wq, cosine, sine, positions)
    up_here, heads, wo, down_rows = together(up_here, heads, wo, down_rows)

    up_w = spread(up_here)
    attn_first, attn_second = by_cols_pass(heads, wo, 1, "out_pass")
    attn_arrived = swap(attn_second, "cc")
    attn_parts = chip_parts(attn_first, attn_arrived, 4)
    attn_parts, down_rows, cot_split = together(attn_parts, down_rows, cot_split)

    down_here = exchange(down_rows, GROUP_AXES)
    cot_3 = shift(cot_split, 3)
    attn_parts = plane_back(attn_parts)
    attn_parts, down_here, cot_3, cot_split = together(attn_parts, down_here, cot_3, cot_split)

    down_w = spread(down_here)
    middle, zhat, squares_a = middle_pass(layer_input, attn_parts)
    zhat_p = column_hop(zhat)
    zhat_p, gate_w, up_w, cot_split = together(zhat_p, gate_w, up_w, cot_split)
    zhat_p, cot_split = together(core_hop(zhat_p), cot_split)

    cot_p = (cot_split, cot_1, shift(cot_split, 2), cot_3)
    hidden, gate_slope, up_slope = hidden_pass(zhat_p, gate_w, up_w)
    hidden, cot_p, gate_slope, down_w = together(hidden, cot_p, gate_slope, down_w)
    cot_p = core_hop(cot_p)
    mlp_first, mlp_second = by_cols_pass(hidden, down_w, 2, "down_pass")
    cot_p, mlp_first, mlp_second = together(cot_p, mlp_first, mlp_second)

    mlp_arrived = swap(mlp_second, "cc")
    grad_gate, grad_up, gz_first, gz_second = grad_hidden_pass(
        cot_p, gate_slope, up_slope, gate_w, up_w, down_w
    )
    gz_second, grad_gate, mlp_arrived = together(gz_second, grad_gate, mlp_arrived)

    def side_sum(term):
        return lax.psum_scatter(term, SIDE_AXES, scatter_dimension=0, tiled=True)

    gz_arrived = swap(gz_second, "cc")
    gate_t = term_pass(zhat_p, grad_gate, 2, 2)
    gz_parts = chip_parts(gz_first, gz_arrived, nz)
    gz_parts, gate_t, mlp_arrived = together(gz_parts, gate_t, mlp_arrived)

    gate_t = side_sum(gate_t)
    gz_parts = column_back(gz_parts)
    up_t = term_pass(zhat_p, grad_up, 2, 2)
    down_t = term_pass(cot_p, hidden, 2, 2)
    mlp_parts = chip_parts(mlp_first, mlp_arrived, nz)
    gz_parts, up_t, down_t, mlp_parts = together(gz_parts, up_t, down_t, mlp_parts)

    up_t = side_sum(up_t)
    grad_middle, grad_out = grad_middle_pass(middle, output_cotangent, gz_parts)
    mlp_1, mlp_3 = shift(mlp_parts[1], -1), shift(mlp_parts[3], -3)
    grad_out_p = plane_hop(grad_out)
    grad_out_p, mlp_1, mlp_3, down_t = together(grad_out_p, mlp_1, mlp_3, down_t)
    grad_out_p, gate_t, down_t = together(core_hop(grad_out_p), gate_t, down_t)

    down_t = side_sum(down_t)
    gate_back = exchange(gate_t, GROUP_AXES)
    mlp_2 = shift(mlp_parts[2], -2)
    grad_qkv = attention_backward(grad_out_p, wo, query, key, value, cosine, sine, positions)
    gx_first, gx_second = by_cols_pass(grad_qkv, wq, 1, "qkv_back_pass")
    qkv_term = term_pass(normed_p, grad_qkv, 2, 1)
    gx_second, qkv_term, gate_back, mlp_2, heads, up_t = together(
        gx_second, qkv_term, gate_back, mlp_2, heads, up_t
    )

    gx_arrived = swap(gx_second, "cc")
    out_term = term_pass(grad_out_p, heads, 2, 1)
    gx_parts = chip_parts(gx_first, gx_arrived, 4)
    gx_parts, out_term, qkv_term, up_t = together(gx_parts, out_term, qkv_term, up_t)

    qkv_sum = exchange(qkv_term, ALL_AXES)
    gx_parts = plane_back(gx_parts)
    gx_parts, qkv_sum, up_t, down_t, out_term = together(
        gx_parts, qkv_sum, up_t, down_t, out_term
    )

    out_term = lax.psum_scatter(out_term, "dp", scatter_dimension=0, tiled=True)
    both_back = exchange(jnp.concatenate([up_t, down_t], axis=1), GROUP_AXES)
    input_grad = input_grad_pass(layer_input, grad_middle, gx_parts)
    layer_output, squares_b = final_pass(middle, (mlp_parts[0], mlp_1, mlp_2, mlp_3))
    both_back, input_grad, out_term, squares_b = together(
        both_back, input_grad, out_term, squares_b
    )
    up_back, down_back = jnp.split(both_back, 2, axis=1)

    squares = jnp.sum(jnp.concatenate([squares_a, squares_b], axis=0), axis=1)
    lanes = jnp.zeros((1, 128), jnp.float32).at[0, :5].set(squares)
    gathered = exchange(jnp.broadcast_to(lanes, (ndev, 128)), ALL_AXES)
    out_sum = exchange(out_term, PLANE_AXES)
    def plane_sum(arrived, cols):
        return jnp.sum(wide(arrived.reshape(nz, plane, d_rows, cols)), axis=0).transpose(1, 0, 2)

    qkv_sum = plane_sum(qkv_sum, own_cols)
    qkv_sum = jnp.concatenate(
        [
            qkv_sum[:, :, :q_cols].reshape(d_rows, -1),
            qkv_sum[:, :, q_cols : q_cols + kv_cols].reshape(d_rows, -1),
            qkv_sum[:, :, q_cols + kv_cols :].reshape(d_rows, -1),
        ],
        axis=1,
    )
    qkv_grad = qkv_sum * gain_a
    attn_gain_grad = jnp.sum(qkv_sum * wide(qkv_weight), axis=1)
    gate_up_grad, gain_sum = unpack_pass(gain_m, gate_up_weight, gate_back, up_back, hgroups)
    down_back = down_back.reshape(hgroups, mlp_rows, hchunk)
    down_grad = wide(down_back.transpose(1, 0, 2).reshape(mlp_rows, ff_local))
    gain_halves = gain_sum.reshape(2, -1)
    gain_keep = jnp.where(x_at == 0, gain_halves[0], gain_halves[1])
    gain_send = jnp.where(x_at == 0, gain_halves[1], gain_halves[0])
    mlp_gain_grad = gain_keep + swap(gain_send[None, :], "uly")[0]

    out_sum = wide(out_sum).reshape(plane, d_rows, q_cols).transpose(1, 0, 2)
    out_weight_grad = out_sum.reshape(d_rows, -1)
    rms_values = jnp.sqrt(jnp.sum(gathered, axis=0)[:5] / (tok * ndev * D))
    return (
        layer_output,
        input_grad,
        qkv_grad,
        out_weight_grad,
        gate_up_grad,
        down_grad,
        attn_gain_grad,
        mlp_gain_grad,
        rms_values,
    )


def solution(mesh):
    sizes = dict(mesh.shape)
    if sizes["blk"] == 4 and sizes["uly"] == 2:
        mesh = Mesh(mesh.devices.reshape(sizes["dp"], 2, 2, 2), ALL_AXES)
        body, blk = plane_plan, ("yy", "cc")
    else:
        body, blk = general_plan, ("blk",)
    every = ("dp", *blk, "uly")
    rows = ("dp", *blk)
    return jax.shard_map(
        body,
        mesh=mesh,
        in_specs=(
            P(every, None),
            P("dp", None),
            P(every, None),
            P(every, None),
            P(rows, None, "uly"),
            P(rows, "uly"),
            P(every),
            P(every),
            P(every, None),
        ),
        out_specs=(
            P(every, None),
            P(every, None),
            P(every, None),
            P(every, None),
            P(rows, None, "uly"),
            P(rows, "uly"),
            P(every),
            P(every),
            P(),
        ),
        check_vma=False,
    )
```

```python
import functools

import jax
import jax.numpy as jnp
from jax import lax
from jax.experimental import pallas as pl
from jax.experimental.pallas import tpu as pltpu
from jax.sharding import Mesh
from jax.sharding import PartitionSpec as P

D = 2048
H = 16
KV = 8
HD = 128


EPSILON = 1e-06
ROPE_BASE = 1000000.0
MASKED = -1e30


def rms_scale(values, gain):
    return values * lax.rsqrt(jnp.mean(values * values, axis=-1, keepdims=True) + EPSILON) * gain


def rope_angles(positions):
    freq_index = jnp.arange(HD // 2, dtype=jnp.float32)
    inverse_freq = ROPE_BASE ** (-2.0 * freq_index / HD)
    return positions.astype(jnp.float32)[:, None] * inverse_freq[None, :]


def rotate_pairs(values, angles):
    half_size = values.shape[-1] // 2
    first_half = values[..., :half_size]
    second_half = values[..., half_size:]
    cosine = jnp.cos(angles)[:, None, :]
    sine = jnp.sin(angles)[:, None, :]
    return jnp.concatenate(
        [first_half * cosine - second_half * sine, second_half * cosine + first_half * sine],
        axis=-1,
    )


def sequence_positions(row_index, span_size, order_row):
    block_index = row_index // span_size
    picks = block_index[:, None] == jnp.arange(order_row.shape[0], dtype=jnp.int32)[None, :]
    chosen = jnp.sum(jnp.where(picks, order_row[None, :], 0), axis=1)
    return chosen * span_size + row_index % span_size


def contract_rows(left_side, right_side):
    return lax.dot_general(
        left_side, right_side, (((0,), (0,)), ((), ())), preferred_element_type=jnp.float32
    )


def contract_cols(left_side, right_side):
    return lax.dot_general(
        left_side, right_side, (((1,), (1,)), ((), ())), preferred_element_type=jnp.float32
    )


def general_plan(
    layer_input,
    span_order,
    qkv_weight,
    out_weight,
    gate_up_weight,
    down_weight,
    attn_gain,
    mlp_gain,
    output_cotangent,
):
    tok_rows = layer_input.shape[0]
    uly_size = lax.axis_size("uly")
    blk_size = lax.axis_size("blk")
    group_rows = tok_rows * uly_size
    seq_rows = group_rows * blk_size
    span_size = group_rows // 2
    order_row = span_order[0]
    local_kv = KV // uly_size
    local_heads = H // uly_size
    group_size = H // KV
    ff_local = down_weight.shape[1]
    score_scale = HD ** (-0.5)
    token_start = (lax.axis_index("blk") * uly_size + lax.axis_index("uly")) * tok_rows
    token_pos = sequence_positions(
        token_start + jnp.arange(tok_rows, dtype=jnp.int32), span_size, order_row
    )
    token_angles = rope_angles(token_pos)
    query_pos = sequence_positions(
        lax.axis_index("blk") * group_rows + jnp.arange(group_rows, dtype=jnp.int32),
        span_size,
        order_row,
    )
    stream_in = layer_input.astype(jnp.float32)
    qkv_full, out_full, attn_gain_full, mlp_gain_full = (
        lax.all_gather(qkv_weight, ("dp", "blk", "uly"), axis=0, tiled=True),
        lax.all_gather(out_weight, ("dp", "blk", "uly"), axis=0, tiled=True),
        lax.all_gather(attn_gain, ("dp", "blk", "uly"), axis=0, tiled=True),
        lax.all_gather(mlp_gain, ("dp", "blk", "uly"), axis=0, tiled=True),
    )
    gate_up_cols, down_cols = (
        lax.all_gather(gate_up_weight, ("dp", "blk"), axis=0, tiled=True),
        lax.all_gather(down_weight, ("dp", "blk"), axis=0, tiled=True),
    )
    attn_gain_wide = attn_gain_full.astype(jnp.float32)
    mlp_gain_wide = mlp_gain_full.astype(jnp.float32)
    normed_attn = rms_scale(stream_in, attn_gain_wide).astype(jnp.bfloat16)
    qkv_all = jnp.dot(normed_attn, qkv_full, preferred_element_type=jnp.float32)
    query_tok = (
        rotate_pairs(qkv_all[:, : H * HD].reshape(tok_rows, H, HD), token_angles)
        .reshape(tok_rows, H * HD)
        .astype(jnp.bfloat16)
    )
    key_tok = (
        rotate_pairs(qkv_all[:, H * HD : (H + KV) * HD].reshape(tok_rows, KV, HD), token_angles)
        .reshape(tok_rows, KV * HD)
        .astype(jnp.bfloat16)
    )
    value_tok = qkv_all[:, (H + KV) * HD :].astype(jnp.bfloat16)
    query_grp, key_grp, value_grp = (
        lax.all_to_all(query_tok, "uly", split_axis=1, concat_axis=0, tiled=True),
        lax.all_to_all(key_tok, "uly", split_axis=1, concat_axis=0, tiled=True),
        lax.all_to_all(value_tok, "uly", split_axis=1, concat_axis=0, tiled=True),
    )
    query_four = query_grp.reshape(group_rows, local_kv, group_size, HD)
    key_whole, value_whole = (
        lax.all_gather(key_grp, "blk", axis=0, tiled=True),
        lax.all_gather(value_grp, "blk", axis=0, tiled=True),
    )
    block_count = seq_rows // group_rows

    def take_block(block_index):
        offset = block_index * group_rows
        key_block = lax.dynamic_slice_in_dim(key_whole, offset, group_rows, 0).reshape(
            group_rows, local_kv, HD
        )
        value_block = lax.dynamic_slice_in_dim(value_whole, offset, group_rows, 0).reshape(
            group_rows, local_kv, HD
        )
        key_pos = sequence_positions(
            offset + jnp.arange(group_rows, dtype=jnp.int32), span_size, order_row
        )
        return (offset, key_block, value_block, key_pos)

    def attend_step(block_index, running):
        top_run, total_run, acc_run = running
        offset, key_block, value_block, key_pos = take_block(block_index)
        scores = (
            jnp.einsum("rkgd,pkd->kgrp", query_four, key_block, preferred_element_type=jnp.float32)
            * score_scale
        )
        allowed = key_pos[None, :] <= query_pos[:, None]
        scores = jnp.where(allowed, scores, MASKED)
        top_new = jnp.maximum(top_run, jnp.max(scores, axis=-1))
        weights = jnp.where(allowed, jnp.exp(scores - top_new[..., None]), 0.0)
        shrink_factor = jnp.exp(top_run - top_new)
        total_new = total_run * shrink_factor + jnp.sum(weights, axis=-1)
        acc_new = acc_run * shrink_factor[..., None] + jnp.einsum(
            "kgrp,pkd->kgrd",
            weights.astype(jnp.bfloat16),
            value_block,
            preferred_element_type=jnp.float32,
        )
        return (top_new, total_new, acc_new)

    start_state = (
        jnp.full((local_kv, group_size, group_rows), MASKED, jnp.float32),
        jnp.zeros((local_kv, group_size, group_rows), jnp.float32),
        jnp.zeros((local_kv, group_size, group_rows, HD), jnp.float32),
    )
    top_end, total_end, acc_end = lax.fori_loop(0, block_count, attend_step, start_state)
    log_total = top_end + jnp.log(total_end)
    head_rows = jnp.transpose(acc_end / total_end[..., None], (2, 0, 1, 3))
    heads_group = head_rows.reshape(group_rows, local_heads * HD).astype(jnp.bfloat16)
    heads_tok = lax.all_to_all(heads_group, "uly", split_axis=0, concat_axis=1, tiled=True)
    attn_out = contract_cols(heads_tok, out_full)
    middle = stream_in + attn_out
    normed_mlp = rms_scale(middle, mlp_gain_wide).astype(jnp.bfloat16)
    normed_grp, cotangent_grp = (
        lax.all_gather(normed_mlp, "uly", axis=0, tiled=True),
        lax.all_gather(output_cotangent, "uly", axis=0, tiled=True),
    )
    gate_up = jnp.einsum(
        "rd,dcf->rcf", normed_grp, gate_up_cols, preferred_element_type=jnp.float32
    )
    gate_part = gate_up[:, 0, :]
    up_part = gate_up[:, 1, :]
    hidden = (jax.nn.silu(gate_part) * up_part).astype(jnp.bfloat16)
    mlp_part = contract_cols(hidden, down_cols)
    mlp_out = lax.psum_scatter(
        mlp_part.astype(jnp.bfloat16), "uly", scatter_dimension=0, tiled=True
    ).astype(jnp.float32)
    final_stream = middle + mlp_out
    local_squares = jnp.stack(
        [
            jnp.sum(stream_in * stream_in),
            jnp.sum(attn_out * attn_out),
            jnp.sum(middle * middle),
            jnp.sum(mlp_out * mlp_out),
            jnp.sum(final_stream * final_stream),
        ]
    )
    total_squares = lax.psum(local_squares, ("dp", "blk", "uly"))
    entry_count = tok_rows * lax.axis_size("dp") * blk_size * uly_size * D
    rms_values = jnp.sqrt(total_squares / entry_count)
    grad_hidden = jnp.dot(cotangent_grp, down_cols, preferred_element_type=jnp.float32)
    sigmoid_gate = jax.nn.sigmoid(gate_part)
    grad_gate = grad_hidden * up_part * sigmoid_gate * (1.0 + gate_part * (1.0 - sigmoid_gate))
    grad_up = grad_hidden * gate_part * sigmoid_gate
    grad_gate_up = jnp.stack([grad_gate, grad_up], axis=1).astype(jnp.bfloat16)
    grad_normed_part = jnp.einsum(
        "rcf,dcf->rd", grad_gate_up, gate_up_cols, preferred_element_type=jnp.float32
    )
    grad_normed_mlp = lax.psum_scatter(
        grad_normed_part.astype(jnp.bfloat16), "uly", scatter_dimension=0, tiled=True
    ).astype(jnp.float32)
    gate_term = jnp.einsum(
        "rd,rcf->dcf", normed_grp, grad_gate_up, preferred_element_type=jnp.float32
    ).reshape(lax.axis_size(("dp", "blk")) * gate_up_weight.shape[0], 2 * ff_local)
    mlp_grads = lax.psum_scatter(
        jnp.concatenate([gate_term, contract_rows(cotangent_grp, hidden)], axis=1).astype(
            jnp.bfloat16
        ),
        ("dp", "blk"),
        scatter_dimension=0,
        tiled=True,
    ).astype(jnp.float32)
    gate_up_grad = mlp_grads[:, : 2 * ff_local].reshape(mlp_grads.shape[0], 2, ff_local)
    down_grad = mlp_grads[:, 2 * ff_local :]
    mlp_value, mlp_pull = jax.vjp(rms_scale, middle, mlp_gain_wide)
    grad_middle_norm, mlp_gain_grad_full = mlp_pull(grad_normed_mlp)
    grad_middle = output_cotangent.astype(jnp.float32) + grad_middle_norm
    grad_attn_out = grad_middle.astype(jnp.bfloat16)
    grad_heads_tok = jnp.dot(grad_attn_out, out_full, preferred_element_type=jnp.float32).astype(
        jnp.bfloat16
    )
    out_weight_term = contract_rows(grad_attn_out, heads_tok)
    grad_heads = lax.all_to_all(grad_heads_tok, "uly", split_axis=1, concat_axis=0, tiled=True)
    grad_four = grad_heads.reshape(group_rows, local_kv, group_size, HD)
    row_delta = jnp.transpose(
        jnp.sum(grad_four.astype(jnp.float32) * head_rows, axis=-1), (1, 2, 0)
    )

    def backward_step(block_index, running):
        grad_query_run, grad_key_all, grad_value_all = running
        offset, key_block, value_block, key_pos = take_block(block_index)
        scores = (
            jnp.einsum("rkgd,pkd->kgrp", query_four, key_block, preferred_element_type=jnp.float32)
            * score_scale
        )
        allowed = key_pos[None, :] <= query_pos[:, None]
        soft_probs = jnp.where(
            allowed, jnp.exp(jnp.where(allowed, scores, MASKED) - log_total[..., None]), 0.0
        )
        grad_probs = jnp.einsum(
            "rkgd,pkd->kgrp", grad_four, value_block, preferred_element_type=jnp.float32
        )
        grad_scores = (soft_probs * (grad_probs - row_delta[..., None])).astype(jnp.bfloat16)
        grad_query_run = (
            grad_query_run
            + jnp.einsum(
                "kgrp,pkd->kgrd", grad_scores, key_block, preferred_element_type=jnp.float32
            )
            * score_scale
        )
        grad_key_block = (
            jnp.einsum(
                "kgrp,rkgd->pkd", grad_scores, query_four, preferred_element_type=jnp.float32
            )
            * score_scale
        ).reshape(group_rows, local_kv * HD)
        grad_value_block = jnp.einsum(
            "kgrp,rkgd->pkd",
            soft_probs.astype(jnp.bfloat16),
            grad_four,
            preferred_element_type=jnp.float32,
        ).reshape(group_rows, local_kv * HD)
        grad_key_all = lax.dynamic_update_slice_in_dim(grad_key_all, grad_key_block, offset, 0)
        grad_value_all = lax.dynamic_update_slice_in_dim(
            grad_value_all, grad_value_block, offset, 0
        )
        return (grad_query_run, grad_key_all, grad_value_all)

    back_state = (
        jnp.zeros((local_kv, group_size, group_rows, HD), jnp.float32),
        jnp.zeros((seq_rows, local_kv * HD), jnp.float32),
        jnp.zeros((seq_rows, local_kv * HD), jnp.float32),
    )
    grad_query_end, grad_key_whole, grad_value_whole = lax.fori_loop(
        0, block_count, backward_step, back_state
    )
    grad_key_own, grad_value_own = (
        lax.psum_scatter(
            grad_key_whole.astype(jnp.bfloat16), "blk", scatter_dimension=0, tiled=True
        ).astype(jnp.float32),
        lax.psum_scatter(
            grad_value_whole.astype(jnp.bfloat16), "blk", scatter_dimension=0, tiled=True
        ).astype(jnp.float32),
    )
    grad_query_rows = (
        jnp.transpose(grad_query_end, (2, 0, 1, 3))
        .reshape(group_rows, local_heads * HD)
        .astype(jnp.bfloat16)
    )
    grad_query_tok, grad_key_tok, grad_value_tok = (
        lax.all_to_all(grad_query_rows, "uly", split_axis=0, concat_axis=1, tiled=True),
        lax.all_to_all(
            grad_key_own.astype(jnp.bfloat16), "uly", split_axis=0, concat_axis=1, tiled=True
        ),
        lax.all_to_all(
            grad_value_own.astype(jnp.bfloat16), "uly", split_axis=0, concat_axis=1, tiled=True
        ),
    )
    back_angles = rope_angles(-token_pos)
    grad_query_plain = rotate_pairs(
        grad_query_tok.astype(jnp.float32).reshape(tok_rows, H, HD), back_angles
    ).reshape(tok_rows, H * HD)
    grad_key_plain = rotate_pairs(
        grad_key_tok.astype(jnp.float32).reshape(tok_rows, KV, HD), back_angles
    ).reshape(tok_rows, KV * HD)
    grad_qkv = jnp.concatenate(
        [grad_query_plain, grad_key_plain, grad_value_tok.astype(jnp.float32)], axis=1
    ).astype(jnp.bfloat16)
    grad_normed_attn = contract_cols(grad_qkv, qkv_full)
    qkv_term = contract_rows(normed_attn, grad_qkv)
    attn_value, attn_pull = jax.vjp(rms_scale, stream_in, attn_gain_wide)
    grad_input_norm, attn_gain_grad_full = attn_pull(grad_normed_attn)
    input_grad = grad_middle + grad_input_norm
    qkv_grad, out_weight_grad, attn_gain_grad, mlp_gain_grad = (
        lax.psum_scatter(qkv_term, ("dp", "blk", "uly"), scatter_dimension=0, tiled=True),
        lax.psum_scatter(out_weight_term, ("dp", "blk", "uly"), scatter_dimension=0, tiled=True),
        lax.psum_scatter(
            attn_gain_grad_full, ("dp", "blk", "uly"), scatter_dimension=0, tiled=True
        ),
        lax.psum_scatter(mlp_gain_grad_full, ("dp", "blk", "uly"), scatter_dimension=0, tiled=True),
    )
    return (
        final_stream.astype(jnp.bfloat16),
        input_grad,
        qkv_grad,
        out_weight_grad,
        gate_up_grad,
        down_grad,
        attn_gain_grad,
        mlp_gain_grad,
        rms_values,
    )


ALL_AXES = ("dp", "yy", "cc", "uly")
SIDE_AXES = ("yy", "uly")
PLANE_AXES = ("yy", "cc", "uly")
GROUP_AXES = ("dp", "cc")
SWAP = [(0, 1), (1, 0)]
DIAGONAL = [(0, 3), (1, 2), (2, 1), (3, 0)]
VMEM_SPEC = pl.BlockSpec(memory_space=pltpu.VMEM)
KERNEL = dict(
    compiler_params=pltpu.CompilerParams(vmem_limit_bytes=58 * 1024 * 1024),
    cost_estimate=pl.CostEstimate(flops=1000, bytes_accessed=1000, transcendentals=0),
)
ROWS = 256
BY_ROWS = (((0,), (0,)), ((), ()))
BY_COLS = (((1,), (1,)), ((), ()))
PLAIN = (((1,), (0,)), ((), ()))


def wide(values):
    return values.astype(jnp.float32)


def low(values):
    return values.astype(jnp.bfloat16)


def dot32(left, right, dims=PLAIN):
    return lax.dot_general(left, right, dims, preferred_element_type=jnp.float32)


def low_shape(rows, cols):
    return jax.ShapeDtypeStruct((rows, cols), jnp.bfloat16)


def wide_shape(rows, cols):
    return jax.ShapeDtypeStruct((rows, cols), jnp.float32)


def once(shape):
    return pl.BlockSpec(shape, lambda *i: (0,) * len(shape), pipeline_mode=pl.Buffered(1))


def row_block(step):
    return pl.ds(pl.multiple_of(step * ROWS, ROWS), ROWS)


def head_cut(head):
    return slice(head * HD, (head + 1) * HD)


def join_rows(pieces, out):
    rows = pieces[0].shape[0]
    for number, piece in enumerate(pieces):
        out[number * rows : (number + 1) * rows, :] = piece[...]


def turn(values, cosine, sine):
    return values * cosine + pltpu.roll(values, HD // 2, 1) * sine


def softmax_rows(query, key, key_pos, query_pos):
    scores = dot32(query, key, BY_COLS) * HD ** (-0.5)
    allowed = key_pos <= query_pos
    scores = jnp.where(allowed, scores, MASKED)
    top = jnp.max(scores, axis=1, keepdims=True)
    weights = jnp.exp(scores - top)
    return weights * (1.0 / jnp.sum(weights, axis=1, keepdims=True))


def attention_forward_body(group, weight, cosine, sine, pos_col, pos_row, *refs):
    pieces, (query_out, key_out, value_out, heads_out, normed) = refs[:-5], refs[-5:]
    join_rows(pieces, normed)
    steps = normed.shape[0] // ROWS

    def project(step, carry):
        at = row_block(step)
        qkv = dot32(normed[at, :], weight[...])
        for head in range(group):
            turned = turn(qkv[:, head_cut(head)], cosine[at, :], sine[at, :])
            query_out[at, head_cut(head)] = low(turned)
        key_out[at, :] = low(turn(qkv[:, head_cut(group)], cosine[at, :], sine[at, :]))
        value_out[at, :] = low(qkv[:, head_cut(group + 1)])
        return carry

    def attend(step, carry):
        at = row_block(step)
        for head in range(group):
            probs = softmax_rows(
                query_out[at, head_cut(head)], key_out[...], pos_row[...], pos_col[at, :]
            )
            heads_out[at, head_cut(head)] = low(dot32(low(probs), value_out[...]))
        return carry

    lax.fori_loop(0, steps, project, 0)
    lax.fori_loop(0, steps, attend, 0)


def attention_forward(pieces, weight, cosine, sine, pos_col, pos_row):
    rows, group = pos_col.shape[0], weight.shape[1] // HD - 2
    return pl.pallas_call(
        functools.partial(attention_forward_body, group),
        out_shape=(
            low_shape(rows, group * HD),
            low_shape(rows, HD),
            low_shape(rows, HD),
            low_shape(rows, group * HD),
        ),
        in_specs=[VMEM_SPEC] * (5 + len(pieces)),
        out_specs=(VMEM_SPEC,) * 4,
        scratch_shapes=[pltpu.VMEM((rows, weight.shape[0]), jnp.bfloat16)],
        name="attention_forward",
        **KERNEL,
    )(weight, cosine, sine, pos_col, pos_row, *pieces)


def attention_backward_body(group, weight, query, key, value, cosine, sine, pos_col, pos_row, *refs):
    pieces, (grad_qkv, grad_out, key_sum, value_sum) = refs[:-4], refs[-4:]
    join_rows(pieces, grad_out)
    steps = query.shape[0] // ROWS
    key_sum[...] = jnp.zeros_like(key_sum)
    value_sum[...] = jnp.zeros_like(value_sum)

    def block(step, carry):
        at = row_block(step)
        grad_heads = low(dot32(grad_out[at, :], weight[...]))
        for head in range(group):
            cut = head_cut(head)
            probs = softmax_rows(query[at, cut], key[...], pos_row[...], pos_col[at, :])
            grad_probs = dot32(grad_heads[:, cut], value[...], BY_COLS)
            delta = jnp.sum(probs * grad_probs, axis=1, keepdims=True)
            grad_scores = low(probs * (grad_probs - delta))
            grad_query = wide(low(dot32(grad_scores, key[...]) * HD ** (-0.5)))
            grad_qkv[at, cut] = low(turn(grad_query, cosine[at, :], -sine[at, :]))
            key_sum[...] += dot32(grad_scores, query[at, cut], BY_ROWS)
            value_sum[...] += dot32(low(probs), grad_heads[:, cut], BY_ROWS)
        return carry

    def finish(step, carry):
        at = row_block(step)
        grad_key = wide(low(key_sum[at, :] * HD ** (-0.5)))
        grad_qkv[at, head_cut(group)] = low(turn(grad_key, cosine[at, :], -sine[at, :]))
        grad_qkv[at, head_cut(group + 1)] = low(value_sum[at, :])
        return carry

    lax.fori_loop(0, steps, block, 0)
    lax.fori_loop(0, steps, finish, 0)


def attention_backward(pieces, weight, query, key, value, cosine, sine, pos_col, pos_row):
    rows, group = query.shape[0], query.shape[1] // HD
    return pl.pallas_call(
        functools.partial(attention_backward_body, group),
        out_shape=low_shape(rows, (group + 2) * HD),
        in_specs=[VMEM_SPEC] * (8 + len(pieces)),
        out_specs=VMEM_SPEC,
        scratch_shapes=[pltpu.VMEM((rows, weight.shape[0]), jnp.bfloat16)]
        + [pltpu.VMEM((rows, HD), jnp.float32)] * 2,
        name="attention_backward",
        **KERNEL,
    )(weight, query, key, value, cosine, sine, pos_col, pos_row, *pieces)


def stripes(weight, parts, number):
    depth = weight.shape[0] // parts**2 // ROWS

    def place(x, step):
        at = jnp.clip(step - number, 0, parts * depth - 1)
        return ((at // depth * parts + x) * depth + at % depth, 0)

    shape = (ROWS, weight.shape[1])
    return [pl.BlockSpec(shape, functools.partial(place, x)) for x in range(parts)]


def stripe_dot(rows, refs):
    chunk = refs[0].shape[1]
    total = dot32(rows[:, :chunk], refs[0][...], BY_COLS)
    for x, ref in enumerate(refs[1:], 1):
        total += dot32(rows[:, x * chunk : (x + 1) * chunk], ref[...], BY_COLS)
    return total


def store_rows(outs, values):
    rows = outs[0].shape[0]
    for number, out in enumerate(outs):
        out[...] = values[number * rows : (number + 1) * rows, :]


def by_cols_body(parts, rows, *refs):
    store_rows(refs[parts:], low(stripe_dot(rows, refs[:parts])))


def by_cols_pass(rows, weight, parts, blocks, name):
    width = weight.shape[0] // parts
    block = rows.shape[0] // blocks
    return pl.pallas_call(
        functools.partial(by_cols_body, parts),
        grid=(width // ROWS,),
        out_shape=(low_shape(block, width),) * blocks,
        in_specs=[once(rows.shape), *stripes(weight, parts, 0)],
        out_specs=(pl.BlockSpec((block, ROWS), lambda step: (0, step)),) * blocks,
        name=name,
        **KERNEL,
    )(rows, *[weight] * parts)


def columns_of(weight):
    shape = (weight.shape[0] // 4, weight.shape[1] // 2)

    def place(y, step):
        at = jnp.minimum(step, 3)
        return (2 * y + at // 2, at % 2)

    return [pl.BlockSpec(shape, functools.partial(place, y)) for y in (0, 1)]


def column_dot(rows, near, far):
    depth = near.shape[0]
    return dot32(rows[:, :depth], near[...]) + dot32(rows[:, depth:], far[...])


def hidden_body(gate_near, gate_far, up_near, up_far, *refs):
    normed_p, (hidden_out, gate_slope, up_slope, normed) = refs[:-4], refs[-4:]

    @pl.when(pl.program_id(0) == 0)
    def _():
        join_rows(normed_p, normed)

    gate = column_dot(normed, gate_near, gate_far)
    up = column_dot(normed, up_near, up_far)
    sig = jax.nn.sigmoid(gate)
    hidden_out[...] = low(gate * sig * up)
    gate_slope[...] = low(up * sig * (1.0 + gate * (1.0 - sig)))
    up_slope[...] = low(gate * sig)


def hidden_pass(normed_p, gate_w, up_w):
    rows, width = len(normed_p) * normed_p[0].shape[0], normed_p[0].shape[1]
    units = 2 * gate_w.shape[1]
    return pl.pallas_call(
        hidden_body,
        grid=(4,),
        out_shape=(low_shape(rows, units),) * 3,
        in_specs=columns_of(gate_w) + columns_of(up_w) + [once(v.shape) for v in normed_p],
        out_specs=(pl.BlockSpec((rows, units // 4), lambda step: (0, step)),) * 3,
        scratch_shapes=[pltpu.VMEM((rows, width), jnp.bfloat16)],
        name="hidden_pass",
        **KERNEL,
    )(gate_w, gate_w, up_w, up_w, *normed_p)


def grad_hidden_body(down_near, down_far, gate_slope, up_slope, *refs):
    gate_s, up_s, refs = refs[:2], refs[2:4], refs[4:]
    count = (len(refs) - 5) // 2
    cot_p, (grad_gate_out, grad_up_out, *outs) = refs[:count], refs[count:-3]
    cot, grad_gate, grad_up = refs[-3:]
    step, chunk = pl.program_id(0), grad_gate_out.shape[1]

    @pl.when(step == 0)
    def _():
        join_rows(cot_p, cot)

    @pl.when(step < 4)
    def _():
        grad_hidden = column_dot(cot, down_near, down_far)
        grad_gate_out[...] = low(grad_hidden * wide(gate_slope[...]))
        grad_up_out[...] = low(grad_hidden * wide(up_slope[...]))

    for number in range(4):

        @pl.when(step == number)
        def _(cut=slice(number * chunk, (number + 1) * chunk)):
            grad_gate[:, cut] = grad_gate_out[...]
            grad_up[:, cut] = grad_up_out[...]

    @pl.when(step >= 4)
    def _():
        store_rows(outs, low(stripe_dot(grad_gate, gate_s) + stripe_dot(grad_up, up_s)))


def grad_hidden_pass(cot_p, gate_slope, up_slope, gate_w, up_w, down_w):
    rows, width = len(cot_p) * cot_p[0].shape[0], cot_p[0].shape[1]
    units = 2 * gate_w.shape[1]
    quarter = pl.BlockSpec((rows, units // 4), lambda step: (0, jnp.minimum(step, 3)))
    stripe = pl.BlockSpec((cot_p[0].shape[0], ROWS), lambda step: (0, jnp.maximum(step - 4, 0)))
    return pl.pallas_call(
        grad_hidden_body,
        grid=(4 + width // ROWS,),
        out_shape=(low_shape(rows, units),) * 2 + tuple(low_shape(*v.shape) for v in cot_p),
        in_specs=columns_of(down_w)
        + [quarter] * 2
        + stripes(gate_w, 2, 4)
        + stripes(up_w, 2, 4)
        + [once(v.shape) for v in cot_p],
        out_specs=(quarter,) * 2 + (stripe,) * len(cot_p),
        scratch_shapes=[pltpu.VMEM((rows, width), jnp.bfloat16)]
        + [pltpu.VMEM((rows, units), jnp.bfloat16)] * 2,
        name="grad_hidden_pass",
        **KERNEL,
    )(down_w, down_w, gate_slope, up_slope, gate_w, gate_w, up_w, up_w, *cot_p)


def term_body(*refs):
    pieces, columns, out = refs[:-2], refs[-2], refs[-1]
    rows = jnp.concatenate([piece[...] for piece in pieces], axis=0)
    out[...] = low(dot32(rows, columns[...], BY_ROWS))


def term_pass(pieces, columns, row_parts, col_parts):
    tokens, width = pieces[0].shape
    depth, chunk = width // row_parts, columns.shape[1] // col_parts
    return pl.pallas_call(
        term_body,
        grid=(row_parts, col_parts),
        out_shape=low_shape(width * col_parts, chunk),
        in_specs=[pl.BlockSpec((tokens, depth), lambda y, x: (0, y))] * len(pieces)
        + [pl.BlockSpec((columns.shape[0], chunk), lambda y, x: (0, x))],
        out_specs=pl.BlockSpec((depth, chunk), lambda y, x: (y * col_parts + x, 0)),
        name="term_pass",
        **KERNEL,
    )(*pieces, columns)


def unit_scale(values):
    return lax.rsqrt(jnp.mean(values * values, axis=-1, keepdims=True) + EPSILON)


def norm_pull(values, grad_scaled):
    scale = unit_scale(values)
    mean = jnp.mean(grad_scaled * values, axis=-1, keepdims=True)
    return scale * grad_scaled - values * (scale * scale * scale) * mean


def pick(bit, near, far):
    return jnp.where(bit == 0, near, far)


def to_split(values):
    step = values.shape[1] // 8
    cuts = [values[:, at * step : (at + 1) * step] for at in range(8)]
    return jnp.concatenate(cuts[0::2] + cuts[1::2], axis=1)


def from_split(values):
    step = values.shape[1] // 8
    cuts = [values[:, at * step : (at + 1) * step] for at in range(8)]
    return jnp.concatenate([cut for pair in zip(cuts[:4], cuts[4:]) for cut in pair], axis=1)


def column_sums(*arrays):
    return jnp.concatenate([jnp.sum(v * v, axis=0, keepdims=True) for v in arrays], axis=0)


def summed(parts):
    total = wide(parts[0][...])
    for part in parts[1:]:
        total += wide(part[...])
    return total


def prepare_body(stream_in, cot, normed_out, cot_out):
    rows = wide(stream_in[...])
    normed_out[...] = low(rows * unit_scale(rows))
    cot_out[...] = to_split(cot[...])


def prepare_pass(stream_in, cot):
    return pl.pallas_call(
        prepare_body,
        out_shape=(low_shape(*stream_in.shape), low_shape(*cot.shape)),
        in_specs=[VMEM_SPEC] * 2,
        out_specs=(VMEM_SPEC,) * 2,
        name="prepare_pass",
        **KERNEL,
    )(stream_in, cot)


def middle_body(stream_in, *refs):
    parts, (middle_out, normed_out, squares_out) = refs[:-3], refs[-3:]
    attn_out, rows = summed(parts), wide(stream_in[...])
    middle = rows + attn_out
    middle_out[...] = middle
    normed_out[...] = to_split(low(middle * unit_scale(middle)))
    squares_out[...] = column_sums(rows, attn_out, middle)


def middle_pass(stream_in, parts):
    rows, width = stream_in.shape
    return pl.pallas_call(
        middle_body,
        out_shape=(wide_shape(rows, width), low_shape(rows, width), wide_shape(3, width)),
        in_specs=[VMEM_SPEC] * (1 + len(parts)),
        out_specs=(VMEM_SPEC,) * 3,
        name="middle_pass",
        **KERNEL,
    )(stream_in, *parts)


def final_body(middle, squares_a, *refs):
    parts, (layer_out, sums_out) = refs[:-2], refs[-2:]
    mlp_out = from_split(summed(parts))
    final = middle[...] + mlp_out
    layer_out[...] = low(final)
    squares = jnp.concatenate([squares_a[...], column_sums(mlp_out, final)], axis=0)
    sums = jnp.sum(squares, axis=1, keepdims=True)
    lane = lax.broadcasted_iota(jnp.int32, (1, sums_out.shape[1]), 1)
    total = jnp.zeros((1, sums_out.shape[1]), jnp.float32)
    for number in range(sums.shape[0]):
        total += jnp.where(lane == number, sums[number : number + 1, :], 0.0)
    sums_out[...] = jnp.broadcast_to(total, sums_out.shape)


def final_pass(middle, squares_a, parts, copies):
    rows, width = middle.shape
    return pl.pallas_call(
        final_body,
        out_shape=(low_shape(rows, width), wide_shape(copies, 128)),
        in_specs=[VMEM_SPEC] * (2 + len(parts)),
        out_specs=(VMEM_SPEC,) * 2,
        name="final_pass",
        **KERNEL,
    )(middle, squares_a, *parts)


def grad_middle_body(middle, cot, *refs):
    parts, (grad_out, low_out) = refs[:-2], refs[-2:]
    grad_normed = from_split(summed(parts))
    grad = wide(cot[...]) + norm_pull(middle[...], grad_normed)
    grad_out[...] = grad
    low_out[...] = low(grad)


def grad_middle_pass(middle, cot, parts):
    rows, width = middle.shape
    return pl.pallas_call(
        grad_middle_body,
        out_shape=(wide_shape(rows, width), low_shape(rows, width)),
        in_specs=[VMEM_SPEC] * (2 + len(parts)),
        out_specs=(VMEM_SPEC,) * 2,
        name="grad_middle_pass",
        **KERNEL,
    )(middle, cot, *parts)


def input_grad_body(stream_in, grad_middle, *refs):
    parts, out = refs[:-1], refs[-1]
    out[...] = grad_middle[...] + norm_pull(wide(stream_in[...]), summed(parts))


def input_grad_pass(stream_in, grad_middle, parts):
    return pl.pallas_call(
        input_grad_body,
        out_shape=wide_shape(*stream_in.shape),
        in_specs=[VMEM_SPEC] * (2 + len(parts)),
        out_specs=VMEM_SPEC,
        name="input_grad_pass",
        **KERNEL,
    )(stream_in, grad_middle, *parts)


def pack_body(gain, gate_up, down, gate_out, up_out, down_out):
    gate_out[...] = low(wide(gate_up[:, 0, :]) * gain[...])
    up_out[...] = low(wide(gate_up[:, 1, :]) * gain[...])
    down_out[...] = down[...]


def pack_pass(gain, gate_up, down, groups):
    rows, chunk = down.shape[0], down.shape[1] // groups
    out = pl.BlockSpec((rows, chunk), lambda g: (g, 0))
    return pl.pallas_call(
        pack_body,
        grid=(groups,),
        out_shape=(low_shape(groups * rows, chunk),) * 3,
        in_specs=[
            pl.BlockSpec((rows, 1), lambda g: (0, 0)),
            pl.BlockSpec((rows, 2, chunk), lambda g: (0, 0, g)),
            pl.BlockSpec((rows, chunk), lambda g: (0, g)),
        ],
        out_specs=(out,) * 3,
        name="pack_pass",
        **KERNEL,
    )(gain, gate_up, down)


def unpack_body(gain, weight, gate, up, out, gain_sum):
    gate_term, up_term = wide(gate[...]), wide(up[...])
    out[:, 0, :] = gate_term * gain[...]
    out[:, 1, :] = up_term * gain[...]
    products = gate_term * wide(weight[:, 0, :]) + up_term * wide(weight[:, 1, :])
    total = jnp.sum(products, axis=1, keepdims=True)

    @pl.when(pl.program_id(0) == 0)
    def _():
        gain_sum[...] = total

    @pl.when(pl.program_id(0) > 0)
    def _():
        gain_sum[...] += total


def unpack_pass(gain, weight, gate, up, groups):
    rows, chunk = weight.shape[0], weight.shape[2] // groups
    column = pl.BlockSpec((rows, 1), lambda g: (0, 0))
    pair = pl.BlockSpec((rows, 2, chunk), lambda g: (0, 0, g))
    by_group = pl.BlockSpec((rows, chunk), lambda g: (g, 0))
    return pl.pallas_call(
        unpack_body,
        grid=(groups,),
        out_shape=(jax.ShapeDtypeStruct(weight.shape, jnp.float32), wide_shape(rows, 1)),
        in_specs=[column, pair, by_group, by_group],
        out_specs=(pair, column),
        name="unpack_pass",
        **KERNEL,
    )(gain, weight, gate, up)


def exchange(values, axes):
    return lax.all_to_all(values, axes, split_axis=0, concat_axis=0, tiled=True)


def after(values, *earlier):
    return lax.optimization_barrier((values, *earlier))[0]


def together(*values):
    return lax.optimization_barrier(values)


def swap(values, *axes):
    pairs = SWAP if len(axes) == 1 else DIAGONAL
    return lax.ppermute(values, axes if len(axes) > 1 else axes[0], pairs)


def plane_hop(rows):
    return (rows, swap(rows, "uly"), swap(rows, "yy"), swap(rows, "yy", "uly"))


def plane_back(parts):
    return (parts[0], swap(parts[1], "uly"), swap(parts[2], "yy"), swap(parts[3], "yy", "uly"))


def shift(values, by):
    count = lax.axis_size("dp")
    return lax.ppermute(values, "dp", [(i, (i + by) % count) for i in range(count)])


def column_hop(rows):
    return (rows, *(shift(rows, by) for by in range(1, lax.axis_size("dp"))))


def column_back(parts):
    return (parts[0], *(shift(v, -by) for by, v in enumerate(parts[1:], 1)))


def core_hop(pieces):
    return (*pieces, *(swap(v, "cc") for v in pieces))


def add_body(*refs):
    count = len(refs) // 3
    for left, right, out in zip(refs[:count], refs[count : 2 * count], refs[2 * count :]):
        out[...] = low(wide(left[...]) + wide(right[...]))


def core_back(blocks):
    half = len(blocks) // 2
    arrived = [swap(v, "cc") for v in blocks[half:]]
    return pl.pallas_call(
        add_body,
        out_shape=tuple(low_shape(*v.shape) for v in arrived),
        in_specs=[VMEM_SPEC] * (2 * half),
        out_specs=(VMEM_SPEC,) * half,
        name="add_pass",
        **KERNEL,
    )(*blocks[:half], *arrived)


def plane_plan(
    layer_input,
    span_order,
    qkv_weight,
    out_weight,
    gate_up_weight,
    down_weight,
    attn_gain,
    mlp_gain,
    output_cotangent,
):
    tok = layer_input.shape[0]
    nz = lax.axis_size("dp")
    ndev = lax.axis_size(ALL_AXES)
    plane = ndev // nz
    span_size = tok * plane // span_order.shape[1]
    y_at, c_at, x_at = lax.axis_index("yy"), lax.axis_index("cc"), lax.axis_index("uly")
    q_cols, kv_cols = H * HD // plane, KV * HD // plane
    own_cols = q_cols + 2 * kv_cols
    d_rows = qkv_weight.shape[0]
    mlp_rows, ff_local = down_weight.shape
    hgroups = lax.axis_size(GROUP_AXES)
    hchunk = ff_local // hgroups

    gain_peer = swap(mlp_gain[None, :], "uly")
    gain_own, gain_peer = wide(mlp_gain)[None, :], wide(gain_peer)
    gain_m = pick(
        x_at,
        jnp.concatenate([gain_own, gain_peer], axis=1),
        jnp.concatenate([gain_peer, gain_own], axis=1),
    ).reshape(mlp_rows, 1)
    gate_rows, up_rows, down_rows = pack_pass(gain_m, gate_up_weight, down_weight, hgroups)
    out_rows = out_weight.reshape(d_rows, plane, q_cols).transpose(1, 0, 2).reshape(-1, q_cols)
    out_here = exchange(out_rows, PLANE_AXES)
    normed, cot_split = prepare_pass(layer_input, output_cotangent)
    cot_1 = shift(cot_split, 1)
    gate_rows, up_rows, down_rows, out_here, normed, cot_split, cot_1, qkv_weight = together(
        gate_rows, up_rows, down_rows, out_here, normed, cot_split, cot_1, qkv_weight
    )

    def spread(here):
        return lax.all_gather(here, SIDE_AXES, axis=0, tiled=True)

    wo = lax.all_gather(out_here, "dp", axis=0, tiled=True)
    gate_here = exchange(gate_rows, GROUP_AXES)
    normed_p = plane_hop(normed)
    gain_a = wide(attn_gain)[:, None]
    folded = low(wide(qkv_weight) * gain_a)
    by_group = jnp.concatenate(
        [
            part.reshape(d_rows, plane, -1)
            for part in jnp.split(folded, [H * HD, (H + KV) * HD], axis=1)
        ],
        axis=2,
    ).transpose(1, 0, 2)
    qkv_rows = jnp.broadcast_to(by_group[None], (nz, *by_group.shape)).reshape(-1, own_cols)
    gate_here, normed_p, qkv_rows, up_rows, down_rows, cot_split = together(
        gate_here, normed_p, qkv_rows, up_rows, down_rows, cot_split
    )

    block = jnp.arange(plane, dtype=jnp.int32)
    core_of, y_of, x_of = (block // 4) ^ c_at, (block // 2) % 2 ^ y_at, block % 2 ^ x_at
    stored = (y_of * 2 + core_of) * 2 + x_of
    row_at = (stored[:, None] * tok + jnp.arange(tok, dtype=jnp.int32)[None, :]).reshape(-1)
    positions = sequence_positions(row_at, span_size, span_order[0])
    angles = rope_angles(positions)
    cosine = jnp.concatenate([jnp.cos(angles)] * 2, axis=1)
    sine = jnp.concatenate([-jnp.sin(angles), jnp.sin(angles)], axis=1)
    gate_w = spread(gate_here)
    wq = exchange(qkv_rows, ALL_AXES)
    normed_p = core_hop(normed_p)
    rows_info = (cosine, sine, positions[:, None], positions[None, :])
    wq, normed_p, up_rows, rows_info = together(wq, normed_p, up_rows, rows_info)

    up_here = exchange(up_rows, GROUP_AXES)
    query, key, value, heads = attention_forward(normed_p, wq, *rows_info)
    attn_parts = core_back(by_cols_pass(heads, wo, 1, plane, "out_pass"))
    up_here, attn_parts, down_rows, cot_split = together(
        up_here, attn_parts, down_rows, cot_split
    )

    up_w = spread(up_here)
    down_here = exchange(down_rows, GROUP_AXES)
    attn_parts = plane_back(attn_parts)
    cot_3 = shift(cot_split, 3)
    attn_parts, down_here, cot_3, cot_split = together(attn_parts, down_here, cot_3, cot_split)

    down_w = spread(down_here)
    middle, zhat, squares_a = middle_pass(layer_input, attn_parts)
    zhat_p = column_hop(zhat)
    zhat_p, gate_w, up_w, cot_split = together(zhat_p, gate_w, up_w, cot_split)
    zhat_p, cot_split = together(core_hop(zhat_p), cot_split)

    cot_p = (cot_split, cot_1, shift(cot_split, 2), cot_3)
    hidden, gate_slope, up_slope = hidden_pass(zhat_p, gate_w, up_w)
    hidden, cot_p, gate_slope, down_w = together(hidden, cot_p, gate_slope, down_w)

    cot_p = core_hop(cot_p)
    mlp_parts = core_back(by_cols_pass(hidden, down_w, 2, 2 * nz, "down_pass"))
    down_t = term_pass(cot_p, hidden, 2, 2)
    cot_p, mlp_parts, down_t = together(cot_p, mlp_parts, down_t)

    def side_sum(term):
        return lax.psum_scatter(term, SIDE_AXES, scatter_dimension=0, tiled=True)

    down_t = side_sum(down_t)
    mlp_2, mlp_3 = shift(mlp_parts[2], -2), shift(mlp_parts[3], -3)
    grad_gate, grad_up, *gz_parts = grad_hidden_pass(
        cot_p, gate_slope, up_slope, gate_w, up_w, down_w
    )
    gz_parts, grad_gate, mlp_2, mlp_3, mlp_parts = together(
        gz_parts, grad_gate, mlp_2, mlp_3, mlp_parts
    )

    gz_parts = core_back(gz_parts)
    mlp_1 = shift(mlp_parts[1], -1)
    gate_t = term_pass(zhat_p, grad_gate, 2, 2)
    gz_parts, gate_t, mlp_1, mlp_parts = together(gz_parts, gate_t, mlp_1, mlp_parts)

    gate_t = side_sum(gate_t)
    gz_parts = column_back(gz_parts)
    up_t = term_pass(zhat_p, grad_up, 2, 2)
    mlp_parts = (mlp_parts[0], mlp_1, mlp_2, mlp_3)
    layer_output, lanes = final_pass(middle, squares_a, mlp_parts, ndev)
    gathered = exchange(lanes, ALL_AXES)
    gz_parts, up_t, down_t, gathered = together(gz_parts, up_t, down_t, gathered)

    down_back = exchange(down_t, GROUP_AXES)
    grad_middle, grad_out = grad_middle_pass(middle, output_cotangent, gz_parts)
    grad_out_p = plane_hop(grad_out)
    grad_out_p, gate_t, down_back, up_t = together(grad_out_p, gate_t, down_back, up_t)
    grad_out_p, gate_t, up_t = together(core_hop(grad_out_p), gate_t, up_t)

    up_t = side_sum(up_t)
    gate_back = exchange(gate_t, GROUP_AXES)
    grad_qkv = attention_backward(grad_out_p, wo, query, key, value, *rows_info)
    gx_parts = core_back(by_cols_pass(grad_qkv, wq, 1, plane, "qkv_back_pass"))
    qkv_term = term_pass(normed_p, grad_qkv, 2, 1)
    gx_parts, qkv_term, gate_back, down_back, heads = together(
        gx_parts, qkv_term, gate_back, down_back, heads
    )

    out_term = term_pass(grad_out_p, heads, 2, 1)
    qkv_sum = exchange(qkv_term, ALL_AXES)
    gx_parts = plane_back(gx_parts)
    down_back = down_back.reshape(hgroups, mlp_rows, hchunk)
    down_grad = wide(down_back.transpose(1, 0, 2).reshape(mlp_rows, ff_local))
    gx_parts, qkv_sum, up_t, out_term, down_grad = together(
        gx_parts, qkv_sum, up_t, out_term, down_grad
    )

    out_term = lax.psum_scatter(out_term, "dp", scatter_dimension=0, tiled=True)
    up_back = exchange(up_t, GROUP_AXES)
    input_grad = input_grad_pass(layer_input, grad_middle, gx_parts)
    up_back, input_grad, out_term = together(up_back, input_grad, out_term)

    out_sum = exchange(out_term, PLANE_AXES)
    gate_up_grad, gain_sum = unpack_pass(gain_m, gate_up_weight, gate_back, up_back, hgroups)
    out_sum, gate_up_grad, gain_sum = together(out_sum, gate_up_grad, gain_sum)
    def plane_sum(arrived, cols):
        return jnp.sum(wide(arrived.reshape(nz, plane, d_rows, cols)), axis=0).transpose(1, 0, 2)

    qkv_sum = plane_sum(qkv_sum, own_cols)
    qkv_sum = jnp.concatenate(
        [
            qkv_sum[:, :, :q_cols].reshape(d_rows, -1),
            qkv_sum[:, :, q_cols : q_cols + kv_cols].reshape(d_rows, -1),
            qkv_sum[:, :, q_cols + kv_cols :].reshape(d_rows, -1),
        ],
        axis=1,
    )
    qkv_grad = qkv_sum * gain_a
    attn_gain_grad = jnp.sum(qkv_sum * wide(qkv_weight), axis=1)
    gain_halves = gain_sum.reshape(2, -1)
    gain_keep = jnp.where(x_at == 0, gain_halves[0], gain_halves[1])
    gain_send = jnp.where(x_at == 0, gain_halves[1], gain_halves[0])
    mlp_gain_grad = gain_keep + swap(gain_send[None, :], "uly")[0]

    out_sum = wide(out_sum).reshape(plane, d_rows, q_cols).transpose(1, 0, 2)
    out_weight_grad = out_sum.reshape(d_rows, -1)
    rms_values = jnp.sqrt(jnp.sum(gathered, axis=0)[:5] / (tok * ndev * D))
    return (
        layer_output,
        input_grad,
        qkv_grad,
        out_weight_grad,
        gate_up_grad,
        down_grad,
        attn_gain_grad,
        mlp_gain_grad,
        rms_values,
    )


def solution(mesh):
    sizes = dict(mesh.shape)
    if sizes["blk"] == 4 and sizes["uly"] == 2:
        mesh = Mesh(mesh.devices.reshape(sizes["dp"], 2, 2, 2), ALL_AXES)
        body, blk = plane_plan, ("yy", "cc")
    else:
        body, blk = general_plan, ("blk",)
    every = ("dp", *blk, "uly")
    rows = ("dp", *blk)
    return jax.shard_map(
        body,
        mesh=mesh,
        in_specs=(
            P(every, None),
            P("dp", None),
            P(every, None),
            P(every, None),
            P(rows, None, "uly"),
            P(rows, "uly"),
            P(every),
            P(every),
            P(every, None),
        ),
        out_specs=(
            P(every, None),
            P(every, None),
            P(every, None),
            P(every, None),
            P(rows, None, "uly"),
            P(rows, "uly"),
            P(every),
            P(every),
            P(),
        ),
        check_vma=False,
    )
```

```python
import functools

import jax
import jax.numpy as jnp
from jax import lax
from jax.experimental import pallas as pl
from jax.experimental.pallas import tpu as pltpu
from jax.sharding import Mesh
from jax.sharding import PartitionSpec as P

D = 2048
H = 16
KV = 8
HD = 128


EPSILON = 1e-06
ROPE_BASE = 1000000.0
MASKED = -1e30


def rms_scale(values, gain):
    return values * lax.rsqrt(jnp.mean(values * values, axis=-1, keepdims=True) + EPSILON) * gain


def rope_angles(positions):
    freq_index = jnp.arange(HD // 2, dtype=jnp.float32)
    inverse_freq = ROPE_BASE ** (-2.0 * freq_index / HD)
    return positions.astype(jnp.float32)[:, None] * inverse_freq[None, :]


def rotate_pairs(values, angles):
    half_size = values.shape[-1] // 2
    first_half = values[..., :half_size]
    second_half = values[..., half_size:]
    cosine = jnp.cos(angles)[:, None, :]
    sine = jnp.sin(angles)[:, None, :]
    return jnp.concatenate(
        [first_half * cosine - second_half * sine, second_half * cosine + first_half * sine],
        axis=-1,
    )


def sequence_positions(row_index, span_size, order_row):
    block_index = row_index // span_size
    picks = block_index[:, None] == jnp.arange(order_row.shape[0], dtype=jnp.int32)[None, :]
    chosen = jnp.sum(jnp.where(picks, order_row[None, :], 0), axis=1)
    return chosen * span_size + row_index % span_size


def contract_rows(left_side, right_side):
    return lax.dot_general(
        left_side, right_side, (((0,), (0,)), ((), ())), preferred_element_type=jnp.float32
    )


def contract_cols(left_side, right_side):
    return lax.dot_general(
        left_side, right_side, (((1,), (1,)), ((), ())), preferred_element_type=jnp.float32
    )


def general_plan(
    layer_input,
    span_order,
    qkv_weight,
    out_weight,
    gate_up_weight,
    down_weight,
    attn_gain,
    mlp_gain,
    output_cotangent,
):
    tok_rows = layer_input.shape[0]
    uly_size = lax.axis_size("uly")
    blk_size = lax.axis_size("blk")
    group_rows = tok_rows * uly_size
    seq_rows = group_rows * blk_size
    span_size = group_rows // 2
    order_row = span_order[0]
    local_kv = KV // uly_size
    local_heads = H // uly_size
    group_size = H // KV
    ff_local = down_weight.shape[1]
    score_scale = HD ** (-0.5)
    token_start = (lax.axis_index("blk") * uly_size + lax.axis_index("uly")) * tok_rows
    token_pos = sequence_positions(
        token_start + jnp.arange(tok_rows, dtype=jnp.int32), span_size, order_row
    )
    token_angles = rope_angles(token_pos)
    query_pos = sequence_positions(
        lax.axis_index("blk") * group_rows + jnp.arange(group_rows, dtype=jnp.int32),
        span_size,
        order_row,
    )
    stream_in = layer_input.astype(jnp.float32)
    qkv_full, out_full, attn_gain_full, mlp_gain_full = (
        lax.all_gather(qkv_weight, ("dp", "blk", "uly"), axis=0, tiled=True),
        lax.all_gather(out_weight, ("dp", "blk", "uly"), axis=0, tiled=True),
        lax.all_gather(attn_gain, ("dp", "blk", "uly"), axis=0, tiled=True),
        lax.all_gather(mlp_gain, ("dp", "blk", "uly"), axis=0, tiled=True),
    )
    gate_up_cols, down_cols = (
        lax.all_gather(gate_up_weight, ("dp", "blk"), axis=0, tiled=True),
        lax.all_gather(down_weight, ("dp", "blk"), axis=0, tiled=True),
    )
    attn_gain_wide = attn_gain_full.astype(jnp.float32)
    mlp_gain_wide = mlp_gain_full.astype(jnp.float32)
    normed_attn = rms_scale(stream_in, attn_gain_wide).astype(jnp.bfloat16)
    qkv_all = jnp.dot(normed_attn, qkv_full, preferred_element_type=jnp.float32)
    query_tok = (
        rotate_pairs(qkv_all[:, : H * HD].reshape(tok_rows, H, HD), token_angles)
        .reshape(tok_rows, H * HD)
        .astype(jnp.bfloat16)
    )
    key_tok = (
        rotate_pairs(qkv_all[:, H * HD : (H + KV) * HD].reshape(tok_rows, KV, HD), token_angles)
        .reshape(tok_rows, KV * HD)
        .astype(jnp.bfloat16)
    )
    value_tok = qkv_all[:, (H + KV) * HD :].astype(jnp.bfloat16)
    query_grp, key_grp, value_grp = (
        lax.all_to_all(query_tok, "uly", split_axis=1, concat_axis=0, tiled=True),
        lax.all_to_all(key_tok, "uly", split_axis=1, concat_axis=0, tiled=True),
        lax.all_to_all(value_tok, "uly", split_axis=1, concat_axis=0, tiled=True),
    )
    query_four = query_grp.reshape(group_rows, local_kv, group_size, HD)
    key_whole, value_whole = (
        lax.all_gather(key_grp, "blk", axis=0, tiled=True),
        lax.all_gather(value_grp, "blk", axis=0, tiled=True),
    )
    block_count = seq_rows // group_rows

    def take_block(block_index):
        offset = block_index * group_rows
        key_block = lax.dynamic_slice_in_dim(key_whole, offset, group_rows, 0).reshape(
            group_rows, local_kv, HD
        )
        value_block = lax.dynamic_slice_in_dim(value_whole, offset, group_rows, 0).reshape(
            group_rows, local_kv, HD
        )
        key_pos = sequence_positions(
            offset + jnp.arange(group_rows, dtype=jnp.int32), span_size, order_row
        )
        return (offset, key_block, value_block, key_pos)

    def attend_step(block_index, running):
        top_run, total_run, acc_run = running
        offset, key_block, value_block, key_pos = take_block(block_index)
        scores = (
            jnp.einsum("rkgd,pkd->kgrp", query_four, key_block, preferred_element_type=jnp.float32)
            * score_scale
        )
        allowed = key_pos[None, :] <= query_pos[:, None]
        scores = jnp.where(allowed, scores, MASKED)
        top_new = jnp.maximum(top_run, jnp.max(scores, axis=-1))
        weights = jnp.where(allowed, jnp.exp(scores - top_new[..., None]), 0.0)
        shrink_factor = jnp.exp(top_run - top_new)
        total_new = total_run * shrink_factor + jnp.sum(weights, axis=-1)
        acc_new = acc_run * shrink_factor[..., None] + jnp.einsum(
            "kgrp,pkd->kgrd",
            weights.astype(jnp.bfloat16),
            value_block,
            preferred_element_type=jnp.float32,
        )
        return (top_new, total_new, acc_new)

    start_state = (
        jnp.full((local_kv, group_size, group_rows), MASKED, jnp.float32),
        jnp.zeros((local_kv, group_size, group_rows), jnp.float32),
        jnp.zeros((local_kv, group_size, group_rows, HD), jnp.float32),
    )
    top_end, total_end, acc_end = lax.fori_loop(0, block_count, attend_step, start_state)
    log_total = top_end + jnp.log(total_end)
    head_rows = jnp.transpose(acc_end / total_end[..., None], (2, 0, 1, 3))
    heads_group = head_rows.reshape(group_rows, local_heads * HD).astype(jnp.bfloat16)
    heads_tok = lax.all_to_all(heads_group, "uly", split_axis=0, concat_axis=1, tiled=True)
    attn_out = contract_cols(heads_tok, out_full)
    middle = stream_in + attn_out
    normed_mlp = rms_scale(middle, mlp_gain_wide).astype(jnp.bfloat16)
    normed_grp, cotangent_grp = (
        lax.all_gather(normed_mlp, "uly", axis=0, tiled=True),
        lax.all_gather(output_cotangent, "uly", axis=0, tiled=True),
    )
    gate_up = jnp.einsum(
        "rd,dcf->rcf", normed_grp, gate_up_cols, preferred_element_type=jnp.float32
    )
    gate_part = gate_up[:, 0, :]
    up_part = gate_up[:, 1, :]
    hidden = (jax.nn.silu(gate_part) * up_part).astype(jnp.bfloat16)
    mlp_part = contract_cols(hidden, down_cols)
    mlp_out = lax.psum_scatter(
        mlp_part.astype(jnp.bfloat16), "uly", scatter_dimension=0, tiled=True
    ).astype(jnp.float32)
    final_stream = middle + mlp_out
    local_squares = jnp.stack(
        [
            jnp.sum(stream_in * stream_in),
            jnp.sum(attn_out * attn_out),
            jnp.sum(middle * middle),
            jnp.sum(mlp_out * mlp_out),
            jnp.sum(final_stream * final_stream),
        ]
    )
    total_squares = lax.psum(local_squares, ("dp", "blk", "uly"))
    entry_count = tok_rows * lax.axis_size("dp") * blk_size * uly_size * D
    rms_values = jnp.sqrt(total_squares / entry_count)
    grad_hidden = jnp.dot(cotangent_grp, down_cols, preferred_element_type=jnp.float32)
    sigmoid_gate = jax.nn.sigmoid(gate_part)
    grad_gate = grad_hidden * up_part * sigmoid_gate * (1.0 + gate_part * (1.0 - sigmoid_gate))
    grad_up = grad_hidden * gate_part * sigmoid_gate
    grad_gate_up = jnp.stack([grad_gate, grad_up], axis=1).astype(jnp.bfloat16)
    grad_normed_part = jnp.einsum(
        "rcf,dcf->rd", grad_gate_up, gate_up_cols, preferred_element_type=jnp.float32
    )
    grad_normed_mlp = lax.psum_scatter(
        grad_normed_part.astype(jnp.bfloat16), "uly", scatter_dimension=0, tiled=True
    ).astype(jnp.float32)
    gate_term = jnp.einsum(
        "rd,rcf->dcf", normed_grp, grad_gate_up, preferred_element_type=jnp.float32
    ).reshape(lax.axis_size(("dp", "blk")) * gate_up_weight.shape[0], 2 * ff_local)
    mlp_grads = lax.psum_scatter(
        jnp.concatenate([gate_term, contract_rows(cotangent_grp, hidden)], axis=1).astype(
            jnp.bfloat16
        ),
        ("dp", "blk"),
        scatter_dimension=0,
        tiled=True,
    ).astype(jnp.float32)
    gate_up_grad = mlp_grads[:, : 2 * ff_local].reshape(mlp_grads.shape[0], 2, ff_local)
    down_grad = mlp_grads[:, 2 * ff_local :]
    mlp_value, mlp_pull = jax.vjp(rms_scale, middle, mlp_gain_wide)
    grad_middle_norm, mlp_gain_grad_full = mlp_pull(grad_normed_mlp)
    grad_middle = output_cotangent.astype(jnp.float32) + grad_middle_norm
    grad_attn_out = grad_middle.astype(jnp.bfloat16)
    grad_heads_tok = jnp.dot(grad_attn_out, out_full, preferred_element_type=jnp.float32).astype(
        jnp.bfloat16
    )
    out_weight_term = contract_rows(grad_attn_out, heads_tok)
    grad_heads = lax.all_to_all(grad_heads_tok, "uly", split_axis=1, concat_axis=0, tiled=True)
    grad_four = grad_heads.reshape(group_rows, local_kv, group_size, HD)
    row_delta = jnp.transpose(
        jnp.sum(grad_four.astype(jnp.float32) * head_rows, axis=-1), (1, 2, 0)
    )

    def backward_step(block_index, running):
        grad_query_run, grad_key_all, grad_value_all = running
        offset, key_block, value_block, key_pos = take_block(block_index)
        scores = (
            jnp.einsum("rkgd,pkd->kgrp", query_four, key_block, preferred_element_type=jnp.float32)
            * score_scale
        )
        allowed = key_pos[None, :] <= query_pos[:, None]
        soft_probs = jnp.where(
            allowed, jnp.exp(jnp.where(allowed, scores, MASKED) - log_total[..., None]), 0.0
        )
        grad_probs = jnp.einsum(
            "rkgd,pkd->kgrp", grad_four, value_block, preferred_element_type=jnp.float32
        )
        grad_scores = (soft_probs * (grad_probs - row_delta[..., None])).astype(jnp.bfloat16)
        grad_query_run = (
            grad_query_run
            + jnp.einsum(
                "kgrp,pkd->kgrd", grad_scores, key_block, preferred_element_type=jnp.float32
            )
            * score_scale
        )
        grad_key_block = (
            jnp.einsum(
                "kgrp,rkgd->pkd", grad_scores, query_four, preferred_element_type=jnp.float32
            )
            * score_scale
        ).reshape(group_rows, local_kv * HD)
        grad_value_block = jnp.einsum(
            "kgrp,rkgd->pkd",
            soft_probs.astype(jnp.bfloat16),
            grad_four,
            preferred_element_type=jnp.float32,
        ).reshape(group_rows, local_kv * HD)
        grad_key_all = lax.dynamic_update_slice_in_dim(grad_key_all, grad_key_block, offset, 0)
        grad_value_all = lax.dynamic_update_slice_in_dim(
            grad_value_all, grad_value_block, offset, 0
        )
        return (grad_query_run, grad_key_all, grad_value_all)

    back_state = (
        jnp.zeros((local_kv, group_size, group_rows, HD), jnp.float32),
        jnp.zeros((seq_rows, local_kv * HD), jnp.float32),
        jnp.zeros((seq_rows, local_kv * HD), jnp.float32),
    )
    grad_query_end, grad_key_whole, grad_value_whole = lax.fori_loop(
        0, block_count, backward_step, back_state
    )
    grad_key_own, grad_value_own = (
        lax.psum_scatter(
            grad_key_whole.astype(jnp.bfloat16), "blk", scatter_dimension=0, tiled=True
        ).astype(jnp.float32),
        lax.psum_scatter(
            grad_value_whole.astype(jnp.bfloat16), "blk", scatter_dimension=0, tiled=True
        ).astype(jnp.float32),
    )
    grad_query_rows = (
        jnp.transpose(grad_query_end, (2, 0, 1, 3))
        .reshape(group_rows, local_heads * HD)
        .astype(jnp.bfloat16)
    )
    grad_query_tok, grad_key_tok, grad_value_tok = (
        lax.all_to_all(grad_query_rows, "uly", split_axis=0, concat_axis=1, tiled=True),
        lax.all_to_all(
            grad_key_own.astype(jnp.bfloat16), "uly", split_axis=0, concat_axis=1, tiled=True
        ),
        lax.all_to_all(
            grad_value_own.astype(jnp.bfloat16), "uly", split_axis=0, concat_axis=1, tiled=True
        ),
    )
    back_angles = rope_angles(-token_pos)
    grad_query_plain = rotate_pairs(
        grad_query_tok.astype(jnp.float32).reshape(tok_rows, H, HD), back_angles
    ).reshape(tok_rows, H * HD)
    grad_key_plain = rotate_pairs(
        grad_key_tok.astype(jnp.float32).reshape(tok_rows, KV, HD), back_angles
    ).reshape(tok_rows, KV * HD)
    grad_qkv = jnp.concatenate(
        [grad_query_plain, grad_key_plain, grad_value_tok.astype(jnp.float32)], axis=1
    ).astype(jnp.bfloat16)
    grad_normed_attn = contract_cols(grad_qkv, qkv_full)
    qkv_term = contract_rows(normed_attn, grad_qkv)
    attn_value, attn_pull = jax.vjp(rms_scale, stream_in, attn_gain_wide)
    grad_input_norm, attn_gain_grad_full = attn_pull(grad_normed_attn)
    input_grad = grad_middle + grad_input_norm
    qkv_grad, out_weight_grad, attn_gain_grad, mlp_gain_grad = (
        lax.psum_scatter(qkv_term, ("dp", "blk", "uly"), scatter_dimension=0, tiled=True),
        lax.psum_scatter(out_weight_term, ("dp", "blk", "uly"), scatter_dimension=0, tiled=True),
        lax.psum_scatter(
            attn_gain_grad_full, ("dp", "blk", "uly"), scatter_dimension=0, tiled=True
        ),
        lax.psum_scatter(mlp_gain_grad_full, ("dp", "blk", "uly"), scatter_dimension=0, tiled=True),
    )
    return (
        final_stream.astype(jnp.bfloat16),
        input_grad,
        qkv_grad,
        out_weight_grad,
        gate_up_grad,
        down_grad,
        attn_gain_grad,
        mlp_gain_grad,
        rms_values,
    )


ALL_AXES = ("dp", "yy", "cc", "uly")
SIDE_AXES = ("yy", "uly")
PLANE_AXES = ("yy", "cc", "uly")
GROUP_AXES = ("dp", "cc")
SWAP = [(0, 1), (1, 0)]
DIAGONAL = [(0, 3), (1, 2), (2, 1), (3, 0)]
VMEM_SPEC = pl.BlockSpec(memory_space=pltpu.VMEM)
SMEM_SPEC = pl.BlockSpec(memory_space=pltpu.SMEM)
KERNEL = dict(
    compiler_params=pltpu.CompilerParams(vmem_limit_bytes=58 * 1024 * 1024),
    cost_estimate=pl.CostEstimate(flops=1000, bytes_accessed=1000, transcendentals=0),
)
ROWS = 256
BY_ROWS = (((0,), (0,)), ((), ()))
BY_COLS = (((1,), (1,)), ((), ()))
PLAIN = (((1,), (0,)), ((), ()))


def wide(values):
    return values.astype(jnp.float32)


def low(values):
    return values.astype(jnp.bfloat16)


def dot32(left, right, dims=PLAIN):
    return lax.dot_general(left, right, dims, preferred_element_type=jnp.float32)


def low_shape(rows, cols):
    return jax.ShapeDtypeStruct((rows, cols), jnp.bfloat16)


def wide_shape(rows, cols):
    return jax.ShapeDtypeStruct((rows, cols), jnp.float32)


def once(shape):
    return pl.BlockSpec(shape, lambda *i: (0,) * len(shape), pipeline_mode=pl.Buffered(1))


def row_block(step):
    return pl.ds(pl.multiple_of(step * ROWS, ROWS), ROWS)


def head_cut(head):
    return slice(head * HD, (head + 1) * HD)


def join_rows(pieces, out):
    rows = pieces[0].shape[0]
    for number, piece in enumerate(pieces):
        out[number * rows : (number + 1) * rows, :] = piece[...]


def turn(values, cosine, sine):
    return values * cosine + pltpu.roll(values, HD // 2, 1) * sine


def softmax_rows(query, key, start):
    scores = dot32(query, key, BY_COLS) * HD ** (-0.5)
    row = lax.broadcasted_iota(jnp.int32, scores.shape, 0) + start
    scores = jnp.where(lax.broadcasted_iota(jnp.int32, scores.shape, 1) <= row, scores, MASKED)
    weights = jnp.exp(scores - jnp.max(scores, axis=1, keepdims=True))
    return weights * (1.0 / jnp.sum(weights, axis=1, keepdims=True))


def rows_at(block, size):
    return pl.ds(pl.multiple_of(block * size, size), size)


def attention_forward_body(group, place, weight, cosine, sine, *refs):
    pieces, (query_out, key_out, value_out, heads_out, normed) = refs[:-5], refs[-5:]
    join_rows(pieces, normed)
    size, rows = pieces[0].shape[0], normed.shape[0]

    def project(step, carry):
        at = rows_at(step, 2 * size)
        qkv = dot32(normed[at, :], weight[...])
        turned = [
            low(turn(qkv[:, head_cut(head)], cosine[at, :], sine[at, :]))
            for head in range(group + 1)
        ]
        value = low(qkv[:, head_cut(group + 1)])
        for part in (0, 1):
            own, to = slice(part * size, (part + 1) * size), rows_at(place[2 * step + part], size)
            for head in range(group):
                query_out[to, head_cut(head)] = turned[head][own]
            key_out[to, :] = turned[group][own]
            value_out[to, :] = value[own]
        return carry

    lax.fori_loop(0, rows // (2 * size), project, 0)
    blocks = rows // size
    for start in range(0, rows, ROWS):
        at, seen = slice(start, start + ROWS), slice(0, start + ROWS)
        for head in range(group):
            probs = softmax_rows(query_out[at, head_cut(head)], key_out[seen, :], start)
            result = low(dot32(low(probs), value_out[seen, :]))
            for part in range(ROWS // size):
                to = rows_at(place[blocks + start // size + part], size)
                own = slice(part * size, (part + 1) * size)
                heads_out[to, head_cut(head)] = result[own]


def attention_forward(pieces, weight, cosine, sine, place):
    rows, group = cosine.shape[0], weight.shape[1] // HD - 2
    return pl.pallas_call(
        functools.partial(attention_forward_body, group),
        out_shape=(
            low_shape(rows, group * HD),
            low_shape(rows, HD),
            low_shape(rows, HD),
            low_shape(rows, group * HD),
        ),
        in_specs=[SMEM_SPEC] + [VMEM_SPEC] * (3 + len(pieces)),
        out_specs=(VMEM_SPEC,) * 4,
        scratch_shapes=[pltpu.VMEM((rows, weight.shape[0]), jnp.bfloat16)],
        name="attention_forward",
        **KERNEL,
    )(place, weight, cosine, sine, *pieces)


def attention_backward_body(group, place, weight, query, key, value, cosine, sine, *refs):
    pieces, (grad_qkv, grad_out, key_sum, value_sum) = refs[:-4], refs[-4:]
    size, rows = pieces[0].shape[0], query.shape[0]
    blocks = rows // size
    for number, piece in enumerate(pieces):
        grad_out[rows_at(place[number], size), :] = piece[...]
    key_sum[...] = jnp.zeros_like(key_sum)
    value_sum[...] = jnp.zeros_like(value_sum)

    def store_turned(start, values, cut, back):
        for part in range(values.shape[0] // size):
            to = rows_at(place[blocks + start // size + part], size)
            own = values[part * size : (part + 1) * size]
            if back:
                own = low(turn(wide(own), cosine[to, :], -sine[to, :]))
            grad_qkv[to, cut] = own

    for start in range(0, rows, ROWS):
        at, seen = slice(start, start + ROWS), slice(0, start + ROWS)
        grad_heads = low(dot32(grad_out[at, :], weight[...]))
        for head in range(group):
            cut = head_cut(head)
            probs = softmax_rows(query[at, cut], key[seen, :], start)
            grad_probs = dot32(grad_heads[:, cut], value[seen, :], BY_COLS)
            delta = jnp.sum(probs * grad_probs, axis=1, keepdims=True)
            grad_scores = low(probs * (grad_probs - delta))
            store_turned(start, low(dot32(grad_scores, key[seen, :]) * HD ** (-0.5)), cut, True)
            key_sum[seen, :] += dot32(grad_scores, query[at, cut], BY_ROWS)
            value_sum[seen, :] += dot32(low(probs), grad_heads[:, cut], BY_ROWS)
    for start in range(0, rows, ROWS):
        at = slice(start, start + ROWS)
        store_turned(start, low(key_sum[at, :] * HD ** (-0.5)), head_cut(group), True)
        store_turned(start, low(value_sum[at, :]), head_cut(group + 1), False)


def attention_backward(pieces, weight, query, key, value, cosine, sine, place):
    rows, group = query.shape[0], query.shape[1] // HD
    return pl.pallas_call(
        functools.partial(attention_backward_body, group),
        out_shape=low_shape(rows, (group + 2) * HD),
        in_specs=[SMEM_SPEC] + [VMEM_SPEC] * (6 + len(pieces)),
        out_specs=VMEM_SPEC,
        scratch_shapes=[pltpu.VMEM((rows, weight.shape[0]), jnp.bfloat16)]
        + [pltpu.VMEM((rows, HD), jnp.float32)] * 2,
        name="attention_backward",
        **KERNEL,
    )(place, weight, query, key, value, cosine, sine, *pieces)


def stripes(weight, parts, number):
    depth = weight.shape[0] // parts**2 // ROWS

    def place(x, step):
        at = jnp.clip(step - number, 0, parts * depth - 1)
        return ((at // depth * parts + x) * depth + at % depth, 0)

    shape = (ROWS, weight.shape[1])
    return [pl.BlockSpec(shape, functools.partial(place, x)) for x in range(parts)]


def stripe_dot(rows, refs):
    weight = [ref[...] for ref in refs]
    weight = weight[0] if len(refs) == 1 else jnp.concatenate(weight, axis=1)
    return dot32(rows[...], weight, BY_COLS)


def store_rows(outs, values):
    rows = outs[0].shape[0]
    for number, out in enumerate(outs):
        out[...] = values[number * rows : (number + 1) * rows, :]


def by_cols_body(parts, rows, *refs):
    store_rows(refs[parts:], low(stripe_dot(rows, refs[:parts])))


def by_cols_pass(rows, weight, parts, blocks, name):
    width = weight.shape[0] // parts
    block = rows.shape[0] // blocks
    return pl.pallas_call(
        functools.partial(by_cols_body, parts),
        grid=(width // ROWS,),
        out_shape=(low_shape(block, width),) * blocks,
        in_specs=[once(rows.shape), *stripes(weight, parts, 0)],
        out_specs=(pl.BlockSpec((block, ROWS), lambda step: (0, step)),) * blocks,
        name=name,
        **KERNEL,
    )(rows, *[weight] * parts)


def by_halves(weight):
    return weight.reshape(2, 2, weight.shape[0] // 4, weight.shape[1])


def columns_of(weight):
    def place(step):
        at = jnp.minimum(step, 3)
        return (0, at // 2, 0, at % 2)

    return pl.BlockSpec((2, 1, weight.shape[0] // 4, weight.shape[1] // 2), place)


def column_dot(rows, ref):
    return dot32(rows[...], ref[...].reshape(rows.shape[1], ref.shape[3]))


def hidden_body(gate_w, up_w, *refs):
    normed_p, (hidden_out, gate_slope, up_slope, normed) = refs[:-4], refs[-4:]

    @pl.when(pl.program_id(0) == 0)
    def _():
        join_rows(normed_p, normed)

    gate, up = column_dot(normed, gate_w), column_dot(normed, up_w)
    sig = jax.nn.sigmoid(gate)
    act = gate * sig
    hidden_out[...] = low(act * up)
    gate_slope[...] = low(up * (sig + act * (1.0 - sig)))
    up_slope[...] = low(act)


def hidden_pass(normed_p, gate_w, up_w):
    rows, width = len(normed_p) * normed_p[0].shape[0], normed_p[0].shape[1]
    units = 2 * gate_w.shape[1]
    return pl.pallas_call(
        hidden_body,
        grid=(4,),
        out_shape=(low_shape(rows, units),) * 3,
        in_specs=[columns_of(gate_w), columns_of(up_w)] + [once(v.shape) for v in normed_p],
        out_specs=(pl.BlockSpec((rows, units // 4), lambda step: (0, step)),) * 3,
        scratch_shapes=[pltpu.VMEM((rows, width), jnp.bfloat16)],
        name="hidden_pass",
        **KERNEL,
    )(by_halves(gate_w), by_halves(up_w), *normed_p)


def grad_hidden_body(down_w, gate_slope, up_slope, *refs):
    stripe_refs, refs = refs[:4], refs[4:]
    count = (len(refs) - 4) // 2
    cot_p, (grad_gate_out, grad_up_out, *outs) = refs[:count], refs[count:-2]
    cot, grads = refs[-2:]
    step, chunk = pl.program_id(0), grad_gate_out.shape[1]

    @pl.when(step == 0)
    def _():
        join_rows(cot_p, cot)

    for number in range(4):

        @pl.when(step == number)
        def _(number=number):
            grad_hidden = column_dot(cot, down_w)
            slopes = (gate_slope, up_slope), (grad_gate_out, grad_up_out)
            for part, (slope, out) in enumerate(zip(*slopes)):
                grad = low(grad_hidden * wide(slope[...]))
                out[...] = grad
                start = (4 * part + number) * chunk
                grads[:, start : start + chunk] = grad

    @pl.when(step >= 4)
    def _():
        weight = jnp.concatenate([ref[...] for ref in stripe_refs], axis=1)
        store_rows(outs, low(dot32(grads[...], weight, BY_COLS)))


def grad_hidden_pass(cot_p, gate_slope, up_slope, gate_w, up_w, down_w):
    rows, width = len(cot_p) * cot_p[0].shape[0], cot_p[0].shape[1]
    units = 2 * gate_w.shape[1]
    quarter = pl.BlockSpec((rows, units // 4), lambda step: (0, jnp.minimum(step, 3)))
    stripe = pl.BlockSpec((cot_p[0].shape[0], ROWS), lambda step: (0, jnp.maximum(step - 4, 0)))
    return pl.pallas_call(
        grad_hidden_body,
        grid=(4 + width // ROWS,),
        out_shape=(low_shape(rows, units),) * 2 + tuple(low_shape(*v.shape) for v in cot_p),
        in_specs=[columns_of(down_w)]
        + [quarter] * 2
        + stripes(gate_w, 2, 4)
        + stripes(up_w, 2, 4)
        + [once(v.shape) for v in cot_p],
        out_specs=(quarter,) * 2 + (stripe,) * len(cot_p),
        scratch_shapes=[pltpu.VMEM((rows, width), jnp.bfloat16)]
        + [pltpu.VMEM((rows, 2 * units), jnp.bfloat16)],
        name="grad_hidden_pass",
        **KERNEL,
    )(by_halves(down_w), gate_slope, up_slope, gate_w, gate_w, up_w, up_w, *cot_p)


def term_body(*refs):
    pieces, columns, out = refs[:-2], refs[-2], refs[-1]
    rows = jnp.concatenate([piece[...] for piece in pieces], axis=0)
    out[...] = low(dot32(rows, columns[...], BY_ROWS))


def term_pass(pieces, columns, row_parts, col_parts):
    tokens, width = pieces[0].shape
    depth, chunk = width // row_parts, columns.shape[1] // col_parts
    return pl.pallas_call(
        term_body,
        grid=(row_parts, col_parts),
        out_shape=low_shape(width * col_parts, chunk),
        in_specs=[pl.BlockSpec((tokens, depth), lambda y, x: (0, y))] * len(pieces)
        + [pl.BlockSpec((columns.shape[0], chunk), lambda y, x: (0, x))],
        out_specs=pl.BlockSpec((depth, chunk), lambda y, x: (y * col_parts + x, 0)),
        name="term_pass",
        **KERNEL,
    )(*pieces, columns)


def unit_scale(values):
    return lax.rsqrt(jnp.mean(values * values, axis=-1, keepdims=True) + EPSILON)


def norm_pull(values, grad_scaled):
    scale = unit_scale(values)
    mean = jnp.mean(grad_scaled * values, axis=-1, keepdims=True)
    return scale * grad_scaled - values * (scale * scale * scale) * mean


def pick(bit, near, far):
    return jnp.where(bit == 0, near, far)


def to_split(values):
    step = values.shape[1] // 8
    cuts = [values[:, at * step : (at + 1) * step] for at in range(8)]
    return jnp.concatenate(cuts[0::2] + cuts[1::2], axis=1)


def from_split(values):
    step = values.shape[1] // 8
    cuts = [values[:, at * step : (at + 1) * step] for at in range(8)]
    return jnp.concatenate([cut for pair in zip(cuts[:4], cuts[4:]) for cut in pair], axis=1)


def column_sums(*arrays):
    return jnp.concatenate([jnp.sum(v * v, axis=0, keepdims=True) for v in arrays], axis=0)


def summed(parts):
    total = wide(parts[0][...])
    for part in parts[1:]:
        total += wide(part[...])
    return total


def prepare_body(stream_in, cot, normed_out, cot_out):
    rows = wide(stream_in[...])
    normed_out[...] = low(rows * unit_scale(rows))
    cot_out[...] = to_split(cot[...])


def prepare_pass(stream_in, cot):
    return pl.pallas_call(
        prepare_body,
        out_shape=(low_shape(*stream_in.shape), low_shape(*cot.shape)),
        in_specs=[VMEM_SPEC] * 2,
        out_specs=(VMEM_SPEC,) * 2,
        name="prepare_pass",
        **KERNEL,
    )(stream_in, cot)


def middle_body(stream_in, *refs):
    parts, (middle_out, normed_out, squares_out) = refs[:-3], refs[-3:]
    attn_out, rows = summed(parts), wide(stream_in[...])
    middle = rows + attn_out
    middle_out[...] = middle
    normed_out[...] = to_split(low(middle * unit_scale(middle)))
    squares_out[...] = column_sums(rows, attn_out, middle)


def middle_pass(stream_in, parts):
    rows, width = stream_in.shape
    return pl.pallas_call(
        middle_body,
        out_shape=(wide_shape(rows, width), low_shape(rows, width), wide_shape(3, width)),
        in_specs=[VMEM_SPEC] * (1 + len(parts)),
        out_specs=(VMEM_SPEC,) * 3,
        name="middle_pass",
        **KERNEL,
    )(stream_in, *parts)


def final_body(middle, squares_a, *refs):
    parts, (layer_out, sums_out) = refs[:-2], refs[-2:]
    mlp_out = from_split(summed(parts))
    final = middle[...] + mlp_out
    layer_out[...] = low(final)
    squares = jnp.concatenate([squares_a[...], column_sums(mlp_out, final)], axis=0)
    sums = jnp.sum(squares, axis=1, keepdims=True)
    lane = lax.broadcasted_iota(jnp.int32, (1, sums_out.shape[1]), 1)
    total = jnp.zeros((1, sums_out.shape[1]), jnp.float32)
    for number in range(sums.shape[0]):
        total += jnp.where(lane == number, sums[number : number + 1, :], 0.0)
    sums_out[...] = jnp.broadcast_to(total, sums_out.shape)


def final_pass(middle, squares_a, parts, copies):
    rows, width = middle.shape
    return pl.pallas_call(
        final_body,
        out_shape=(low_shape(rows, width), wide_shape(copies, 128)),
        in_specs=[VMEM_SPEC] * (2 + len(parts)),
        out_specs=(VMEM_SPEC,) * 2,
        name="final_pass",
        **KERNEL,
    )(middle, squares_a, *parts)


def grad_middle_body(middle, cot, *refs):
    parts, (grad_out, low_out) = refs[:-2], refs[-2:]
    grad_normed = from_split(summed(parts))
    grad = wide(cot[...]) + norm_pull(middle[...], grad_normed)
    grad_out[...] = grad
    low_out[...] = low(grad)


def grad_middle_pass(middle, cot, parts):
    rows, width = middle.shape
    return pl.pallas_call(
        grad_middle_body,
        out_shape=(wide_shape(rows, width), low_shape(rows, width)),
        in_specs=[VMEM_SPEC] * (2 + len(parts)),
        out_specs=(VMEM_SPEC,) * 2,
        name="grad_middle_pass",
        **KERNEL,
    )(middle, cot, *parts)


def input_grad_body(stream_in, grad_middle, *refs):
    parts, out = refs[:-1], refs[-1]
    out[...] = grad_middle[...] + norm_pull(wide(stream_in[...]), summed(parts))


def input_grad_pass(stream_in, grad_middle, parts):
    return pl.pallas_call(
        input_grad_body,
        out_shape=wide_shape(*stream_in.shape),
        in_specs=[VMEM_SPEC] * (2 + len(parts)),
        out_specs=VMEM_SPEC,
        name="input_grad_pass",
        **KERNEL,
    )(stream_in, grad_middle, *parts)


def pack_body(gain, gate_up, out):
    out[...] = low(wide(gate_up[:, 0, :]) * gain[...])


def pack_more_body(gain, gate_up, down, up_out, down_out):
    up_out[...] = low(wide(gate_up[:, 1, :]) * gain[...])
    down_out[...] = down[...]


def pack_pass(body, outs, groups, gain, gate_up, *down):
    rows, chunk = gate_up.shape[0], gate_up.shape[2] // groups
    return pl.pallas_call(
        body,
        grid=(groups,),
        out_shape=(low_shape(groups * rows, chunk),) * outs,
        in_specs=[
            pl.BlockSpec((rows, 1), lambda g: (0, 0)),
            pl.BlockSpec((rows, 2, chunk), lambda g: (0, 0, g)),
        ]
        + [pl.BlockSpec((rows, chunk), lambda g: (0, g))] * len(down),
        out_specs=(pl.BlockSpec((rows, chunk), lambda g: (g, 0)),) * outs,
        name="pack_pass",
        **KERNEL,
    )(gain, gate_up, *down)


def qkv_pack_body(gain, query, key, value, out):
    start = 0
    for part in (query, key, value):
        cut = slice(start, start + part.shape[1])
        rows = low(wide(part[...]) * gain[...])
        for plane in range(out.shape[0]):
            out[plane, 0, :, cut] = rows
        start += part.shape[1]


def qkv_pack_pass(gain, weight, planes, groups):
    rows = weight.shape[0]
    query, rest = H * HD // groups, KV * HD // groups
    first = H * HD // rest
    block = (planes, 1, rows, query + 2 * rest)
    out = pl.pallas_call(
        qkv_pack_body,
        grid=(groups,),
        out_shape=jax.ShapeDtypeStruct((planes, groups, *block[2:]), jnp.bfloat16),
        in_specs=[
            pl.BlockSpec((rows, 1), lambda g: (0, 0)),
            pl.BlockSpec((rows, query), lambda g: (0, g)),
            pl.BlockSpec((rows, rest), lambda g: (0, first + g)),
            pl.BlockSpec((rows, rest), lambda g: (0, first + groups + g)),
        ],
        out_specs=pl.BlockSpec(block, lambda g: (0, g, 0, 0)),
        name="qkv_pack_pass",
        **KERNEL,
    )(gain, weight, weight, weight)
    return out.reshape(-1, block[3])


def unpack_body(gain, weight, gate, up, out, gain_sum):
    gate_term, up_term = wide(gate[...]), wide(up[...])
    out[:, 0, :] = gate_term * gain[...]
    out[:, 1, :] = up_term * gain[...]
    products = gate_term * wide(weight[:, 0, :]) + up_term * wide(weight[:, 1, :])
    total = jnp.sum(products, axis=1, keepdims=True)

    @pl.when(pl.program_id(0) == 0)
    def _():
        gain_sum[...] = total

    @pl.when(pl.program_id(0) > 0)
    def _():
        gain_sum[...] += total


def unpack_pass(gain, weight, gate, up, groups):
    rows, chunk = weight.shape[0], weight.shape[2] // groups
    column = pl.BlockSpec((rows, 1), lambda g: (0, 0))
    pair = pl.BlockSpec((rows, 2, chunk), lambda g: (0, 0, g))
    by_group = pl.BlockSpec((rows, chunk), lambda g: (g, 0))
    return pl.pallas_call(
        unpack_body,
        grid=(groups,),
        out_shape=(jax.ShapeDtypeStruct(weight.shape, jnp.float32), wide_shape(rows, 1)),
        in_specs=[column, pair, by_group, by_group],
        out_specs=(pair, column),
        name="unpack_pass",
        **KERNEL,
    )(gain, weight, gate, up)


def side_by_side_body(part, out):
    out[...] = wide(part[...])


def side_by_side(values, groups):
    rows, cols = values.shape[0] // groups, values.shape[1]
    return pl.pallas_call(
        side_by_side_body,
        grid=(groups,),
        out_shape=wide_shape(rows, groups * cols),
        in_specs=[pl.BlockSpec((rows, cols), lambda g: (g, 0))],
        out_specs=pl.BlockSpec((rows, cols), lambda g: (0, g)),
        name="side_by_side",
        **KERNEL,
    )(values)


def exchange(values, axes):
    return lax.all_to_all(values, axes, split_axis=0, concat_axis=0, tiled=True)


def after(values, *earlier):
    return lax.optimization_barrier((values, *earlier))[0]


def together(*values):
    return lax.optimization_barrier(values)


def swap(values, *axes):
    pairs = SWAP if len(axes) == 1 else DIAGONAL
    return lax.ppermute(values, axes if len(axes) > 1 else axes[0], pairs)


def plane_hop(rows):
    return (rows, swap(rows, "uly"), swap(rows, "yy"), swap(rows, "yy", "uly"))


def plane_back(parts):
    return (parts[0], swap(parts[1], "uly"), swap(parts[2], "yy"), swap(parts[3], "yy", "uly"))


def shift(values, by):
    count = lax.axis_size("dp")
    return lax.ppermute(values, "dp", [(i, (i + by) % count) for i in range(count)])


def column_hop(rows):
    return (rows, *(shift(rows, by) for by in range(1, lax.axis_size("dp"))))


def column_back(parts):
    return (parts[0], *(shift(v, -by) for by, v in enumerate(parts[1:], 1)))


def core_hop(pieces):
    return (*pieces, *(swap(v, "cc") for v in pieces))


def add_body(*refs):
    count = len(refs) // 3
    for left, right, out in zip(refs[:count], refs[count : 2 * count], refs[2 * count :]):
        out[...] = low(wide(left[...]) + wide(right[...]))


def core_back(blocks):
    half = len(blocks) // 2
    arrived = [swap(v, "cc") for v in blocks[half:]]
    return pl.pallas_call(
        add_body,
        out_shape=tuple(low_shape(*v.shape) for v in arrived),
        in_specs=[VMEM_SPEC] * (2 * half),
        out_specs=(VMEM_SPEC,) * half,
        name="add_pass",
        **KERNEL,
    )(*blocks[:half], *arrived)


def plane_plan(
    layer_input,
    span_order,
    qkv_weight,
    out_weight,
    gate_up_weight,
    down_weight,
    attn_gain,
    mlp_gain,
    output_cotangent,
):
    tok = layer_input.shape[0]
    nz = lax.axis_size("dp")
    ndev = lax.axis_size(ALL_AXES)
    plane = ndev // nz
    span_size = tok * plane // span_order.shape[1]
    y_at, c_at, x_at = lax.axis_index("yy"), lax.axis_index("cc"), lax.axis_index("uly")
    q_cols, kv_cols = H * HD // plane, KV * HD // plane
    own_cols = q_cols + 2 * kv_cols
    d_rows = qkv_weight.shape[0]
    mlp_rows, ff_local = down_weight.shape
    hgroups = lax.axis_size(GROUP_AXES)
    hchunk = ff_local // hgroups

    gain_peer = swap(mlp_gain[None, :], "uly")
    gain_own, gain_peer = wide(mlp_gain)[None, :], wide(gain_peer)
    gain_m = pick(
        x_at,
        jnp.concatenate([gain_own, gain_peer], axis=1),
        jnp.concatenate([gain_peer, gain_own], axis=1),
    ).reshape(mlp_rows, 1)
    (gate_rows,) = pack_pass(pack_body, 1, hgroups, gain_m, gate_up_weight)
    out_rows = out_weight.reshape(d_rows, plane, q_cols).transpose(1, 0, 2).reshape(-1, q_cols)
    out_here = exchange(out_rows, PLANE_AXES)
    normed, cot_split = prepare_pass(layer_input, output_cotangent)
    gate_rows, gain_m, out_here, normed, cot_split, qkv_weight, down_weight = together(
        gate_rows, gain_m, out_here, normed, cot_split, qkv_weight, down_weight
    )

    def spread(here):
        return lax.all_gather(here, SIDE_AXES, axis=0, tiled=True)

    wo = lax.all_gather(out_here, "dp", axis=0, tiled=True)
    gate_here = exchange(gate_rows, GROUP_AXES)
    normed_p = plane_hop(normed)
    gain_a = wide(attn_gain)[:, None]
    qkv_rows = qkv_pack_pass(gain_a, qkv_weight, nz, plane)
    up_rows, down_rows = pack_pass(
        pack_more_body, 2, hgroups, gain_m, gate_up_weight, down_weight
    )
    gate_here, normed_p, qkv_rows, up_rows, down_rows, cot_split = together(
        gate_here, normed_p, qkv_rows, up_rows, down_rows, cot_split
    )

    block = jnp.arange(plane, dtype=jnp.int32)
    core_of, y_of, x_of = (block // 4) ^ c_at, (block // 2) % 2 ^ y_at, block % 2 ^ x_at
    stored = (y_of * 2 + core_of) * 2 + x_of
    row_at = (stored[:, None] * tok + jnp.arange(tok, dtype=jnp.int32)[None, :]).reshape(-1)
    positions = sequence_positions(row_at, span_size, span_order[0])
    angles = rope_angles(positions)
    cosine = jnp.concatenate([jnp.cos(angles)] * 2, axis=1)
    sine = jnp.concatenate([-jnp.sin(angles), jnp.sin(angles)], axis=1)
    gate_w = spread(gate_here)
    wq = exchange(qkv_rows, ALL_AXES)
    normed_p = core_hop(normed_p)
    place = positions[::tok] // span_size
    ordered = place[None, :] == block[:, None]
    place = jnp.concatenate([place, jnp.sum(jnp.where(ordered, block[None, :], 0), axis=1)])
    rows_info = (cosine, sine, place)
    wq, normed_p, up_rows, rows_info = together(wq, normed_p, up_rows, rows_info)

    up_here = exchange(up_rows, GROUP_AXES)
    query, key, value, heads = attention_forward(normed_p, wq, *rows_info)
    attn_parts = core_back(by_cols_pass(heads, wo, 1, plane, "out_pass"))
    up_here, attn_parts, down_rows, cot_split = together(
        up_here, attn_parts, down_rows, cot_split
    )

    up_w = spread(up_here)
    down_here = exchange(down_rows, GROUP_AXES)
    attn_parts = plane_back(attn_parts)
    cot_3 = shift(cot_split, 3)
    attn_parts, down_here, cot_3, cot_split = together(attn_parts, down_here, cot_3, cot_split)

    middle, zhat, squares_a = middle_pass(layer_input, attn_parts)
    zhat, down_here = together(zhat, down_here)
    down_w = spread(down_here)
    zhat_p = core_hop(column_hop(zhat))
    zhat_p, gate_w, up_w, cot_split = together(zhat_p, gate_w, up_w, cot_split)

    cot_2 = shift(cot_split, 2)
    hidden, gate_slope, up_slope = hidden_pass(zhat_p, gate_w, up_w)
    hidden, cot_2, cot_split, gate_slope, down_w = together(
        hidden, cot_2, cot_split, gate_slope, down_w
    )

    cot_p = core_hop((cot_split, shift(cot_split, 1), cot_2, cot_3))
    mlp_parts = core_back(by_cols_pass(hidden, down_w, 2, 2 * nz, "down_pass"))
    cot_p, mlp_parts = together(cot_p, mlp_parts)
    mlp_1 = shift(mlp_parts[1], -1)
    down_t = term_pass(cot_p, hidden, 2, 2)
    mlp_1, mlp_parts, down_t = together(mlp_1, mlp_parts, down_t)

    def side_sum(term):
        return lax.psum_scatter(term, SIDE_AXES, scatter_dimension=0, tiled=True)

    down_t = side_sum(down_t)
    mlp_2 = shift(mlp_parts[2], -2)
    grad_gate, grad_up, *gz_parts = grad_hidden_pass(
        cot_p, gate_slope, up_slope, gate_w, up_w, down_w
    )
    gz_parts, grad_gate, mlp_2, mlp_parts = together(gz_parts, grad_gate, mlp_2, mlp_parts)

    gz_parts = core_back(gz_parts)
    mlp_3 = shift(mlp_parts[3], -3)
    gate_t = term_pass(zhat_p, grad_gate, 2, 2)
    gz_parts, gate_t, mlp_3, mlp_parts = together(gz_parts, gate_t, mlp_3, mlp_parts)

    gate_t = side_sum(gate_t)
    gz_parts = column_back(gz_parts)
    up_t = term_pass(zhat_p, grad_up, 2, 2)
    mlp_parts = (mlp_parts[0], mlp_1, mlp_2, mlp_3)
    layer_output, lanes = final_pass(middle, squares_a, mlp_parts, ndev)
    gathered = exchange(lanes, ALL_AXES)
    gz_parts, up_t, down_t, gathered = together(gz_parts, up_t, down_t, gathered)

    down_back = exchange(down_t, GROUP_AXES)
    grad_middle, grad_out = grad_middle_pass(middle, output_cotangent, gz_parts)
    grad_out_p = plane_hop(grad_out)
    grad_out_p, gate_t, down_back, up_t = together(grad_out_p, gate_t, down_back, up_t)
    grad_out_p, gate_t, up_t = together(core_hop(grad_out_p), gate_t, up_t)

    up_t = side_sum(up_t)
    gate_back = exchange(gate_t, GROUP_AXES)
    grad_qkv = attention_backward(grad_out_p, wo, query, key, value, *rows_info)
    gx_parts = core_back(by_cols_pass(grad_qkv, wq, 1, plane, "qkv_back_pass"))
    qkv_term = term_pass(normed_p, grad_qkv, 2, 1)
    gx_parts, qkv_term, gate_back, down_back, heads = together(
        gx_parts, qkv_term, gate_back, down_back, heads
    )

    out_term = term_pass(grad_out_p, heads, 2, 1)
    qkv_sum = exchange(qkv_term, ALL_AXES)
    gx_parts = plane_back(gx_parts)
    down_grad = side_by_side(down_back, hgroups)
    gx_parts, qkv_sum, up_t, out_term, down_grad = together(
        gx_parts, qkv_sum, up_t, out_term, down_grad
    )

    out_term = lax.psum_scatter(out_term, "dp", scatter_dimension=0, tiled=True)
    up_back = exchange(up_t, GROUP_AXES)
    input_grad = input_grad_pass(layer_input, grad_middle, gx_parts)

    def plane_sum(arrived, cols):
        return jnp.sum(wide(arrived.reshape(nz, plane, d_rows, cols)), axis=0).transpose(1, 0, 2)

    qkv_sum = plane_sum(qkv_sum, own_cols)
    qkv_sum = jnp.concatenate(
        [
            qkv_sum[:, :, :q_cols].reshape(d_rows, -1),
            qkv_sum[:, :, q_cols : q_cols + kv_cols].reshape(d_rows, -1),
            qkv_sum[:, :, q_cols + kv_cols :].reshape(d_rows, -1),
        ],
        axis=1,
    )
    qkv_grad = qkv_sum * gain_a
    attn_gain_grad = jnp.sum(qkv_sum * wide(qkv_weight), axis=1)
    up_back, input_grad, out_term, qkv_grad, attn_gain_grad = together(
        up_back, input_grad, out_term, qkv_grad, attn_gain_grad
    )

    out_sum = exchange(out_term, PLANE_AXES)
    gate_up_grad, gain_sum = unpack_pass(gain_m, gate_up_weight, gate_back, up_back, hgroups)
    out_sum, gate_up_grad, gain_sum = together(out_sum, gate_up_grad, gain_sum)
    gain_halves = gain_sum.reshape(2, -1)
    gain_keep = jnp.where(x_at == 0, gain_halves[0], gain_halves[1])
    gain_send = jnp.where(x_at == 0, gain_halves[1], gain_halves[0])
    mlp_gain_grad = gain_keep + swap(gain_send[None, :], "uly")[0]

    out_sum = wide(out_sum).reshape(plane, d_rows, q_cols).transpose(1, 0, 2)
    out_weight_grad = out_sum.reshape(d_rows, -1)
    rms_values = jnp.sqrt(jnp.sum(gathered, axis=0)[:5] / (tok * ndev * D))
    return (
        layer_output,
        input_grad,
        qkv_grad,
        out_weight_grad,
        gate_up_grad,
        down_grad,
        attn_gain_grad,
        mlp_gain_grad,
        rms_values,
    )


def solution(mesh):
    sizes = dict(mesh.shape)
    if sizes["blk"] == 4 and sizes["uly"] == 2:
        mesh = Mesh(mesh.devices.reshape(sizes["dp"], 2, 2, 2), ALL_AXES)
        body, blk = plane_plan, ("yy", "cc")
    else:
        body, blk = general_plan, ("blk",)
    every = ("dp", *blk, "uly")
    rows = ("dp", *blk)
    return jax.shard_map(
        body,
        mesh=mesh,
        in_specs=(
            P(every, None),
            P("dp", None),
            P(every, None),
            P(every, None),
            P(rows, None, "uly"),
            P(rows, "uly"),
            P(every),
            P(every),
            P(every, None),
        ),
        out_specs=(
            P(every, None),
            P(every, None),
            P(every, None),
            P(every, None),
            P(rows, None, "uly"),
            P(rows, "uly"),
            P(every),
            P(every),
            P(),
        ),
        check_vma=False,
    )
```

```python
import functools

import jax
import jax.numpy as jnp
from jax import lax
from jax.experimental import pallas as pl
from jax.experimental.pallas import tpu as pltpu
from jax.sharding import Mesh
from jax.sharding import PartitionSpec as P

D = 2048
H = 16
KV = 8
HD = 128


EPSILON = 1e-06
ROPE_BASE = 1000000.0
MASKED = -1e30


def rms_scale(values, gain):
    return values * lax.rsqrt(jnp.mean(values * values, axis=-1, keepdims=True) + EPSILON) * gain


def rope_angles(positions):
    freq_index = jnp.arange(HD // 2, dtype=jnp.float32)
    inverse_freq = ROPE_BASE ** (-2.0 * freq_index / HD)
    return positions.astype(jnp.float32)[:, None] * inverse_freq[None, :]


def rotate_pairs(values, angles):
    half_size = values.shape[-1] // 2
    first_half = values[..., :half_size]
    second_half = values[..., half_size:]
    cosine = jnp.cos(angles)[:, None, :]
    sine = jnp.sin(angles)[:, None, :]
    return jnp.concatenate(
        [first_half * cosine - second_half * sine, second_half * cosine + first_half * sine],
        axis=-1,
    )


def sequence_positions(row_index, span_size, order_row):
    block_index = row_index // span_size
    picks = block_index[:, None] == jnp.arange(order_row.shape[0], dtype=jnp.int32)[None, :]
    chosen = jnp.sum(jnp.where(picks, order_row[None, :], 0), axis=1)
    return chosen * span_size + row_index % span_size


def contract_rows(left_side, right_side):
    return lax.dot_general(
        left_side, right_side, (((0,), (0,)), ((), ())), preferred_element_type=jnp.float32
    )


def contract_cols(left_side, right_side):
    return lax.dot_general(
        left_side, right_side, (((1,), (1,)), ((), ())), preferred_element_type=jnp.float32
    )


def general_plan(
    layer_input,
    span_order,
    qkv_weight,
    out_weight,
    gate_up_weight,
    down_weight,
    attn_gain,
    mlp_gain,
    output_cotangent,
):
    tok_rows = layer_input.shape[0]
    uly_size = lax.axis_size("uly")
    blk_size = lax.axis_size("blk")
    group_rows = tok_rows * uly_size
    seq_rows = group_rows * blk_size
    span_size = group_rows // 2
    order_row = span_order[0]
    local_kv = KV // uly_size
    local_heads = H // uly_size
    group_size = H // KV
    ff_local = down_weight.shape[1]
    score_scale = HD ** (-0.5)
    token_start = (lax.axis_index("blk") * uly_size + lax.axis_index("uly")) * tok_rows
    token_pos = sequence_positions(
        token_start + jnp.arange(tok_rows, dtype=jnp.int32), span_size, order_row
    )
    token_angles = rope_angles(token_pos)
    query_pos = sequence_positions(
        lax.axis_index("blk") * group_rows + jnp.arange(group_rows, dtype=jnp.int32),
        span_size,
        order_row,
    )
    stream_in = layer_input.astype(jnp.float32)
    qkv_full, out_full, attn_gain_full, mlp_gain_full = (
        lax.all_gather(qkv_weight, ("dp", "blk", "uly"), axis=0, tiled=True),
        lax.all_gather(out_weight, ("dp", "blk", "uly"), axis=0, tiled=True),
        lax.all_gather(attn_gain, ("dp", "blk", "uly"), axis=0, tiled=True),
        lax.all_gather(mlp_gain, ("dp", "blk", "uly"), axis=0, tiled=True),
    )
    gate_up_cols, down_cols = (
        lax.all_gather(gate_up_weight, ("dp", "blk"), axis=0, tiled=True),
        lax.all_gather(down_weight, ("dp", "blk"), axis=0, tiled=True),
    )
    attn_gain_wide = attn_gain_full.astype(jnp.float32)
    mlp_gain_wide = mlp_gain_full.astype(jnp.float32)
    normed_attn = rms_scale(stream_in, attn_gain_wide).astype(jnp.bfloat16)
    qkv_all = jnp.dot(normed_attn, qkv_full, preferred_element_type=jnp.float32)
    query_tok = (
        rotate_pairs(qkv_all[:, : H * HD].reshape(tok_rows, H, HD), token_angles)
        .reshape(tok_rows, H * HD)
        .astype(jnp.bfloat16)
    )
    key_tok = (
        rotate_pairs(qkv_all[:, H * HD : (H + KV) * HD].reshape(tok_rows, KV, HD), token_angles)
        .reshape(tok_rows, KV * HD)
        .astype(jnp.bfloat16)
    )
    value_tok = qkv_all[:, (H + KV) * HD :].astype(jnp.bfloat16)
    query_grp, key_grp, value_grp = (
        lax.all_to_all(query_tok, "uly", split_axis=1, concat_axis=0, tiled=True),
        lax.all_to_all(key_tok, "uly", split_axis=1, concat_axis=0, tiled=True),
        lax.all_to_all(value_tok, "uly", split_axis=1, concat_axis=0, tiled=True),
    )
    query_four = query_grp.reshape(group_rows, local_kv, group_size, HD)
    key_whole, value_whole = (
        lax.all_gather(key_grp, "blk", axis=0, tiled=True),
        lax.all_gather(value_grp, "blk", axis=0, tiled=True),
    )
    block_count = seq_rows // group_rows

    def take_block(block_index):
        offset = block_index * group_rows
        key_block = lax.dynamic_slice_in_dim(key_whole, offset, group_rows, 0).reshape(
            group_rows, local_kv, HD
        )
        value_block = lax.dynamic_slice_in_dim(value_whole, offset, group_rows, 0).reshape(
            group_rows, local_kv, HD
        )
        key_pos = sequence_positions(
            offset + jnp.arange(group_rows, dtype=jnp.int32), span_size, order_row
        )
        return (offset, key_block, value_block, key_pos)

    def attend_step(block_index, running):
        top_run, total_run, acc_run = running
        offset, key_block, value_block, key_pos = take_block(block_index)
        scores = (
            jnp.einsum("rkgd,pkd->kgrp", query_four, key_block, preferred_element_type=jnp.float32)
            * score_scale
        )
        allowed = key_pos[None, :] <= query_pos[:, None]
        scores = jnp.where(allowed, scores, MASKED)
        top_new = jnp.maximum(top_run, jnp.max(scores, axis=-1))
        weights = jnp.where(allowed, jnp.exp(scores - top_new[..., None]), 0.0)
        shrink_factor = jnp.exp(top_run - top_new)
        total_new = total_run * shrink_factor + jnp.sum(weights, axis=-1)
        acc_new = acc_run * shrink_factor[..., None] + jnp.einsum(
            "kgrp,pkd->kgrd",
            weights.astype(jnp.bfloat16),
            value_block,
            preferred_element_type=jnp.float32,
        )
        return (top_new, total_new, acc_new)

    start_state = (
        jnp.full((local_kv, group_size, group_rows), MASKED, jnp.float32),
        jnp.zeros((local_kv, group_size, group_rows), jnp.float32),
        jnp.zeros((local_kv, group_size, group_rows, HD), jnp.float32),
    )
    top_end, total_end, acc_end = lax.fori_loop(0, block_count, attend_step, start_state)
    log_total = top_end + jnp.log(total_end)
    head_rows = jnp.transpose(acc_end / total_end[..., None], (2, 0, 1, 3))
    heads_group = head_rows.reshape(group_rows, local_heads * HD).astype(jnp.bfloat16)
    heads_tok = lax.all_to_all(heads_group, "uly", split_axis=0, concat_axis=1, tiled=True)
    attn_out = contract_cols(heads_tok, out_full)
    middle = stream_in + attn_out
    normed_mlp = rms_scale(middle, mlp_gain_wide).astype(jnp.bfloat16)
    normed_grp, cotangent_grp = (
        lax.all_gather(normed_mlp, "uly", axis=0, tiled=True),
        lax.all_gather(output_cotangent, "uly", axis=0, tiled=True),
    )
    gate_up = jnp.einsum(
        "rd,dcf->rcf", normed_grp, gate_up_cols, preferred_element_type=jnp.float32
    )
    gate_part = gate_up[:, 0, :]
    up_part = gate_up[:, 1, :]
    hidden = (jax.nn.silu(gate_part) * up_part).astype(jnp.bfloat16)
    mlp_part = contract_cols(hidden, down_cols)
    mlp_out = lax.psum_scatter(
        mlp_part.astype(jnp.bfloat16), "uly", scatter_dimension=0, tiled=True
    ).astype(jnp.float32)
    final_stream = middle + mlp_out
    local_squares = jnp.stack(
        [
            jnp.sum(stream_in * stream_in),
            jnp.sum(attn_out * attn_out),
            jnp.sum(middle * middle),
            jnp.sum(mlp_out * mlp_out),
            jnp.sum(final_stream * final_stream),
        ]
    )
    total_squares = lax.psum(local_squares, ("dp", "blk", "uly"))
    entry_count = tok_rows * lax.axis_size("dp") * blk_size * uly_size * D
    rms_values = jnp.sqrt(total_squares / entry_count)
    grad_hidden = jnp.dot(cotangent_grp, down_cols, preferred_element_type=jnp.float32)
    sigmoid_gate = jax.nn.sigmoid(gate_part)
    grad_gate = grad_hidden * up_part * sigmoid_gate * (1.0 + gate_part * (1.0 - sigmoid_gate))
    grad_up = grad_hidden * gate_part * sigmoid_gate
    grad_gate_up = jnp.stack([grad_gate, grad_up], axis=1).astype(jnp.bfloat16)
    grad_normed_part = jnp.einsum(
        "rcf,dcf->rd", grad_gate_up, gate_up_cols, preferred_element_type=jnp.float32
    )
    grad_normed_mlp = lax.psum_scatter(
        grad_normed_part.astype(jnp.bfloat16), "uly", scatter_dimension=0, tiled=True
    ).astype(jnp.float32)
    gate_term = jnp.einsum(
        "rd,rcf->dcf", normed_grp, grad_gate_up, preferred_element_type=jnp.float32
    ).reshape(lax.axis_size(("dp", "blk")) * gate_up_weight.shape[0], 2 * ff_local)
    mlp_grads = lax.psum_scatter(
        jnp.concatenate([gate_term, contract_rows(cotangent_grp, hidden)], axis=1).astype(
            jnp.bfloat16
        ),
        ("dp", "blk"),
        scatter_dimension=0,
        tiled=True,
    ).astype(jnp.float32)
    gate_up_grad = mlp_grads[:, : 2 * ff_local].reshape(mlp_grads.shape[0], 2, ff_local)
    down_grad = mlp_grads[:, 2 * ff_local :]
    mlp_value, mlp_pull = jax.vjp(rms_scale, middle, mlp_gain_wide)
    grad_middle_norm, mlp_gain_grad_full = mlp_pull(grad_normed_mlp)
    grad_middle = output_cotangent.astype(jnp.float32) + grad_middle_norm
    grad_attn_out = grad_middle.astype(jnp.bfloat16)
    grad_heads_tok = jnp.dot(grad_attn_out, out_full, preferred_element_type=jnp.float32).astype(
        jnp.bfloat16
    )
    out_weight_term = contract_rows(grad_attn_out, heads_tok)
    grad_heads = lax.all_to_all(grad_heads_tok, "uly", split_axis=1, concat_axis=0, tiled=True)
    grad_four = grad_heads.reshape(group_rows, local_kv, group_size, HD)
    row_delta = jnp.transpose(
        jnp.sum(grad_four.astype(jnp.float32) * head_rows, axis=-1), (1, 2, 0)
    )

    def backward_step(block_index, running):
        grad_query_run, grad_key_all, grad_value_all = running
        offset, key_block, value_block, key_pos = take_block(block_index)
        scores = (
            jnp.einsum("rkgd,pkd->kgrp", query_four, key_block, preferred_element_type=jnp.float32)
            * score_scale
        )
        allowed = key_pos[None, :] <= query_pos[:, None]
        soft_probs = jnp.where(
            allowed, jnp.exp(jnp.where(allowed, scores, MASKED) - log_total[..., None]), 0.0
        )
        grad_probs = jnp.einsum(
            "rkgd,pkd->kgrp", grad_four, value_block, preferred_element_type=jnp.float32
        )
        grad_scores = (soft_probs * (grad_probs - row_delta[..., None])).astype(jnp.bfloat16)
        grad_query_run = (
            grad_query_run
            + jnp.einsum(
                "kgrp,pkd->kgrd", grad_scores, key_block, preferred_element_type=jnp.float32
            )
            * score_scale
        )
        grad_key_block = (
            jnp.einsum(
                "kgrp,rkgd->pkd", grad_scores, query_four, preferred_element_type=jnp.float32
            )
            * score_scale
        ).reshape(group_rows, local_kv * HD)
        grad_value_block = jnp.einsum(
            "kgrp,rkgd->pkd",
            soft_probs.astype(jnp.bfloat16),
            grad_four,
            preferred_element_type=jnp.float32,
        ).reshape(group_rows, local_kv * HD)
        grad_key_all = lax.dynamic_update_slice_in_dim(grad_key_all, grad_key_block, offset, 0)
        grad_value_all = lax.dynamic_update_slice_in_dim(
            grad_value_all, grad_value_block, offset, 0
        )
        return (grad_query_run, grad_key_all, grad_value_all)

    back_state = (
        jnp.zeros((local_kv, group_size, group_rows, HD), jnp.float32),
        jnp.zeros((seq_rows, local_kv * HD), jnp.float32),
        jnp.zeros((seq_rows, local_kv * HD), jnp.float32),
    )
    grad_query_end, grad_key_whole, grad_value_whole = lax.fori_loop(
        0, block_count, backward_step, back_state
    )
    grad_key_own, grad_value_own = (
        lax.psum_scatter(
            grad_key_whole.astype(jnp.bfloat16), "blk", scatter_dimension=0, tiled=True
        ).astype(jnp.float32),
        lax.psum_scatter(
            grad_value_whole.astype(jnp.bfloat16), "blk", scatter_dimension=0, tiled=True
        ).astype(jnp.float32),
    )
    grad_query_rows = (
        jnp.transpose(grad_query_end, (2, 0, 1, 3))
        .reshape(group_rows, local_heads * HD)
        .astype(jnp.bfloat16)
    )
    grad_query_tok, grad_key_tok, grad_value_tok = (
        lax.all_to_all(grad_query_rows, "uly", split_axis=0, concat_axis=1, tiled=True),
        lax.all_to_all(
            grad_key_own.astype(jnp.bfloat16), "uly", split_axis=0, concat_axis=1, tiled=True
        ),
        lax.all_to_all(
            grad_value_own.astype(jnp.bfloat16), "uly", split_axis=0, concat_axis=1, tiled=True
        ),
    )
    back_angles = rope_angles(-token_pos)
    grad_query_plain = rotate_pairs(
        grad_query_tok.astype(jnp.float32).reshape(tok_rows, H, HD), back_angles
    ).reshape(tok_rows, H * HD)
    grad_key_plain = rotate_pairs(
        grad_key_tok.astype(jnp.float32).reshape(tok_rows, KV, HD), back_angles
    ).reshape(tok_rows, KV * HD)
    grad_qkv = jnp.concatenate(
        [grad_query_plain, grad_key_plain, grad_value_tok.astype(jnp.float32)], axis=1
    ).astype(jnp.bfloat16)
    grad_normed_attn = contract_cols(grad_qkv, qkv_full)
    qkv_term = contract_rows(normed_attn, grad_qkv)
    attn_value, attn_pull = jax.vjp(rms_scale, stream_in, attn_gain_wide)
    grad_input_norm, attn_gain_grad_full = attn_pull(grad_normed_attn)
    input_grad = grad_middle + grad_input_norm
    qkv_grad, out_weight_grad, attn_gain_grad, mlp_gain_grad = (
        lax.psum_scatter(qkv_term, ("dp", "blk", "uly"), scatter_dimension=0, tiled=True),
        lax.psum_scatter(out_weight_term, ("dp", "blk", "uly"), scatter_dimension=0, tiled=True),
        lax.psum_scatter(
            attn_gain_grad_full, ("dp", "blk", "uly"), scatter_dimension=0, tiled=True
        ),
        lax.psum_scatter(mlp_gain_grad_full, ("dp", "blk", "uly"), scatter_dimension=0, tiled=True),
    )
    return (
        final_stream.astype(jnp.bfloat16),
        input_grad,
        qkv_grad,
        out_weight_grad,
        gate_up_grad,
        down_grad,
        attn_gain_grad,
        mlp_gain_grad,
        rms_values,
    )


ALL_AXES = ("dp", "yy", "cc", "uly")
SIDE_AXES = ("yy", "uly")
PLANE_AXES = ("yy", "cc", "uly")
GROUP_AXES = ("dp", "cc")
SWAP = [(0, 1), (1, 0)]
DIAGONAL = [(0, 3), (1, 2), (2, 1), (3, 0)]
VMEM_SPEC = pl.BlockSpec(memory_space=pltpu.VMEM)
SMEM_SPEC = pl.BlockSpec(memory_space=pltpu.SMEM)
KERNEL = dict(
    compiler_params=pltpu.CompilerParams(vmem_limit_bytes=58 * 1024 * 1024),
    cost_estimate=pl.CostEstimate(flops=1000, bytes_accessed=1000, transcendentals=0),
)
ROWS = 256
BY_ROWS = (((0,), (0,)), ((), ()))
BY_COLS = (((1,), (1,)), ((), ()))
PLAIN = (((1,), (0,)), ((), ()))


def wide(values):
    return values.astype(jnp.float32)


def low(values):
    return values.astype(jnp.bfloat16)


def dot32(left, right, dims=PLAIN):
    return lax.dot_general(left, right, dims, preferred_element_type=jnp.float32)


def low_shape(rows, cols):
    return jax.ShapeDtypeStruct((rows, cols), jnp.bfloat16)


def wide_shape(rows, cols):
    return jax.ShapeDtypeStruct((rows, cols), jnp.float32)


def once(shape):
    return pl.BlockSpec(shape, lambda *i: (0,) * len(shape), pipeline_mode=pl.Buffered(1))


def row_block(step):
    return pl.ds(pl.multiple_of(step * ROWS, ROWS), ROWS)


def head_cut(head):
    return slice(head * HD, (head + 1) * HD)


def join_rows(pieces, out):
    rows = pieces[0].shape[0]
    for number, piece in enumerate(pieces):
        out[number * rows : (number + 1) * rows, :] = piece[...]


def turn(values, cosine, sine):
    return values * cosine + pltpu.roll(values, HD // 2, 1) * sine


def softmax_rows(query, key, start):
    scores = dot32(query, key, BY_COLS) * HD ** (-0.5)
    row = lax.broadcasted_iota(jnp.int32, scores.shape, 0) + start
    scores = jnp.where(lax.broadcasted_iota(jnp.int32, scores.shape, 1) <= row, scores, MASKED)
    weights = jnp.exp(scores - jnp.max(scores, axis=1, keepdims=True))
    return weights * (1.0 / jnp.sum(weights, axis=1, keepdims=True))


def rows_at(block, size):
    return pl.ds(pl.multiple_of(block * size, size), size)


def attention_forward_body(group, place, weight, cosine, sine, *refs):
    pieces, (query_out, key_out, value_out, heads_out, normed) = refs[:-5], refs[-5:]
    join_rows(pieces, normed)
    size, rows = pieces[0].shape[0], normed.shape[0]

    def project(step, carry):
        at = rows_at(step, 2 * size)
        qkv = dot32(normed[at, :], weight[...])
        turned = [
            low(turn(qkv[:, head_cut(head)], cosine[at, :], sine[at, :]))
            for head in range(group + 1)
        ]
        value = low(qkv[:, head_cut(group + 1)])
        for part in (0, 1):
            own, to = slice(part * size, (part + 1) * size), rows_at(place[2 * step + part], size)
            for head in range(group):
                query_out[to, head_cut(head)] = turned[head][own]
            key_out[to, :] = turned[group][own]
            value_out[to, :] = value[own]
        return carry

    lax.fori_loop(0, rows // (2 * size), project, 0)
    blocks = rows // size
    for start in range(0, rows, ROWS):
        at, seen = slice(start, start + ROWS), slice(0, start + ROWS)
        for head in range(group):
            probs = softmax_rows(query_out[at, head_cut(head)], key_out[seen, :], start)
            result = low(dot32(low(probs), value_out[seen, :]))
            for part in range(ROWS // size):
                to = rows_at(place[blocks + start // size + part], size)
                own = slice(part * size, (part + 1) * size)
                heads_out[to, head_cut(head)] = result[own]


def attention_forward(pieces, weight, cosine, sine, place):
    rows, group = cosine.shape[0], weight.shape[1] // HD - 2
    return pl.pallas_call(
        functools.partial(attention_forward_body, group),
        out_shape=(
            low_shape(rows, group * HD),
            low_shape(rows, HD),
            low_shape(rows, HD),
            low_shape(rows, group * HD),
        ),
        in_specs=[SMEM_SPEC] + [VMEM_SPEC] * (3 + len(pieces)),
        out_specs=(VMEM_SPEC,) * 4,
        scratch_shapes=[pltpu.VMEM((rows, weight.shape[0]), jnp.bfloat16)],
        name="attention_forward",
        **KERNEL,
    )(place, weight, cosine, sine, *pieces)


def attention_backward_body(group, place, weight, query, key, value, cosine, sine, *refs):
    pieces, (grad_qkv, grad_out, key_sum, value_sum) = refs[:-4], refs[-4:]
    size, rows = pieces[0].shape[0], query.shape[0]
    blocks = rows // size
    for number, piece in enumerate(pieces):
        grad_out[rows_at(place[number], size), :] = piece[...]
    key_sum[...] = jnp.zeros_like(key_sum)
    value_sum[...] = jnp.zeros_like(value_sum)

    def store_turned(start, values, cut, back):
        for part in range(values.shape[0] // size):
            to = rows_at(place[blocks + start // size + part], size)
            own = values[part * size : (part + 1) * size]
            if back:
                own = low(turn(wide(own), cosine[to, :], -sine[to, :]))
            grad_qkv[to, cut] = own

    for start in range(0, rows, ROWS):
        at, seen = slice(start, start + ROWS), slice(0, start + ROWS)
        grad_heads = low(dot32(grad_out[at, :], weight[...]))
        for head in range(group):
            cut = head_cut(head)
            probs = softmax_rows(query[at, cut], key[seen, :], start)
            grad_probs = dot32(grad_heads[:, cut], value[seen, :], BY_COLS)
            delta = jnp.sum(probs * grad_probs, axis=1, keepdims=True)
            grad_scores = low(probs * (grad_probs - delta))
            store_turned(start, low(dot32(grad_scores, key[seen, :]) * HD ** (-0.5)), cut, True)
            key_sum[seen, :] += dot32(grad_scores, query[at, cut], BY_ROWS)
            value_sum[seen, :] += dot32(low(probs), grad_heads[:, cut], BY_ROWS)
    for start in range(0, rows, ROWS):
        at = slice(start, start + ROWS)
        store_turned(start, low(key_sum[at, :] * HD ** (-0.5)), head_cut(group), True)
        store_turned(start, low(value_sum[at, :]), head_cut(group + 1), False)


def attention_backward(pieces, weight, query, key, value, cosine, sine, place):
    rows, group = query.shape[0], query.shape[1] // HD
    return pl.pallas_call(
        functools.partial(attention_backward_body, group),
        out_shape=low_shape(rows, (group + 2) * HD),
        in_specs=[SMEM_SPEC] + [VMEM_SPEC] * (6 + len(pieces)),
        out_specs=VMEM_SPEC,
        scratch_shapes=[pltpu.VMEM((rows, weight.shape[0]), jnp.bfloat16)]
        + [pltpu.VMEM((rows, HD), jnp.float32)] * 2,
        name="attention_backward",
        **KERNEL,
    )(place, weight, query, key, value, cosine, sine, *pieces)


def stripes(weight, parts, number):
    depth = weight.shape[0] // parts**2 // ROWS

    def place(x, step):
        at = jnp.clip(step - number, 0, parts * depth - 1)
        return ((at // depth * parts + x) * depth + at % depth, 0)

    shape = (ROWS, weight.shape[1])
    return [pl.BlockSpec(shape, functools.partial(place, x)) for x in range(parts)]


def stripe_dot(rows, refs):
    weight = [ref[...] for ref in refs]
    weight = weight[0] if len(refs) == 1 else jnp.concatenate(weight, axis=1)
    return dot32(rows[...], weight, BY_COLS)


def store_rows(outs, values):
    rows = outs[0].shape[0]
    for number, out in enumerate(outs):
        out[...] = values[number * rows : (number + 1) * rows, :]


def by_cols_body(parts, rows, *refs):
    store_rows(refs[parts:], low(stripe_dot(rows, refs[:parts])))


def by_cols_pass(rows, weight, parts, blocks, name):
    width = weight.shape[0] // parts
    block = rows.shape[0] // blocks
    return pl.pallas_call(
        functools.partial(by_cols_body, parts),
        grid=(width // ROWS,),
        out_shape=(low_shape(block, width),) * blocks,
        in_specs=[once(rows.shape), *stripes(weight, parts, 0)],
        out_specs=(pl.BlockSpec((block, ROWS), lambda step: (0, step)),) * blocks,
        name=name,
        **KERNEL,
    )(rows, *[weight] * parts)


def by_halves(weight):
    return weight.reshape(2, 2, weight.shape[0] // 4, weight.shape[1])


def columns_of(weight):
    def place(step):
        at = jnp.minimum(step, 3)
        return (0, at // 2, 0, at % 2)

    return pl.BlockSpec((2, 1, weight.shape[0] // 4, weight.shape[1] // 2), place)


def column_dot(rows, ref):
    return dot32(rows[...], ref[...].reshape(rows.shape[1], ref.shape[3]))


def hidden_body(gate_w, up_w, *refs):
    normed_p, (hidden_out, gate_slope, up_slope, normed) = refs[:-4], refs[-4:]

    @pl.when(pl.program_id(0) == 0)
    def _():
        join_rows(normed_p, normed)

    gate, up = column_dot(normed, gate_w), column_dot(normed, up_w)
    sig = jax.nn.sigmoid(gate)
    act = gate * sig
    hidden_out[...] = low(act * up)
    gate_slope[...] = low(up * (sig + act * (1.0 - sig)))
    up_slope[...] = low(act)


def hidden_pass(normed_p, gate_w, up_w):
    rows, width = len(normed_p) * normed_p[0].shape[0], normed_p[0].shape[1]
    units = 2 * gate_w.shape[1]
    return pl.pallas_call(
        hidden_body,
        grid=(4,),
        out_shape=(low_shape(rows, units),) * 3,
        in_specs=[columns_of(gate_w), columns_of(up_w)] + [once(v.shape) for v in normed_p],
        out_specs=(pl.BlockSpec((rows, units // 4), lambda step: (0, step)),) * 3,
        scratch_shapes=[pltpu.VMEM((rows, width), jnp.bfloat16)],
        name="hidden_pass",
        **KERNEL,
    )(by_halves(gate_w), by_halves(up_w), *normed_p)


def grad_hidden_body(down_w, gate_slope, up_slope, *refs):
    stripe_refs, refs = refs[:4], refs[4:]
    count = (len(refs) - 4) // 2
    cot_p, (grad_gate_out, grad_up_out, *outs) = refs[:count], refs[count:-2]
    cot, grads = refs[-2:]
    step, chunk = pl.program_id(0), grad_gate_out.shape[1]

    @pl.when(step == 0)
    def _():
        join_rows(cot_p, cot)

    for number in range(4):

        @pl.when(step == number)
        def _(number=number):
            grad_hidden = column_dot(cot, down_w)
            slopes = (gate_slope, up_slope), (grad_gate_out, grad_up_out)
            for part, (slope, out) in enumerate(zip(*slopes)):
                grad = low(grad_hidden * wide(slope[...]))
                out[...] = grad
                start = (4 * part + number) * chunk
                grads[:, start : start + chunk] = grad

    @pl.when(step >= 4)
    def _():
        weight = jnp.concatenate([ref[...] for ref in stripe_refs], axis=1)
        store_rows(outs, low(dot32(grads[...], weight, BY_COLS)))


def grad_hidden_pass(cot_p, gate_slope, up_slope, gate_w, up_w, down_w):
    rows, width = len(cot_p) * cot_p[0].shape[0], cot_p[0].shape[1]
    units = 2 * gate_w.shape[1]
    quarter = pl.BlockSpec((rows, units // 4), lambda step: (0, jnp.minimum(step, 3)))
    stripe = pl.BlockSpec((cot_p[0].shape[0], ROWS), lambda step: (0, jnp.maximum(step - 4, 0)))
    return pl.pallas_call(
        grad_hidden_body,
        grid=(4 + width // ROWS,),
        out_shape=(low_shape(rows, units),) * 2 + tuple(low_shape(*v.shape) for v in cot_p),
        in_specs=[columns_of(down_w)]
        + [quarter] * 2
        + stripes(gate_w, 2, 4)
        + stripes(up_w, 2, 4)
        + [once(v.shape) for v in cot_p],
        out_specs=(quarter,) * 2 + (stripe,) * len(cot_p),
        scratch_shapes=[pltpu.VMEM((rows, width), jnp.bfloat16)]
        + [pltpu.VMEM((rows, 2 * units), jnp.bfloat16)],
        name="grad_hidden_pass",
        **KERNEL,
    )(by_halves(down_w), gate_slope, up_slope, gate_w, gate_w, up_w, up_w, *cot_p)


def term_body(*refs):
    pieces, columns, out = refs[:-2], refs[-2], refs[-1]
    rows = jnp.concatenate([piece[...] for piece in pieces], axis=0)
    out[...] = low(dot32(rows, columns[...], BY_ROWS))


def term_halves_body(*refs):
    pieces, columns, outs = refs[:-3], refs[-3], refs[-2:]
    rows = jnp.concatenate([piece[...] for piece in pieces], axis=0)
    term = low(dot32(rows, columns[...], BY_ROWS))
    for number, out in enumerate(outs):

        @pl.when(pl.program_id(1) == number)
        def _(out=out):
            out[...] = term


def term_halves(pieces, columns):
    tokens, width = pieces[0].shape
    depth, chunk = width // 2, columns.shape[1] // 2
    return pl.pallas_call(
        term_halves_body,
        grid=(2, 2),
        out_shape=(low_shape(width, chunk),) * 2,
        in_specs=[pl.BlockSpec((tokens, depth), lambda y, x: (0, y))] * len(pieces)
        + [pl.BlockSpec((columns.shape[0], chunk), lambda y, x: (0, x))],
        out_specs=(pl.BlockSpec((depth, chunk), lambda y, x: (y, 0)),) * 2,
        name="term_halves",
        **KERNEL,
    )(*pieces, columns)


def term_pass(pieces, columns, row_parts, col_parts):
    tokens, width = pieces[0].shape
    depth, chunk = width // row_parts, columns.shape[1] // col_parts
    return pl.pallas_call(
        term_body,
        grid=(row_parts, col_parts),
        out_shape=low_shape(width * col_parts, chunk),
        in_specs=[pl.BlockSpec((tokens, depth), lambda y, x: (0, y))] * len(pieces)
        + [pl.BlockSpec((columns.shape[0], chunk), lambda y, x: (0, x))],
        out_specs=pl.BlockSpec((depth, chunk), lambda y, x: (y * col_parts + x, 0)),
        name="term_pass",
        **KERNEL,
    )(*pieces, columns)


def unit_scale(values):
    return lax.rsqrt(jnp.mean(values * values, axis=-1, keepdims=True) + EPSILON)


def norm_pull(values, grad_scaled):
    scale = unit_scale(values)
    mean = jnp.mean(grad_scaled * values, axis=-1, keepdims=True)
    return scale * grad_scaled - values * (scale * scale * scale) * mean


def pick(bit, near, far):
    return jnp.where(bit == 0, near, far)


def to_split(values):
    step = values.shape[1] // 8
    cuts = [values[:, at * step : (at + 1) * step] for at in range(8)]
    return jnp.concatenate(cuts[0::2] + cuts[1::2], axis=1)


def from_split(values):
    step = values.shape[1] // 8
    cuts = [values[:, at * step : (at + 1) * step] for at in range(8)]
    return jnp.concatenate([cut for pair in zip(cuts[:4], cuts[4:]) for cut in pair], axis=1)


def column_sums(*arrays):
    return jnp.concatenate([jnp.sum(v * v, axis=0, keepdims=True) for v in arrays], axis=0)


def summed(parts):
    total = wide(parts[0][...])
    for part in parts[1:]:
        total += wide(part[...])
    return total


def prepare_body(stream_in, cot, normed_out, cot_out):
    rows = wide(stream_in[...])
    normed_out[...] = low(rows * unit_scale(rows))
    cot_out[...] = to_split(cot[...])


def prepare_pass(stream_in, cot):
    return pl.pallas_call(
        prepare_body,
        out_shape=(low_shape(*stream_in.shape), low_shape(*cot.shape)),
        in_specs=[VMEM_SPEC] * 2,
        out_specs=(VMEM_SPEC,) * 2,
        name="prepare_pass",
        **KERNEL,
    )(stream_in, cot)


def middle_body(stream_in, *refs):
    parts, (middle_out, normed_out, squares_out) = refs[:-3], refs[-3:]
    attn_out, rows = summed(parts), wide(stream_in[...])
    middle = rows + attn_out
    middle_out[...] = middle
    normed_out[...] = to_split(low(middle * unit_scale(middle)))
    squares_out[...] = column_sums(rows, attn_out, middle)


def middle_pass(stream_in, parts):
    rows, width = stream_in.shape
    return pl.pallas_call(
        middle_body,
        out_shape=(wide_shape(rows, width), low_shape(rows, width), wide_shape(3, width)),
        in_specs=[VMEM_SPEC] * (1 + len(parts)),
        out_specs=(VMEM_SPEC,) * 3,
        name="middle_pass",
        **KERNEL,
    )(stream_in, *parts)


def final_body(middle, squares_a, *refs):
    parts, (layer_out, sums_out) = refs[:-2], refs[-2:]
    mlp_out = from_split(summed(parts))
    final = middle[...] + mlp_out
    layer_out[...] = low(final)
    squares = jnp.concatenate([squares_a[...], column_sums(mlp_out, final)], axis=0)
    sums = jnp.sum(squares, axis=1, keepdims=True)
    lane = lax.broadcasted_iota(jnp.int32, (1, sums_out.shape[1]), 1)
    total = jnp.zeros((1, sums_out.shape[1]), jnp.float32)
    for number in range(sums.shape[0]):
        total += jnp.where(lane == number, sums[number : number + 1, :], 0.0)
    sums_out[...] = jnp.broadcast_to(total, sums_out.shape)


def final_pass(middle, squares_a, parts, copies):
    rows, width = middle.shape
    return pl.pallas_call(
        final_body,
        out_shape=(low_shape(rows, width), wide_shape(copies, 128)),
        in_specs=[VMEM_SPEC] * (2 + len(parts)),
        out_specs=(VMEM_SPEC,) * 2,
        name="final_pass",
        **KERNEL,
    )(middle, squares_a, *parts)


def grad_middle_body(middle, cot, *refs):
    parts, (grad_out, low_out) = refs[:-2], refs[-2:]
    grad_normed = from_split(summed(parts))
    grad = wide(cot[...]) + norm_pull(middle[...], grad_normed)
    grad_out[...] = grad
    low_out[...] = low(grad)


def grad_middle_pass(middle, cot, parts):
    rows, width = middle.shape
    return pl.pallas_call(
        grad_middle_body,
        out_shape=(wide_shape(rows, width), low_shape(rows, width)),
        in_specs=[VMEM_SPEC] * (2 + len(parts)),
        out_specs=(VMEM_SPEC,) * 2,
        name="grad_middle_pass",
        **KERNEL,
    )(middle, cot, *parts)


def input_grad_body(stream_in, grad_middle, *refs):
    parts, out = refs[:-1], refs[-1]
    out[...] = grad_middle[...] + norm_pull(wide(stream_in[...]), summed(parts))


def input_grad_pass(stream_in, grad_middle, parts):
    return pl.pallas_call(
        input_grad_body,
        out_shape=wide_shape(*stream_in.shape),
        in_specs=[VMEM_SPEC] * (2 + len(parts)),
        out_specs=VMEM_SPEC,
        name="input_grad_pass",
        **KERNEL,
    )(stream_in, grad_middle, *parts)


def pack_body(gain, gate_up, out):
    out[...] = low(wide(gate_up[:, 0, :]) * gain[...])


def pack_more_body(gain, gate_up, down, up_out, down_out):
    up_out[...] = low(wide(gate_up[:, 1, :]) * gain[...])
    down_out[...] = down[...]


def pack_pass(body, outs, groups, gain, gate_up, *down):
    rows, chunk = gate_up.shape[0], gate_up.shape[2] // groups
    return pl.pallas_call(
        body,
        grid=(groups,),
        out_shape=(low_shape(groups * rows, chunk),) * outs,
        in_specs=[
            pl.BlockSpec((rows, 1), lambda g: (0, 0)),
            pl.BlockSpec((rows, 2, chunk), lambda g: (0, 0, g)),
        ]
        + [pl.BlockSpec((rows, chunk), lambda g: (0, g))] * len(down),
        out_specs=(pl.BlockSpec((rows, chunk), lambda g: (g, 0)),) * outs,
        name="pack_pass",
        **KERNEL,
    )(gain, gate_up, *down)


def qkv_pack_body(gain, query, key, value, out):
    start = 0
    for part in (query, key, value):
        cut = slice(start, start + part.shape[1])
        rows = low(wide(part[...]) * gain[...])
        for plane in range(out.shape[0]):
            out[plane, 0, :, cut] = rows
        start += part.shape[1]


def qkv_pack_pass(gain, weight, planes, groups):
    rows = weight.shape[0]
    query, rest = H * HD // groups, KV * HD // groups
    first = H * HD // rest
    block = (planes, 1, rows, query + 2 * rest)
    out = pl.pallas_call(
        qkv_pack_body,
        grid=(groups,),
        out_shape=jax.ShapeDtypeStruct((planes, groups, *block[2:]), jnp.bfloat16),
        in_specs=[
            pl.BlockSpec((rows, 1), lambda g: (0, 0)),
            pl.BlockSpec((rows, query), lambda g: (0, g)),
            pl.BlockSpec((rows, rest), lambda g: (0, first + g)),
            pl.BlockSpec((rows, rest), lambda g: (0, first + groups + g)),
        ],
        out_specs=pl.BlockSpec(block, lambda g: (0, g, 0, 0)),
        name="qkv_pack_pass",
        **KERNEL,
    )(gain, weight, weight, weight)
    return out.reshape(-1, block[3])


def unpack_body(gain, weight, gate, up, out, gain_sum):
    gate_term, up_term = wide(gate[...]), wide(up[...])
    out[:, 0, :] = gate_term * gain[...]
    out[:, 1, :] = up_term * gain[...]
    products = gate_term * wide(weight[:, 0, :]) + up_term * wide(weight[:, 1, :])
    total = jnp.sum(products, axis=1, keepdims=True)

    @pl.when(pl.program_id(0) == 0)
    def _():
        gain_sum[...] = total

    @pl.when(pl.program_id(0) > 0)
    def _():
        gain_sum[...] += total


def unpack_pass(gain, weight, gate, up, groups):
    rows, chunk = weight.shape[0], weight.shape[2] // groups
    column = pl.BlockSpec((rows, 1), lambda g: (0, 0))
    pair = pl.BlockSpec((rows, 2, chunk), lambda g: (0, 0, g))
    by_group = pl.BlockSpec((rows, chunk), lambda g: (g, 0))
    return pl.pallas_call(
        unpack_body,
        grid=(groups,),
        out_shape=(jax.ShapeDtypeStruct(weight.shape, jnp.float32), wide_shape(rows, 1)),
        in_specs=[column, pair, by_group, by_group],
        out_specs=(pair, column),
        name="unpack_pass",
        **KERNEL,
    )(gain, weight, gate, up)


def side_by_side_body(part, out):
    out[...] = wide(part[...])


def side_by_side(values, groups):
    rows, cols = values.shape[0] // groups, values.shape[1]
    return pl.pallas_call(
        side_by_side_body,
        grid=(groups,),
        out_shape=wide_shape(rows, groups * cols),
        in_specs=[pl.BlockSpec((rows, cols), lambda g: (g, 0))],
        out_specs=pl.BlockSpec((rows, cols), lambda g: (0, g)),
        name="side_by_side",
        **KERNEL,
    )(values)


def exchange(values, axes):
    return lax.all_to_all(values, axes, split_axis=0, concat_axis=0, tiled=True)


def after(values, *earlier):
    return lax.optimization_barrier((values, *earlier))[0]


def together(*values):
    return lax.optimization_barrier(values)


def swap(values, *axes):
    pairs = SWAP if len(axes) == 1 else DIAGONAL
    return lax.ppermute(values, axes if len(axes) > 1 else axes[0], pairs)


def plane_hop(rows):
    return (rows, swap(rows, "uly"), swap(rows, "yy"), swap(rows, "yy", "uly"))


def plane_back(parts):
    return (parts[0], swap(parts[1], "uly"), swap(parts[2], "yy"), swap(parts[3], "yy", "uly"))


def shift(values, by):
    count = lax.axis_size("dp")
    return lax.ppermute(values, "dp", [(i, (i + by) % count) for i in range(count)])


def column_hop(rows):
    return (rows, *(shift(rows, by) for by in range(1, lax.axis_size("dp"))))


def column_back(parts):
    return (parts[0], *(shift(v, -by) for by, v in enumerate(parts[1:], 1)))


def core_hop(pieces):
    return (*pieces, *(swap(v, "cc") for v in pieces))


def add_body(*refs):
    count = len(refs) // 3
    for left, right, out in zip(refs[:count], refs[count : 2 * count], refs[2 * count :]):
        out[...] = low(wide(left[...]) + wide(right[...]))


def core_back(blocks):
    half = len(blocks) // 2
    arrived = [swap(v, "cc") for v in blocks[half:]]
    return pl.pallas_call(
        add_body,
        out_shape=tuple(low_shape(*v.shape) for v in arrived),
        in_specs=[VMEM_SPEC] * (2 * half),
        out_specs=(VMEM_SPEC,) * half,
        name="add_pass",
        **KERNEL,
    )(*blocks[:half], *arrived)


def plane_plan(
    layer_input,
    span_order,
    qkv_weight,
    out_weight,
    gate_up_weight,
    down_weight,
    attn_gain,
    mlp_gain,
    output_cotangent,
):
    tok = layer_input.shape[0]
    nz = lax.axis_size("dp")
    ndev = lax.axis_size(ALL_AXES)
    plane = ndev // nz
    span_size = tok * plane // span_order.shape[1]
    y_at, c_at, x_at = lax.axis_index("yy"), lax.axis_index("cc"), lax.axis_index("uly")
    q_cols, kv_cols = H * HD // plane, KV * HD // plane
    own_cols = q_cols + 2 * kv_cols
    d_rows = qkv_weight.shape[0]
    mlp_rows, ff_local = down_weight.shape
    hgroups = lax.axis_size(GROUP_AXES)
    hchunk = ff_local // hgroups

    gain_peer = swap(mlp_gain[None, :], "uly")
    gain_own, gain_peer = wide(mlp_gain)[None, :], wide(gain_peer)
    gain_m = pick(
        x_at,
        jnp.concatenate([gain_own, gain_peer], axis=1),
        jnp.concatenate([gain_peer, gain_own], axis=1),
    ).reshape(mlp_rows, 1)
    (gate_rows,) = pack_pass(pack_body, 1, hgroups, gain_m, gate_up_weight)
    out_rows = out_weight.reshape(d_rows, plane, q_cols).transpose(1, 0, 2).reshape(-1, q_cols)
    out_here = exchange(out_rows, PLANE_AXES)
    normed, cot_split = prepare_pass(layer_input, output_cotangent)
    gate_rows, gain_m, out_here, normed, cot_split, qkv_weight, down_weight = together(
        gate_rows, gain_m, out_here, normed, cot_split, qkv_weight, down_weight
    )

    def spread(here):
        return lax.all_gather(here, SIDE_AXES, axis=0, tiled=True)

    wo = lax.all_gather(out_here, "dp", axis=0, tiled=True)
    gate_here = exchange(gate_rows, GROUP_AXES)
    normed_p = plane_hop(normed)
    gain_a = wide(attn_gain)[:, None]
    qkv_rows = qkv_pack_pass(gain_a, qkv_weight, nz, plane)
    up_rows, down_rows = pack_pass(
        pack_more_body, 2, hgroups, gain_m, gate_up_weight, down_weight
    )
    gate_here, normed_p, qkv_rows, up_rows, down_rows, cot_split = together(
        gate_here, normed_p, qkv_rows, up_rows, down_rows, cot_split
    )

    block = jnp.arange(plane, dtype=jnp.int32)
    core_of, y_of, x_of = (block // 4) ^ c_at, (block // 2) % 2 ^ y_at, block % 2 ^ x_at
    stored = (y_of * 2 + core_of) * 2 + x_of
    row_at = (stored[:, None] * tok + jnp.arange(tok, dtype=jnp.int32)[None, :]).reshape(-1)
    positions = sequence_positions(row_at, span_size, span_order[0])
    angles = rope_angles(positions)
    cosine = jnp.concatenate([jnp.cos(angles)] * 2, axis=1)
    sine = jnp.concatenate([-jnp.sin(angles), jnp.sin(angles)], axis=1)
    gate_w = spread(gate_here)
    wq = exchange(qkv_rows, ALL_AXES)
    normed_p = core_hop(normed_p)
    place = positions[::tok] // span_size
    ordered = place[None, :] == block[:, None]
    place = jnp.concatenate([place, jnp.sum(jnp.where(ordered, block[None, :], 0), axis=1)])
    rows_info = (cosine, sine, place)
    wq, normed_p, up_rows, rows_info = together(wq, normed_p, up_rows, rows_info)

    up_here = exchange(up_rows, GROUP_AXES)
    query, key, value, heads = attention_forward(normed_p, wq, *rows_info)
    attn_parts = core_back(by_cols_pass(heads, wo, 1, plane, "out_pass"))
    up_here, attn_parts, down_rows, cot_split = together(
        up_here, attn_parts, down_rows, cot_split
    )

    up_w = spread(up_here)
    down_here = exchange(down_rows, GROUP_AXES)
    attn_parts = plane_back(attn_parts)
    cot_3 = shift(cot_split, 3)
    attn_parts, down_here, cot_3, cot_split = together(attn_parts, down_here, cot_3, cot_split)

    middle, zhat, squares_a = middle_pass(layer_input, attn_parts)
    zhat, down_here = together(zhat, down_here)
    down_w = spread(down_here)
    zhat_p = core_hop(column_hop(zhat))
    zhat_p, gate_w, up_w, cot_split = together(zhat_p, gate_w, up_w, cot_split)

    cot_2 = shift(cot_split, 2)
    hidden, gate_slope, up_slope = hidden_pass(zhat_p, gate_w, up_w)
    hidden, cot_2, cot_split, gate_slope, down_w = together(
        hidden, cot_2, cot_split, gate_slope, down_w
    )

    cot_p = core_hop((cot_split, shift(cot_split, 1), cot_2, cot_3))
    mlp_parts = core_back(by_cols_pass(hidden, down_w, 2, 2 * nz, "down_pass"))
    cot_p, mlp_parts = together(cot_p, mlp_parts)
    mlp_1 = shift(mlp_parts[1], -1)
    down_t = term_pass(cot_p, hidden, 2, 2)
    mlp_1, mlp_parts, down_t = together(mlp_1, mlp_parts, down_t)

    def side_sum(term):
        return lax.psum_scatter(term, SIDE_AXES, scatter_dimension=0, tiled=True)

    down_t = side_sum(down_t)
    mlp_2 = shift(mlp_parts[2], -2)
    grad_gate, grad_up, *gz_parts = grad_hidden_pass(
        cot_p, gate_slope, up_slope, gate_w, up_w, down_w
    )
    gz_parts, grad_gate, mlp_2, mlp_parts = together(gz_parts, grad_gate, mlp_2, mlp_parts)

    gz_parts = core_back(gz_parts)
    mlp_3 = shift(mlp_parts[3], -3)
    gate_t = term_pass(zhat_p, grad_gate, 2, 2)
    gz_parts, gate_t, mlp_3, mlp_parts = together(gz_parts, gate_t, mlp_3, mlp_parts)

    gate_t = side_sum(gate_t)
    gz_parts = column_back(gz_parts)
    up_t = term_pass(zhat_p, grad_up, 2, 2)
    mlp_parts = (mlp_parts[0], mlp_1, mlp_2, mlp_3)
    layer_output, lanes = final_pass(middle, squares_a, mlp_parts, ndev)
    gathered = exchange(lanes, ALL_AXES)
    gz_parts, up_t, down_t, gathered = together(gz_parts, up_t, down_t, gathered)

    down_back = exchange(down_t, GROUP_AXES)
    grad_middle, grad_out = grad_middle_pass(middle, output_cotangent, gz_parts)
    grad_out_p = plane_hop(grad_out)
    grad_out_p, gate_t, down_back, up_t = together(grad_out_p, gate_t, down_back, up_t)
    grad_out_p, gate_t, up_t = together(core_hop(grad_out_p), gate_t, up_t)

    up_t = side_sum(up_t)
    gate_back = exchange(gate_t, GROUP_AXES)
    grad_qkv = attention_backward(grad_out_p, wo, query, key, value, *rows_info)
    gx_parts = core_back(by_cols_pass(grad_qkv, wq, 1, plane, "qkv_back_pass"))
    query_term, rest_term = term_halves(normed_p, grad_qkv)
    gx_parts, query_term, rest_term, gate_back, down_back, heads = together(
        gx_parts, query_term, rest_term, gate_back, down_back, heads
    )

    query_sum = exchange(query_term, ALL_AXES)
    out_term = term_pass(grad_out_p, heads, 2, 1)
    down_grad = side_by_side(down_back, hgroups)
    query_sum, up_t, out_term, down_grad, rest_term, gx_parts = together(
        query_sum, up_t, out_term, down_grad, rest_term, gx_parts
    )

    out_term = lax.psum_scatter(out_term, "dp", scatter_dimension=0, tiled=True)
    up_back = exchange(up_t, GROUP_AXES)
    gx_parts = plane_back(gx_parts)

    def plane_sum(arrived):
        parts = wide(arrived.reshape(nz, plane, d_rows, arrived.shape[1]))
        return jnp.sum(parts, axis=0).transpose(1, 0, 2)

    query_sum = plane_sum(query_sum).reshape(d_rows, -1)
    up_back, gx_parts, rest_term, query_sum = together(up_back, gx_parts, rest_term, query_sum)

    rest_sum = exchange(rest_term, ALL_AXES)
    input_grad = input_grad_pass(layer_input, grad_middle, gx_parts)
    gate_up_grad, gain_sum = unpack_pass(gain_m, gate_up_weight, gate_back, up_back, hgroups)
    rest_sum, input_grad, gate_up_grad, gain_sum, out_term = together(
        rest_sum, input_grad, gate_up_grad, gain_sum, out_term
    )
    out_sum = exchange(out_term, PLANE_AXES)

    rest_sum = plane_sum(rest_sum)
    qkv_sum = jnp.concatenate(
        [
            query_sum,
            rest_sum[:, :, :kv_cols].reshape(d_rows, -1),
            rest_sum[:, :, kv_cols:].reshape(d_rows, -1),
        ],
        axis=1,
    )
    qkv_grad = qkv_sum * gain_a
    attn_gain_grad = jnp.sum(qkv_sum * wide(qkv_weight), axis=1)
    gain_halves = gain_sum.reshape(2, -1)
    gain_keep = jnp.where(x_at == 0, gain_halves[0], gain_halves[1])
    gain_send = jnp.where(x_at == 0, gain_halves[1], gain_halves[0])
    mlp_gain_grad = gain_keep + swap(gain_send[None, :], "uly")[0]

    out_sum = wide(out_sum).reshape(plane, d_rows, q_cols).transpose(1, 0, 2)
    out_weight_grad = out_sum.reshape(d_rows, -1)
    rms_values = jnp.sqrt(jnp.sum(gathered, axis=0)[:5] / (tok * ndev * D))
    return (
        layer_output,
        input_grad,
        qkv_grad,
        out_weight_grad,
        gate_up_grad,
        down_grad,
        attn_gain_grad,
        mlp_gain_grad,
        rms_values,
    )


def solution(mesh):
    sizes = dict(mesh.shape)
    if sizes["blk"] == 4 and sizes["uly"] == 2:
        mesh = Mesh(mesh.devices.reshape(sizes["dp"], 2, 2, 2), ALL_AXES)
        body, blk = plane_plan, ("yy", "cc")
    else:
        body, blk = general_plan, ("blk",)
    every = ("dp", *blk, "uly")
    rows = ("dp", *blk)
    return jax.shard_map(
        body,
        mesh=mesh,
        in_specs=(
            P(every, None),
            P("dp", None),
            P(every, None),
            P(every, None),
            P(rows, None, "uly"),
            P(rows, "uly"),
            P(every),
            P(every),
            P(every, None),
        ),
        out_specs=(
            P(every, None),
            P(every, None),
            P(every, None),
            P(every, None),
            P(rows, None, "uly"),
            P(rows, "uly"),
            P(every),
            P(every),
            P(),
        ),
        check_vma=False,
    )
```

```python
import functools

import jax
import jax.numpy as jnp
from jax import lax
from jax.experimental import pallas as pl
from jax.experimental.pallas import tpu as pltpu
from jax.sharding import Mesh
from jax.sharding import PartitionSpec as P

D = 2048
H = 16
KV = 8
HD = 128


EPSILON = 1e-06
ROPE_BASE = 1000000.0
MASKED = -1e30


def rms_scale(values, gain):
    return values * lax.rsqrt(jnp.mean(values * values, axis=-1, keepdims=True) + EPSILON) * gain


def rope_angles(positions):
    freq_index = jnp.arange(HD // 2, dtype=jnp.float32)
    inverse_freq = ROPE_BASE ** (-2.0 * freq_index / HD)
    return positions.astype(jnp.float32)[:, None] * inverse_freq[None, :]


def rotate_pairs(values, angles):
    half_size = values.shape[-1] // 2
    first_half = values[..., :half_size]
    second_half = values[..., half_size:]
    cosine = jnp.cos(angles)[:, None, :]
    sine = jnp.sin(angles)[:, None, :]
    return jnp.concatenate(
        [first_half * cosine - second_half * sine, second_half * cosine + first_half * sine],
        axis=-1,
    )


def sequence_positions(row_index, span_size, order_row):
    block_index = row_index // span_size
    picks = block_index[:, None] == jnp.arange(order_row.shape[0], dtype=jnp.int32)[None, :]
    chosen = jnp.sum(jnp.where(picks, order_row[None, :], 0), axis=1)
    return chosen * span_size + row_index % span_size


def contract_rows(left_side, right_side):
    return lax.dot_general(
        left_side, right_side, (((0,), (0,)), ((), ())), preferred_element_type=jnp.float32
    )


def contract_cols(left_side, right_side):
    return lax.dot_general(
        left_side, right_side, (((1,), (1,)), ((), ())), preferred_element_type=jnp.float32
    )


def general_plan(
    layer_input,
    span_order,
    qkv_weight,
    out_weight,
    gate_up_weight,
    down_weight,
    attn_gain,
    mlp_gain,
    output_cotangent,
):
    tok_rows = layer_input.shape[0]
    uly_size = lax.axis_size("uly")
    blk_size = lax.axis_size("blk")
    group_rows = tok_rows * uly_size
    seq_rows = group_rows * blk_size
    span_size = group_rows // 2
    order_row = span_order[0]
    local_kv = KV // uly_size
    local_heads = H // uly_size
    group_size = H // KV
    ff_local = down_weight.shape[1]
    score_scale = HD ** (-0.5)
    token_start = (lax.axis_index("blk") * uly_size + lax.axis_index("uly")) * tok_rows
    token_pos = sequence_positions(
        token_start + jnp.arange(tok_rows, dtype=jnp.int32), span_size, order_row
    )
    token_angles = rope_angles(token_pos)
    query_pos = sequence_positions(
        lax.axis_index("blk") * group_rows + jnp.arange(group_rows, dtype=jnp.int32),
        span_size,
        order_row,
    )
    stream_in = layer_input.astype(jnp.float32)
    qkv_full, out_full, attn_gain_full, mlp_gain_full = (
        lax.all_gather(qkv_weight, ("dp", "blk", "uly"), axis=0, tiled=True),
        lax.all_gather(out_weight, ("dp", "blk", "uly"), axis=0, tiled=True),
        lax.all_gather(attn_gain, ("dp", "blk", "uly"), axis=0, tiled=True),
        lax.all_gather(mlp_gain, ("dp", "blk", "uly"), axis=0, tiled=True),
    )
    gate_up_cols, down_cols = (
        lax.all_gather(gate_up_weight, ("dp", "blk"), axis=0, tiled=True),
        lax.all_gather(down_weight, ("dp", "blk"), axis=0, tiled=True),
    )
    attn_gain_wide = attn_gain_full.astype(jnp.float32)
    mlp_gain_wide = mlp_gain_full.astype(jnp.float32)
    normed_attn = rms_scale(stream_in, attn_gain_wide).astype(jnp.bfloat16)
    qkv_all = jnp.dot(normed_attn, qkv_full, preferred_element_type=jnp.float32)
    query_tok = (
        rotate_pairs(qkv_all[:, : H * HD].reshape(tok_rows, H, HD), token_angles)
        .reshape(tok_rows, H * HD)
        .astype(jnp.bfloat16)
    )
    key_tok = (
        rotate_pairs(qkv_all[:, H * HD : (H + KV) * HD].reshape(tok_rows, KV, HD), token_angles)
        .reshape(tok_rows, KV * HD)
        .astype(jnp.bfloat16)
    )
    value_tok = qkv_all[:, (H + KV) * HD :].astype(jnp.bfloat16)
    query_grp, key_grp, value_grp = (
        lax.all_to_all(query_tok, "uly", split_axis=1, concat_axis=0, tiled=True),
        lax.all_to_all(key_tok, "uly", split_axis=1, concat_axis=0, tiled=True),
        lax.all_to_all(value_tok, "uly", split_axis=1, concat_axis=0, tiled=True),
    )
    query_four = query_grp.reshape(group_rows, local_kv, group_size, HD)
    key_whole, value_whole = (
        lax.all_gather(key_grp, "blk", axis=0, tiled=True),
        lax.all_gather(value_grp, "blk", axis=0, tiled=True),
    )
    block_count = seq_rows // group_rows

    def take_block(block_index):
        offset = block_index * group_rows
        key_block = lax.dynamic_slice_in_dim(key_whole, offset, group_rows, 0).reshape(
            group_rows, local_kv, HD
        )
        value_block = lax.dynamic_slice_in_dim(value_whole, offset, group_rows, 0).reshape(
            group_rows, local_kv, HD
        )
        key_pos = sequence_positions(
            offset + jnp.arange(group_rows, dtype=jnp.int32), span_size, order_row
        )
        return (offset, key_block, value_block, key_pos)

    def attend_step(block_index, running):
        top_run, total_run, acc_run = running
        offset, key_block, value_block, key_pos = take_block(block_index)
        scores = (
            jnp.einsum("rkgd,pkd->kgrp", query_four, key_block, preferred_element_type=jnp.float32)
            * score_scale
        )
        allowed = key_pos[None, :] <= query_pos[:, None]
        scores = jnp.where(allowed, scores, MASKED)
        top_new = jnp.maximum(top_run, jnp.max(scores, axis=-1))
        weights = jnp.where(allowed, jnp.exp(scores - top_new[..., None]), 0.0)
        shrink_factor = jnp.exp(top_run - top_new)
        total_new = total_run * shrink_factor + jnp.sum(weights, axis=-1)
        acc_new = acc_run * shrink_factor[..., None] + jnp.einsum(
            "kgrp,pkd->kgrd",
            weights.astype(jnp.bfloat16),
            value_block,
            preferred_element_type=jnp.float32,
        )
        return (top_new, total_new, acc_new)

    start_state = (
        jnp.full((local_kv, group_size, group_rows), MASKED, jnp.float32),
        jnp.zeros((local_kv, group_size, group_rows), jnp.float32),
        jnp.zeros((local_kv, group_size, group_rows, HD), jnp.float32),
    )
    top_end, total_end, acc_end = lax.fori_loop(0, block_count, attend_step, start_state)
    log_total = top_end + jnp.log(total_end)
    head_rows = jnp.transpose(acc_end / total_end[..., None], (2, 0, 1, 3))
    heads_group = head_rows.reshape(group_rows, local_heads * HD).astype(jnp.bfloat16)
    heads_tok = lax.all_to_all(heads_group, "uly", split_axis=0, concat_axis=1, tiled=True)
    attn_out = contract_cols(heads_tok, out_full)
    middle = stream_in + attn_out
    normed_mlp = rms_scale(middle, mlp_gain_wide).astype(jnp.bfloat16)
    normed_grp, cotangent_grp = (
        lax.all_gather(normed_mlp, "uly", axis=0, tiled=True),
        lax.all_gather(output_cotangent, "uly", axis=0, tiled=True),
    )
    gate_up = jnp.einsum(
        "rd,dcf->rcf", normed_grp, gate_up_cols, preferred_element_type=jnp.float32
    )
    gate_part = gate_up[:, 0, :]
    up_part = gate_up[:, 1, :]
    hidden = (jax.nn.silu(gate_part) * up_part).astype(jnp.bfloat16)
    mlp_part = contract_cols(hidden, down_cols)
    mlp_out = lax.psum_scatter(
        mlp_part.astype(jnp.bfloat16), "uly", scatter_dimension=0, tiled=True
    ).astype(jnp.float32)
    final_stream = middle + mlp_out
    local_squares = jnp.stack(
        [
            jnp.sum(stream_in * stream_in),
            jnp.sum(attn_out * attn_out),
            jnp.sum(middle * middle),
            jnp.sum(mlp_out * mlp_out),
            jnp.sum(final_stream * final_stream),
        ]
    )
    total_squares = lax.psum(local_squares, ("dp", "blk", "uly"))
    entry_count = tok_rows * lax.axis_size("dp") * blk_size * uly_size * D
    rms_values = jnp.sqrt(total_squares / entry_count)
    grad_hidden = jnp.dot(cotangent_grp, down_cols, preferred_element_type=jnp.float32)
    sigmoid_gate = jax.nn.sigmoid(gate_part)
    grad_gate = grad_hidden * up_part * sigmoid_gate * (1.0 + gate_part * (1.0 - sigmoid_gate))
    grad_up = grad_hidden * gate_part * sigmoid_gate
    grad_gate_up = jnp.stack([grad_gate, grad_up], axis=1).astype(jnp.bfloat16)
    grad_normed_part = jnp.einsum(
        "rcf,dcf->rd", grad_gate_up, gate_up_cols, preferred_element_type=jnp.float32
    )
    grad_normed_mlp = lax.psum_scatter(
        grad_normed_part.astype(jnp.bfloat16), "uly", scatter_dimension=0, tiled=True
    ).astype(jnp.float32)
    gate_term = jnp.einsum(
        "rd,rcf->dcf", normed_grp, grad_gate_up, preferred_element_type=jnp.float32
    ).reshape(lax.axis_size(("dp", "blk")) * gate_up_weight.shape[0], 2 * ff_local)
    mlp_grads = lax.psum_scatter(
        jnp.concatenate([gate_term, contract_rows(cotangent_grp, hidden)], axis=1).astype(
            jnp.bfloat16
        ),
        ("dp", "blk"),
        scatter_dimension=0,
        tiled=True,
    ).astype(jnp.float32)
    gate_up_grad = mlp_grads[:, : 2 * ff_local].reshape(mlp_grads.shape[0], 2, ff_local)
    down_grad = mlp_grads[:, 2 * ff_local :]
    mlp_value, mlp_pull = jax.vjp(rms_scale, middle, mlp_gain_wide)
    grad_middle_norm, mlp_gain_grad_full = mlp_pull(grad_normed_mlp)
    grad_middle = output_cotangent.astype(jnp.float32) + grad_middle_norm
    grad_attn_out = grad_middle.astype(jnp.bfloat16)
    grad_heads_tok = jnp.dot(grad_attn_out, out_full, preferred_element_type=jnp.float32).astype(
        jnp.bfloat16
    )
    out_weight_term = contract_rows(grad_attn_out, heads_tok)
    grad_heads = lax.all_to_all(grad_heads_tok, "uly", split_axis=1, concat_axis=0, tiled=True)
    grad_four = grad_heads.reshape(group_rows, local_kv, group_size, HD)
    row_delta = jnp.transpose(
        jnp.sum(grad_four.astype(jnp.float32) * head_rows, axis=-1), (1, 2, 0)
    )

    def backward_step(block_index, running):
        grad_query_run, grad_key_all, grad_value_all = running
        offset, key_block, value_block, key_pos = take_block(block_index)
        scores = (
            jnp.einsum("rkgd,pkd->kgrp", query_four, key_block, preferred_element_type=jnp.float32)
            * score_scale
        )
        allowed = key_pos[None, :] <= query_pos[:, None]
        soft_probs = jnp.where(
            allowed, jnp.exp(jnp.where(allowed, scores, MASKED) - log_total[..., None]), 0.0
        )
        grad_probs = jnp.einsum(
            "rkgd,pkd->kgrp", grad_four, value_block, preferred_element_type=jnp.float32
        )
        grad_scores = (soft_probs * (grad_probs - row_delta[..., None])).astype(jnp.bfloat16)
        grad_query_run = (
            grad_query_run
            + jnp.einsum(
                "kgrp,pkd->kgrd", grad_scores, key_block, preferred_element_type=jnp.float32
            )
            * score_scale
        )
        grad_key_block = (
            jnp.einsum(
                "kgrp,rkgd->pkd", grad_scores, query_four, preferred_element_type=jnp.float32
            )
            * score_scale
        ).reshape(group_rows, local_kv * HD)
        grad_value_block = jnp.einsum(
            "kgrp,rkgd->pkd",
            soft_probs.astype(jnp.bfloat16),
            grad_four,
            preferred_element_type=jnp.float32,
        ).reshape(group_rows, local_kv * HD)
        grad_key_all = lax.dynamic_update_slice_in_dim(grad_key_all, grad_key_block, offset, 0)
        grad_value_all = lax.dynamic_update_slice_in_dim(
            grad_value_all, grad_value_block, offset, 0
        )
        return (grad_query_run, grad_key_all, grad_value_all)

    back_state = (
        jnp.zeros((local_kv, group_size, group_rows, HD), jnp.float32),
        jnp.zeros((seq_rows, local_kv * HD), jnp.float32),
        jnp.zeros((seq_rows, local_kv * HD), jnp.float32),
    )
    grad_query_end, grad_key_whole, grad_value_whole = lax.fori_loop(
        0, block_count, backward_step, back_state
    )
    grad_key_own, grad_value_own = (
        lax.psum_scatter(
            grad_key_whole.astype(jnp.bfloat16), "blk", scatter_dimension=0, tiled=True
        ).astype(jnp.float32),
        lax.psum_scatter(
            grad_value_whole.astype(jnp.bfloat16), "blk", scatter_dimension=0, tiled=True
        ).astype(jnp.float32),
    )
    grad_query_rows = (
        jnp.transpose(grad_query_end, (2, 0, 1, 3))
        .reshape(group_rows, local_heads * HD)
        .astype(jnp.bfloat16)
    )
    grad_query_tok, grad_key_tok, grad_value_tok = (
        lax.all_to_all(grad_query_rows, "uly", split_axis=0, concat_axis=1, tiled=True),
        lax.all_to_all(
            grad_key_own.astype(jnp.bfloat16), "uly", split_axis=0, concat_axis=1, tiled=True
        ),
        lax.all_to_all(
            grad_value_own.astype(jnp.bfloat16), "uly", split_axis=0, concat_axis=1, tiled=True
        ),
    )
    back_angles = rope_angles(-token_pos)
    grad_query_plain = rotate_pairs(
        grad_query_tok.astype(jnp.float32).reshape(tok_rows, H, HD), back_angles
    ).reshape(tok_rows, H * HD)
    grad_key_plain = rotate_pairs(
        grad_key_tok.astype(jnp.float32).reshape(tok_rows, KV, HD), back_angles
    ).reshape(tok_rows, KV * HD)
    grad_qkv = jnp.concatenate(
        [grad_query_plain, grad_key_plain, grad_value_tok.astype(jnp.float32)], axis=1
    ).astype(jnp.bfloat16)
    grad_normed_attn = contract_cols(grad_qkv, qkv_full)
    qkv_term = contract_rows(normed_attn, grad_qkv)
    attn_value, attn_pull = jax.vjp(rms_scale, stream_in, attn_gain_wide)
    grad_input_norm, attn_gain_grad_full = attn_pull(grad_normed_attn)
    input_grad = grad_middle + grad_input_norm
    qkv_grad, out_weight_grad, attn_gain_grad, mlp_gain_grad = (
        lax.psum_scatter(qkv_term, ("dp", "blk", "uly"), scatter_dimension=0, tiled=True),
        lax.psum_scatter(out_weight_term, ("dp", "blk", "uly"), scatter_dimension=0, tiled=True),
        lax.psum_scatter(
            attn_gain_grad_full, ("dp", "blk", "uly"), scatter_dimension=0, tiled=True
        ),
        lax.psum_scatter(mlp_gain_grad_full, ("dp", "blk", "uly"), scatter_dimension=0, tiled=True),
    )
    return (
        final_stream.astype(jnp.bfloat16),
        input_grad,
        qkv_grad,
        out_weight_grad,
        gate_up_grad,
        down_grad,
        attn_gain_grad,
        mlp_gain_grad,
        rms_values,
    )


ALL_AXES = ("dp", "yy", "cc", "uly")
SIDE_AXES = ("yy", "uly")
PLANE_AXES = ("yy", "cc", "uly")
GROUP_AXES = ("dp", "cc")
SWAP = [(0, 1), (1, 0)]
DIAGONAL = [(0, 3), (1, 2), (2, 1), (3, 0)]
VMEM_SPEC = pl.BlockSpec(memory_space=pltpu.VMEM)
SMEM_SPEC = pl.BlockSpec(memory_space=pltpu.SMEM)
KERNEL = dict(
    compiler_params=pltpu.CompilerParams(vmem_limit_bytes=58 * 1024 * 1024),
    cost_estimate=pl.CostEstimate(flops=1000, bytes_accessed=1000, transcendentals=0),
)
ROWS = 256
STRIPE = 1024
BY_ROWS = (((0,), (0,)), ((), ()))
BY_COLS = (((1,), (1,)), ((), ()))
PLAIN = (((1,), (0,)), ((), ()))


def wide(values):
    return values.astype(jnp.float32)


def low(values):
    return values.astype(jnp.bfloat16)


def dot32(left, right, dims=PLAIN):
    return lax.dot_general(left, right, dims, preferred_element_type=jnp.float32)


def low_shape(rows, cols):
    return jax.ShapeDtypeStruct((rows, cols), jnp.bfloat16)


def wide_shape(rows, cols):
    return jax.ShapeDtypeStruct((rows, cols), jnp.float32)


def once(shape):
    return pl.BlockSpec(shape, lambda *i: (0,) * len(shape), pipeline_mode=pl.Buffered(1))


def row_block(step):
    return pl.ds(pl.multiple_of(step * ROWS, ROWS), ROWS)


def head_cut(head):
    return slice(head * HD, (head + 1) * HD)


def join_rows(pieces, out):
    rows = pieces[0].shape[0]
    for number, piece in enumerate(pieces):
        out[number * rows : (number + 1) * rows, :] = piece[...]


def turn(values, cosine, sine):
    return values * cosine + pltpu.roll(values, HD // 2, 1) * sine


def softmax_rows(query, key, start):
    scores = dot32(query, key, BY_COLS) * HD ** (-0.5)
    row = lax.broadcasted_iota(jnp.int32, scores.shape, 0) + start
    scores = jnp.where(lax.broadcasted_iota(jnp.int32, scores.shape, 1) <= row, scores, MASKED)
    weights = jnp.exp(scores - jnp.max(scores, axis=1, keepdims=True))
    return weights * (1.0 / jnp.sum(weights, axis=1, keepdims=True))


def rows_at(block, size):
    return pl.ds(pl.multiple_of(block * size, size), size)


def attention_forward_body(group, place, weight, cosine, sine, *refs):
    pieces, (query_out, key_out, value_out, heads_out, normed) = refs[:-5], refs[-5:]
    join_rows(pieces, normed)
    size, rows = pieces[0].shape[0], normed.shape[0]

    def project(step, carry):
        at = rows_at(step, 2 * size)
        qkv = dot32(normed[at, :], weight[...])
        turned = [
            low(turn(qkv[:, head_cut(head)], cosine[at, :], sine[at, :]))
            for head in range(group + 1)
        ]
        value = low(qkv[:, head_cut(group + 1)])
        for part in (0, 1):
            own, to = slice(part * size, (part + 1) * size), rows_at(place[2 * step + part], size)
            for head in range(group):
                query_out[to, head_cut(head)] = turned[head][own]
            key_out[to, :] = turned[group][own]
            value_out[to, :] = value[own]
        return carry

    lax.fori_loop(0, rows // (2 * size), project, 0)
    blocks = rows // size
    for start in range(0, rows, ROWS):
        at, seen = slice(start, start + ROWS), slice(0, start + ROWS)
        for head in range(group):
            probs = softmax_rows(query_out[at, head_cut(head)], key_out[seen, :], start)
            result = low(dot32(low(probs), value_out[seen, :]))
            for part in range(ROWS // size):
                to = rows_at(place[blocks + start // size + part], size)
                own = slice(part * size, (part + 1) * size)
                heads_out[to, head_cut(head)] = result[own]


def attention_forward(pieces, weight, cosine, sine, place):
    rows, group = cosine.shape[0], weight.shape[1] // HD - 2
    return pl.pallas_call(
        functools.partial(attention_forward_body, group),
        out_shape=(
            low_shape(rows, group * HD),
            low_shape(rows, HD),
            low_shape(rows, HD),
            low_shape(rows, group * HD),
        ),
        in_specs=[SMEM_SPEC] + [VMEM_SPEC] * (3 + len(pieces)),
        out_specs=(VMEM_SPEC,) * 4,
        scratch_shapes=[pltpu.VMEM((rows, weight.shape[0]), jnp.bfloat16)],
        name="attention_forward",
        **KERNEL,
    )(place, weight, cosine, sine, *pieces)


def attention_backward_body(group, place, weight, query, key, value, cosine, sine, *refs):
    pieces, (grad_qkv, grad_out, key_sum, value_sum) = refs[:-4], refs[-4:]
    size, rows = pieces[0].shape[0], query.shape[0]
    blocks = rows // size
    for number, piece in enumerate(pieces):
        grad_out[rows_at(place[number], size), :] = piece[...]
    key_sum[...] = jnp.zeros_like(key_sum)
    value_sum[...] = jnp.zeros_like(value_sum)

    def store_turned(start, values, cut, back):
        for part in range(values.shape[0] // size):
            to = rows_at(place[blocks + start // size + part], size)
            own = values[part * size : (part + 1) * size]
            if back:
                own = low(turn(wide(own), cosine[to, :], -sine[to, :]))
            grad_qkv[to, cut] = own

    for start in range(0, rows, ROWS):
        at, seen = slice(start, start + ROWS), slice(0, start + ROWS)
        grad_heads = low(dot32(grad_out[at, :], weight[...]))
        for head in range(group):
            cut = head_cut(head)
            probs = softmax_rows(query[at, cut], key[seen, :], start)
            grad_probs = dot32(grad_heads[:, cut], value[seen, :], BY_COLS)
            delta = jnp.sum(probs * grad_probs, axis=1, keepdims=True)
            grad_scores = low(probs * (grad_probs - delta))
            store_turned(start, low(dot32(grad_scores, key[seen, :]) * HD ** (-0.5)), cut, True)
            key_sum[seen, :] += dot32(grad_scores, query[at, cut], BY_ROWS)
            value_sum[seen, :] += dot32(low(probs), grad_heads[:, cut], BY_ROWS)
    for start in range(0, rows, ROWS):
        at = slice(start, start + ROWS)
        store_turned(start, low(key_sum[at, :] * HD ** (-0.5)), head_cut(group), True)
        store_turned(start, low(value_sum[at, :]), head_cut(group + 1), False)


def attention_backward(pieces, weight, query, key, value, cosine, sine, place):
    rows, group = query.shape[0], query.shape[1] // HD
    return pl.pallas_call(
        functools.partial(attention_backward_body, group),
        out_shape=low_shape(rows, (group + 2) * HD),
        in_specs=[SMEM_SPEC] + [VMEM_SPEC] * (6 + len(pieces)),
        out_specs=VMEM_SPEC,
        scratch_shapes=[pltpu.VMEM((rows, weight.shape[0]), jnp.bfloat16)]
        + [pltpu.VMEM((rows, HD), jnp.float32)] * 2,
        name="attention_backward",
        **KERNEL,
    )(place, weight, query, key, value, cosine, sine, *pieces)


def stripes(weight, parts, number):
    depth = weight.shape[0] // parts**2 // STRIPE

    def place(x, step):
        at = jnp.clip(step - number, 0, parts * depth - 1)
        return ((at // depth * parts + x) * depth + at % depth, 0)

    shape = (STRIPE, weight.shape[1])
    return [pl.BlockSpec(shape, functools.partial(place, x)) for x in range(parts)]


def stripe_dot(rows, refs):
    weight = [ref[...] for ref in refs]
    weight = weight[0] if len(refs) == 1 else jnp.concatenate(weight, axis=1)
    return dot32(rows[...], weight, BY_COLS)


def store_rows(outs, values):
    rows = outs[0].shape[0]
    for number, out in enumerate(outs):
        out[...] = values[number * rows : (number + 1) * rows, :]


def by_cols_body(parts, rows, *refs):
    store_rows(refs[parts:], low(stripe_dot(rows, refs[:parts])))


def by_cols_pass(rows, weight, parts, blocks, name):
    width = weight.shape[0] // parts
    block = rows.shape[0] // blocks
    return pl.pallas_call(
        functools.partial(by_cols_body, parts),
        grid=(width // STRIPE,),
        out_shape=(low_shape(block, width),) * blocks,
        in_specs=[once(rows.shape), *stripes(weight, parts, 0)],
        out_specs=(pl.BlockSpec((block, STRIPE), lambda step: (0, step)),) * blocks,
        name=name,
        **KERNEL,
    )(rows, *[weight] * parts)


def by_halves(weight):
    return weight.reshape(2, 2, weight.shape[0] // 4, weight.shape[1])


def columns_of(weight):
    def place(step):
        at = jnp.minimum(step, 3)
        return (0, at // 2, 0, at % 2)

    return pl.BlockSpec((2, 1, weight.shape[0] // 4, weight.shape[1] // 2), place)


def column_dot(rows, ref):
    return dot32(rows[...], ref[...].reshape(rows.shape[1], ref.shape[3]))


def hidden_body(gate_w, up_w, *refs):
    normed_p, (hidden_out, gate_slope, up_slope, normed) = refs[:-4], refs[-4:]

    @pl.when(pl.program_id(0) == 0)
    def _():
        join_rows(normed_p, normed)

    gate, up = column_dot(normed, gate_w), column_dot(normed, up_w)
    sig = jax.nn.sigmoid(gate)
    act = gate * sig
    hidden_out[...] = low(act * up)
    gate_slope[...] = low(up * (sig + act * (1.0 - sig)))
    up_slope[...] = low(act)


def hidden_pass(normed_p, gate_w, up_w):
    rows, width = len(normed_p) * normed_p[0].shape[0], normed_p[0].shape[1]
    units = 2 * gate_w.shape[1]
    return pl.pallas_call(
        hidden_body,
        grid=(4,),
        out_shape=(low_shape(rows, units),) * 3,
        in_specs=[columns_of(gate_w), columns_of(up_w)] + [once(v.shape) for v in normed_p],
        out_specs=(pl.BlockSpec((rows, units // 4), lambda step: (0, step)),) * 3,
        scratch_shapes=[pltpu.VMEM((rows, width), jnp.bfloat16)],
        name="hidden_pass",
        **KERNEL,
    )(by_halves(gate_w), by_halves(up_w), *normed_p)


def grad_hidden_body(down_w, gate_slope, up_slope, *refs):
    stripe_refs, refs = refs[:4], refs[4:]
    count = (len(refs) - 4) // 2
    cot_p, (grad_gate_out, grad_up_out, *outs) = refs[:count], refs[count:-2]
    cot, grads = refs[-2:]
    step, chunk = pl.program_id(0), grad_gate_out.shape[1]

    @pl.when(step == 0)
    def _():
        join_rows(cot_p, cot)

    for number in range(4):

        @pl.when(step == number)
        def _(number=number):
            grad_hidden = column_dot(cot, down_w)
            slopes = (gate_slope, up_slope), (grad_gate_out, grad_up_out)
            for part, (slope, out) in enumerate(zip(*slopes)):
                grad = low(grad_hidden * wide(slope[...]))
                out[...] = grad
                start = (4 * part + number) * chunk
                grads[:, start : start + chunk] = grad

    @pl.when(step >= 4)
    def _():
        weight = jnp.concatenate([ref[...] for ref in stripe_refs], axis=1)
        store_rows(outs, low(dot32(grads[...], weight, BY_COLS)))


def grad_hidden_pass(cot_p, gate_slope, up_slope, gate_w, up_w, down_w):
    rows, width = len(cot_p) * cot_p[0].shape[0], cot_p[0].shape[1]
    units = 2 * gate_w.shape[1]
    quarter = pl.BlockSpec((rows, units // 4), lambda step: (0, jnp.minimum(step, 3)))
    stripe = pl.BlockSpec((cot_p[0].shape[0], STRIPE), lambda step: (0, jnp.maximum(step - 4, 0)))
    return pl.pallas_call(
        grad_hidden_body,
        grid=(4 + width // STRIPE,),
        out_shape=(low_shape(rows, units),) * 2 + tuple(low_shape(*v.shape) for v in cot_p),
        in_specs=[columns_of(down_w)]
        + [quarter] * 2
        + stripes(gate_w, 2, 4)
        + stripes(up_w, 2, 4)
        + [once(v.shape) for v in cot_p],
        out_specs=(quarter,) * 2 + (stripe,) * len(cot_p),
        scratch_shapes=[pltpu.VMEM((rows, width), jnp.bfloat16)]
        + [pltpu.VMEM((rows, 2 * units), jnp.bfloat16)],
        name="grad_hidden_pass",
        **KERNEL,
    )(by_halves(down_w), gate_slope, up_slope, gate_w, gate_w, up_w, up_w, *cot_p)


def term_body(*refs):
    pieces, columns, out = refs[:-2], refs[-2], refs[-1]
    rows = jnp.concatenate([piece[...] for piece in pieces], axis=0)
    out[...] = low(dot32(rows, columns[...], BY_ROWS))


def term_halves_body(*refs):
    pieces, columns, outs = refs[:-3], refs[-3], refs[-2:]
    rows = jnp.concatenate([piece[...] for piece in pieces], axis=0)
    term = low(dot32(rows, columns[...], BY_ROWS))
    for number, out in enumerate(outs):

        @pl.when(pl.program_id(1) == number)
        def _(out=out):
            out[...] = term


def term_halves(pieces, columns):
    tokens, width = pieces[0].shape
    depth, chunk = width // 2, columns.shape[1] // 2
    return pl.pallas_call(
        term_halves_body,
        grid=(2, 2),
        out_shape=(low_shape(width, chunk),) * 2,
        in_specs=[pl.BlockSpec((tokens, depth), lambda y, x: (0, y))] * len(pieces)
        + [pl.BlockSpec((columns.shape[0], chunk), lambda y, x: (0, x))],
        out_specs=(pl.BlockSpec((depth, chunk), lambda y, x: (y, 0)),) * 2,
        name="term_halves",
        **KERNEL,
    )(*pieces, columns)


def term_pass(pieces, columns, row_parts, col_parts):
    tokens, width = pieces[0].shape
    depth, chunk = width // row_parts, columns.shape[1] // col_parts
    return pl.pallas_call(
        term_body,
        grid=(row_parts, col_parts),
        out_shape=low_shape(width * col_parts, chunk),
        in_specs=[pl.BlockSpec((tokens, depth), lambda y, x: (0, y))] * len(pieces)
        + [pl.BlockSpec((columns.shape[0], chunk), lambda y, x: (0, x))],
        out_specs=pl.BlockSpec((depth, chunk), lambda y, x: (y * col_parts + x, 0)),
        name="term_pass",
        **KERNEL,
    )(*pieces, columns)


def unit_scale(values):
    return lax.rsqrt(jnp.mean(values * values, axis=-1, keepdims=True) + EPSILON)


def norm_pull(values, grad_scaled):
    scale = unit_scale(values)
    mean = jnp.mean(grad_scaled * values, axis=-1, keepdims=True)
    return scale * grad_scaled - values * (scale * scale * scale) * mean


def pick(bit, near, far):
    return jnp.where(bit == 0, near, far)


def to_split(values):
    step = values.shape[1] // 8
    cuts = [values[:, at * step : (at + 1) * step] for at in range(8)]
    return jnp.concatenate(cuts[0::2] + cuts[1::2], axis=1)


def from_split(values):
    step = values.shape[1] // 8
    cuts = [values[:, at * step : (at + 1) * step] for at in range(8)]
    return jnp.concatenate([cut for pair in zip(cuts[:4], cuts[4:]) for cut in pair], axis=1)


def column_sums(*arrays):
    return jnp.concatenate([jnp.sum(v * v, axis=0, keepdims=True) for v in arrays], axis=0)


def summed(parts):
    total = wide(parts[0][...])
    for part in parts[1:]:
        total += wide(part[...])
    return total


def prepare_body(stream_in, cot, normed_out, cot_out):
    rows = wide(stream_in[...])
    normed_out[...] = low(rows * unit_scale(rows))
    cot_out[...] = to_split(cot[...])


def prepare_pass(stream_in, cot):
    return pl.pallas_call(
        prepare_body,
        out_shape=(low_shape(*stream_in.shape), low_shape(*cot.shape)),
        in_specs=[VMEM_SPEC] * 2,
        out_specs=(VMEM_SPEC,) * 2,
        name="prepare_pass",
        **KERNEL,
    )(stream_in, cot)


def middle_body(stream_in, *refs):
    parts, (middle_out, normed_out, squares_out) = refs[:-3], refs[-3:]
    attn_out, rows = summed(parts), wide(stream_in[...])
    middle = rows + attn_out
    middle_out[...] = middle
    normed_out[...] = to_split(low(middle * unit_scale(middle)))
    squares_out[...] = column_sums(rows, attn_out, middle)


def middle_pass(stream_in, parts):
    rows, width = stream_in.shape
    return pl.pallas_call(
        middle_body,
        out_shape=(wide_shape(rows, width), low_shape(rows, width), wide_shape(3, width)),
        in_specs=[VMEM_SPEC] * (1 + len(parts)),
        out_specs=(VMEM_SPEC,) * 3,
        name="middle_pass",
        **KERNEL,
    )(stream_in, *parts)


def final_body(middle, squares_a, *refs):
    parts, (layer_out, sums_out) = refs[:-2], refs[-2:]
    mlp_out = from_split(summed(parts))
    final = middle[...] + mlp_out
    layer_out[...] = low(final)
    squares = jnp.concatenate([squares_a[...], column_sums(mlp_out, final)], axis=0)
    sums = jnp.sum(squares, axis=1, keepdims=True)
    lane = lax.broadcasted_iota(jnp.int32, (1, sums_out.shape[1]), 1)
    total = jnp.zeros((1, sums_out.shape[1]), jnp.float32)
    for number in range(sums.shape[0]):
        total += jnp.where(lane == number, sums[number : number + 1, :], 0.0)
    sums_out[...] = jnp.broadcast_to(total, sums_out.shape)


def final_pass(middle, squares_a, parts, copies):
    rows, width = middle.shape
    return pl.pallas_call(
        final_body,
        out_shape=(low_shape(rows, width), wide_shape(copies, 128)),
        in_specs=[VMEM_SPEC] * (2 + len(parts)),
        out_specs=(VMEM_SPEC,) * 2,
        name="final_pass",
        **KERNEL,
    )(middle, squares_a, *parts)


def grad_middle_body(middle, cot, *refs):
    parts, (grad_out, low_out) = refs[:-2], refs[-2:]
    grad_normed = from_split(summed(parts))
    grad = wide(cot[...]) + norm_pull(middle[...], grad_normed)
    grad_out[...] = grad
    low_out[...] = low(grad)


def grad_middle_pass(middle, cot, parts):
    rows, width = middle.shape
    return pl.pallas_call(
        grad_middle_body,
        out_shape=(wide_shape(rows, width), low_shape(rows, width)),
        in_specs=[VMEM_SPEC] * (2 + len(parts)),
        out_specs=(VMEM_SPEC,) * 2,
        name="grad_middle_pass",
        **KERNEL,
    )(middle, cot, *parts)


def input_grad_body(stream_in, grad_middle, *refs):
    parts, out = refs[:-1], refs[-1]
    out[...] = grad_middle[...] + norm_pull(wide(stream_in[...]), summed(parts))


def input_grad_pass(stream_in, grad_middle, parts):
    return pl.pallas_call(
        input_grad_body,
        out_shape=wide_shape(*stream_in.shape),
        in_specs=[VMEM_SPEC] * (2 + len(parts)),
        out_specs=VMEM_SPEC,
        name="input_grad_pass",
        **KERNEL,
    )(stream_in, grad_middle, *parts)


def stack_groups(out, values):
    rows, chunk = values.shape[0], out.shape[1]
    for number in range(out.shape[0] // rows):
        out[number * rows : (number + 1) * rows, :] = values[:, number * chunk : (number + 1) * chunk]


def pack_body(gain, gate_up, out):
    stack_groups(out, low(wide(gate_up[:, 0, :]) * gain[...]))


def pack_more_body(gain, gate_up, down, up_out, down_out):
    stack_groups(up_out, low(wide(gate_up[:, 1, :]) * gain[...]))
    stack_groups(down_out, down[...])


def pack_pass(body, outs, groups, gain, gate_up, *down):
    rows, chunk = gate_up.shape[0], gate_up.shape[2] // groups
    steps = 2
    per_step = groups // steps
    return pl.pallas_call(
        body,
        grid=(steps,),
        out_shape=(low_shape(groups * rows, chunk),) * outs,
        in_specs=[
            pl.BlockSpec((rows, 1), lambda g: (0, 0)),
            pl.BlockSpec((rows, 2, per_step * chunk), lambda g: (0, 0, g)),
        ]
        + [pl.BlockSpec((rows, per_step * chunk), lambda g: (0, g))] * len(down),
        out_specs=(pl.BlockSpec((per_step * rows, chunk), lambda g: (g, 0)),) * outs,
        name="pack_pass",
        **KERNEL,
    )(gain, gate_up, *down)


def qkv_pack_body(gain, query, key, value, out):
    start = 0
    for part in (query, key, value):
        cut = slice(start, start + part.shape[1])
        rows = low(wide(part[...]) * gain[...])
        for plane in range(out.shape[0]):
            out[plane, 0, :, cut] = rows
        start += part.shape[1]


def qkv_pack_pass(gain, weight, planes, groups):
    rows = weight.shape[0]
    query, rest = H * HD // groups, KV * HD // groups
    first = H * HD // rest
    block = (planes, 1, rows, query + 2 * rest)
    out = pl.pallas_call(
        qkv_pack_body,
        grid=(groups,),
        out_shape=jax.ShapeDtypeStruct((planes, groups, *block[2:]), jnp.bfloat16),
        in_specs=[
            pl.BlockSpec((rows, 1), lambda g: (0, 0)),
            pl.BlockSpec((rows, query), lambda g: (0, g)),
            pl.BlockSpec((rows, rest), lambda g: (0, first + g)),
            pl.BlockSpec((rows, rest), lambda g: (0, first + groups + g)),
        ],
        out_specs=pl.BlockSpec(block, lambda g: (0, g, 0, 0)),
        name="qkv_pack_pass",
        **KERNEL,
    )(gain, weight, weight, weight)
    return out.reshape(-1, block[3])


def unpack_body(gain, weight, gate, up, out, gain_sum):
    gate_term, up_term = wide(gate[...]), wide(up[...])
    out[:, 0, :] = gate_term * gain[...]
    out[:, 1, :] = up_term * gain[...]
    products = gate_term * wide(weight[:, 0, :]) + up_term * wide(weight[:, 1, :])
    total = jnp.sum(products, axis=1, keepdims=True)

    @pl.when(pl.program_id(0) == 0)
    def _():
        gain_sum[...] = total

    @pl.when(pl.program_id(0) > 0)
    def _():
        gain_sum[...] += total


def unpack_pass(gain, weight, gate, up, groups):
    rows, chunk = weight.shape[0], weight.shape[2] // groups
    column = pl.BlockSpec((rows, 1), lambda g: (0, 0))
    pair = pl.BlockSpec((rows, 2, chunk), lambda g: (0, 0, g))
    by_group = pl.BlockSpec((rows, chunk), lambda g: (g, 0))
    return pl.pallas_call(
        unpack_body,
        grid=(groups,),
        out_shape=(jax.ShapeDtypeStruct(weight.shape, jnp.float32), wide_shape(rows, 1)),
        in_specs=[column, pair, by_group, by_group],
        out_specs=(pair, column),
        name="unpack_pass",
        **KERNEL,
    )(gain, weight, gate, up)


def side_by_side_body(part, out):
    out[...] = wide(part[...])


def side_by_side(values, groups):
    rows, cols = values.shape[0] // groups, values.shape[1]
    return pl.pallas_call(
        side_by_side_body,
        grid=(groups,),
        out_shape=wide_shape(rows, groups * cols),
        in_specs=[pl.BlockSpec((rows, cols), lambda g: (g, 0))],
        out_specs=pl.BlockSpec((rows, cols), lambda g: (0, g)),
        name="side_by_side",
        **KERNEL,
    )(values)


def exchange(values, axes):
    return lax.all_to_all(values, axes, split_axis=0, concat_axis=0, tiled=True)


def after(values, *earlier):
    return lax.optimization_barrier((values, *earlier))[0]


def together(*values):
    return lax.optimization_barrier(values)


def swap(values, *axes):
    pairs = SWAP if len(axes) == 1 else DIAGONAL
    return lax.ppermute(values, axes if len(axes) > 1 else axes[0], pairs)


def plane_hop(rows):
    return (rows, swap(rows, "uly"), swap(rows, "yy"), swap(rows, "yy", "uly"))


def plane_back(parts):
    return (parts[0], swap(parts[1], "uly"), swap(parts[2], "yy"), swap(parts[3], "yy", "uly"))


def shift(values, by):
    count = lax.axis_size("dp")
    return lax.ppermute(values, "dp", [(i, (i + by) % count) for i in range(count)])


def column_hop(rows):
    return (rows, *(shift(rows, by) for by in range(1, lax.axis_size("dp"))))


def column_back(parts):
    return (parts[0], *(shift(v, -by) for by, v in enumerate(parts[1:], 1)))


def core_hop(pieces):
    return (*pieces, *(swap(v, "cc") for v in pieces))


def add_body(*refs):
    count = len(refs) // 3
    for left, right, out in zip(refs[:count], refs[count : 2 * count], refs[2 * count :]):
        out[...] = low(wide(left[...]) + wide(right[...]))


def core_back(blocks):
    half = len(blocks) // 2
    arrived = [swap(v, "cc") for v in blocks[half:]]
    return pl.pallas_call(
        add_body,
        out_shape=tuple(low_shape(*v.shape) for v in arrived),
        in_specs=[VMEM_SPEC] * (2 * half),
        out_specs=(VMEM_SPEC,) * half,
        name="add_pass",
        **KERNEL,
    )(*blocks[:half], *arrived)


def plane_plan(
    layer_input,
    span_order,
    qkv_weight,
    out_weight,
    gate_up_weight,
    down_weight,
    attn_gain,
    mlp_gain,
    output_cotangent,
):
    tok = layer_input.shape[0]
    nz = lax.axis_size("dp")
    ndev = lax.axis_size(ALL_AXES)
    plane = ndev // nz
    span_size = tok * plane // span_order.shape[1]
    y_at, c_at, x_at = lax.axis_index("yy"), lax.axis_index("cc"), lax.axis_index("uly")
    q_cols, kv_cols = H * HD // plane, KV * HD // plane
    own_cols = q_cols + 2 * kv_cols
    d_rows = qkv_weight.shape[0]
    mlp_rows, ff_local = down_weight.shape
    hgroups = lax.axis_size(GROUP_AXES)
    hchunk = ff_local // hgroups

    gain_peer = swap(mlp_gain[None, :], "uly")
    gain_own, gain_peer = wide(mlp_gain)[None, :], wide(gain_peer)
    gain_m = pick(
        x_at,
        jnp.concatenate([gain_own, gain_peer], axis=1),
        jnp.concatenate([gain_peer, gain_own], axis=1),
    ).reshape(mlp_rows, 1)
    (gate_rows,) = pack_pass(pack_body, 1, hgroups, gain_m, gate_up_weight)
    out_rows = out_weight.reshape(d_rows, plane, q_cols).transpose(1, 0, 2).reshape(-1, q_cols)
    out_here = exchange(out_rows, PLANE_AXES)
    normed, cot_split = prepare_pass(layer_input, output_cotangent)
    gate_rows, gain_m, out_here, normed, cot_split, qkv_weight, down_weight = together(
        gate_rows, gain_m, out_here, normed, cot_split, qkv_weight, down_weight
    )

    def spread(here):
        return lax.all_gather(here, SIDE_AXES, axis=0, tiled=True)

    wo = lax.all_gather(out_here, "dp", axis=0, tiled=True)
    gate_here = exchange(gate_rows, GROUP_AXES)
    normed_p = plane_hop(normed)
    gain_a = wide(attn_gain)[:, None]
    qkv_rows = qkv_pack_pass(gain_a, qkv_weight, nz, plane)
    up_rows, down_rows = pack_pass(
        pack_more_body, 2, hgroups, gain_m, gate_up_weight, down_weight
    )
    gate_here, normed_p, qkv_rows, up_rows, down_rows, cot_split = together(
        gate_here, normed_p, qkv_rows, up_rows, down_rows, cot_split
    )

    block = jnp.arange(plane, dtype=jnp.int32)
    core_of, y_of, x_of = (block // 4) ^ c_at, (block // 2) % 2 ^ y_at, block % 2 ^ x_at
    stored = (y_of * 2 + core_of) * 2 + x_of
    row_at = (stored[:, None] * tok + jnp.arange(tok, dtype=jnp.int32)[None, :]).reshape(-1)
    positions = sequence_positions(row_at, span_size, span_order[0])
    angles = rope_angles(positions)
    cosine = jnp.concatenate([jnp.cos(angles)] * 2, axis=1)
    sine = jnp.concatenate([-jnp.sin(angles), jnp.sin(angles)], axis=1)
    gate_w = spread(gate_here)
    wq = exchange(qkv_rows, ALL_AXES)
    normed_p = core_hop(normed_p)
    place = positions[::tok] // span_size
    ordered = place[None, :] == block[:, None]
    place = jnp.concatenate([place, jnp.sum(jnp.where(ordered, block[None, :], 0), axis=1)])
    rows_info = (cosine, sine, place)
    wq, normed_p, up_rows, rows_info = together(wq, normed_p, up_rows, rows_info)

    up_here = exchange(up_rows, GROUP_AXES)
    query, key, value, heads = attention_forward(normed_p, wq, *rows_info)
    attn_parts = core_back(by_cols_pass(heads, wo, 1, plane, "out_pass"))
    up_here, attn_parts, down_rows, cot_split = together(
        up_here, attn_parts, down_rows, cot_split
    )

    up_w = spread(up_here)
    down_here = exchange(down_rows, GROUP_AXES)
    attn_parts = plane_back(attn_parts)
    cot_3 = shift(cot_split, 3)
    attn_parts, down_here, cot_3, cot_split = together(attn_parts, down_here, cot_3, cot_split)

    middle, zhat, squares_a = middle_pass(layer_input, attn_parts)
    zhat, down_here = together(zhat, down_here)
    down_w = spread(down_here)
    zhat_p = core_hop(column_hop(zhat))
    zhat_p, gate_w, up_w, cot_split = together(zhat_p, gate_w, up_w, cot_split)

    cot_2 = shift(cot_split, 2)
    hidden, gate_slope, up_slope = hidden_pass(zhat_p, gate_w, up_w)
    hidden, cot_2, cot_split, gate_slope, down_w = together(
        hidden, cot_2, cot_split, gate_slope, down_w
    )

    cot_p = core_hop((cot_split, shift(cot_split, 1), cot_2, cot_3))
    mlp_parts = core_back(by_cols_pass(hidden, down_w, 2, 2 * nz, "down_pass"))
    cot_p, mlp_parts = together(cot_p, mlp_parts)
    mlp_1 = shift(mlp_parts[1], -1)
    down_t = term_pass(cot_p, hidden, 2, 2)
    mlp_1, mlp_parts, down_t = together(mlp_1, mlp_parts, down_t)

    def side_sum(term):
        return lax.psum_scatter(term, SIDE_AXES, scatter_dimension=0, tiled=True)

    down_t = side_sum(down_t)
    mlp_2 = shift(mlp_parts[2], -2)
    grad_gate, grad_up, *gz_parts = grad_hidden_pass(
        cot_p, gate_slope, up_slope, gate_w, up_w, down_w
    )
    gz_parts, grad_gate, mlp_2, mlp_parts = together(gz_parts, grad_gate, mlp_2, mlp_parts)

    gz_parts = core_back(gz_parts)
    mlp_3 = shift(mlp_parts[3], -3)
    gate_t = term_pass(zhat_p, grad_gate, 2, 2)
    gz_parts, gate_t, mlp_3, mlp_parts = together(gz_parts, gate_t, mlp_3, mlp_parts)

    gate_t = side_sum(gate_t)
    gz_parts = column_back(gz_parts)
    up_t = term_pass(zhat_p, grad_up, 2, 2)
    mlp_parts = (mlp_parts[0], mlp_1, mlp_2, mlp_3)
    layer_output, lanes = final_pass(middle, squares_a, mlp_parts, ndev)
    gathered = exchange(lanes, ALL_AXES)
    gz_parts, up_t, down_t, gathered = together(gz_parts, up_t, down_t, gathered)

    down_back = exchange(down_t, GROUP_AXES)
    grad_middle, grad_out = grad_middle_pass(middle, output_cotangent, gz_parts)
    grad_out_p = plane_hop(grad_out)
    grad_out_p, gate_t, down_back, up_t = together(grad_out_p, gate_t, down_back, up_t)
    grad_out_p, gate_t, up_t = together(core_hop(grad_out_p), gate_t, up_t)

    up_t = side_sum(up_t)
    gate_back = exchange(gate_t, GROUP_AXES)
    grad_qkv = attention_backward(grad_out_p, wo, query, key, value, *rows_info)
    gx_parts = core_back(by_cols_pass(grad_qkv, wq, 1, plane, "qkv_back_pass"))
    query_term, rest_term = term_halves(normed_p, grad_qkv)
    gx_parts, query_term, rest_term, gate_back, down_back, heads = together(
        gx_parts, query_term, rest_term, gate_back, down_back, heads
    )

    query_sum = exchange(query_term, ALL_AXES)
    out_term = term_pass(grad_out_p, heads, 2, 1)
    down_grad = side_by_side(down_back, hgroups)
    query_sum, up_t, out_term, down_grad, rest_term, gx_parts = together(
        query_sum, up_t, out_term, down_grad, rest_term, gx_parts
    )

    out_term = lax.psum_scatter(out_term, "dp", scatter_dimension=0, tiled=True)
    up_back = exchange(up_t, GROUP_AXES)
    gx_parts = plane_back(gx_parts)

    def plane_sum(arrived):
        parts = wide(arrived.reshape(nz, plane, d_rows, arrived.shape[1]))
        return jnp.sum(parts, axis=0).transpose(1, 0, 2)

    query_sum = plane_sum(query_sum).reshape(d_rows, -1)
    up_back, gx_parts, rest_term, query_sum = together(up_back, gx_parts, rest_term, query_sum)

    rest_sum = exchange(rest_term, ALL_AXES)
    input_grad = input_grad_pass(layer_input, grad_middle, gx_parts)
    gate_up_grad, gain_sum = unpack_pass(gain_m, gate_up_weight, gate_back, up_back, hgroups)
    rest_sum, input_grad, gate_up_grad, gain_sum, out_term = together(
        rest_sum, input_grad, gate_up_grad, gain_sum, out_term
    )
    out_sum = exchange(out_term, PLANE_AXES)

    rest_sum = plane_sum(rest_sum)
    qkv_sum = jnp.concatenate(
        [
            query_sum,
            rest_sum[:, :, :kv_cols].reshape(d_rows, -1),
            rest_sum[:, :, kv_cols:].reshape(d_rows, -1),
        ],
        axis=1,
    )
    qkv_grad = qkv_sum * gain_a
    attn_gain_grad = jnp.sum(qkv_sum * wide(qkv_weight), axis=1)
    gain_halves = gain_sum.reshape(2, -1)
    gain_keep = jnp.where(x_at == 0, gain_halves[0], gain_halves[1])
    gain_send = jnp.where(x_at == 0, gain_halves[1], gain_halves[0])
    mlp_gain_grad = gain_keep + swap(gain_send[None, :], "uly")[0]

    out_sum = wide(out_sum).reshape(plane, d_rows, q_cols).transpose(1, 0, 2)
    out_weight_grad = out_sum.reshape(d_rows, -1)
    rms_values = jnp.sqrt(jnp.sum(gathered, axis=0)[:5] / (tok * ndev * D))
    return (
        layer_output,
        input_grad,
        qkv_grad,
        out_weight_grad,
        gate_up_grad,
        down_grad,
        attn_gain_grad,
        mlp_gain_grad,
        rms_values,
    )


def solution(mesh):
    sizes = dict(mesh.shape)
    if sizes["blk"] == 4 and sizes["uly"] == 2:
        mesh = Mesh(mesh.devices.reshape(sizes["dp"], 2, 2, 2), ALL_AXES)
        body, blk = plane_plan, ("yy", "cc")
    else:
        body, blk = general_plan, ("blk",)
    every = ("dp", *blk, "uly")
    rows = ("dp", *blk)
    return jax.shard_map(
        body,
        mesh=mesh,
        in_specs=(
            P(every, None),
            P("dp", None),
            P(every, None),
            P(every, None),
            P(rows, None, "uly"),
            P(rows, "uly"),
            P(every),
            P(every),
            P(every, None),
        ),
        out_specs=(
            P(every, None),
            P(every, None),
            P(every, None),
            P(every, None),
            P(rows, None, "uly"),
            P(rows, "uly"),
            P(every),
            P(every),
            P(),
        ),
        check_vma=False,
    )
```

```python
import functools

import jax
import jax.numpy as jnp
from jax import lax
from jax.experimental import pallas as pl
from jax.experimental.pallas import tpu as pltpu
from jax.sharding import Mesh
from jax.sharding import PartitionSpec as P

D = 2048
H = 16
KV = 8
HD = 128


EPSILON = 1e-06
ROPE_BASE = 1000000.0
MASKED = -1e30


def rms_scale(values, gain):
    return values * lax.rsqrt(jnp.mean(values * values, axis=-1, keepdims=True) + EPSILON) * gain


def rope_angles(positions):
    freq_index = jnp.arange(HD // 2, dtype=jnp.float32)
    inverse_freq = ROPE_BASE ** (-2.0 * freq_index / HD)
    return positions.astype(jnp.float32)[:, None] * inverse_freq[None, :]


def rotate_pairs(values, angles):
    half_size = values.shape[-1] // 2
    first_half = values[..., :half_size]
    second_half = values[..., half_size:]
    cosine = jnp.cos(angles)[:, None, :]
    sine = jnp.sin(angles)[:, None, :]
    return jnp.concatenate(
        [first_half * cosine - second_half * sine, second_half * cosine + first_half * sine],
        axis=-1,
    )


def sequence_positions(row_index, span_size, order_row):
    block_index = row_index // span_size
    picks = block_index[:, None] == jnp.arange(order_row.shape[0], dtype=jnp.int32)[None, :]
    chosen = jnp.sum(jnp.where(picks, order_row[None, :], 0), axis=1)
    return chosen * span_size + row_index % span_size


def contract_rows(left_side, right_side):
    return lax.dot_general(
        left_side, right_side, (((0,), (0,)), ((), ())), preferred_element_type=jnp.float32
    )


def contract_cols(left_side, right_side):
    return lax.dot_general(
        left_side, right_side, (((1,), (1,)), ((), ())), preferred_element_type=jnp.float32
    )


def general_plan(
    layer_input,
    span_order,
    qkv_weight,
    out_weight,
    gate_up_weight,
    down_weight,
    attn_gain,
    mlp_gain,
    output_cotangent,
):
    tok_rows = layer_input.shape[0]
    uly_size = lax.axis_size("uly")
    blk_size = lax.axis_size("blk")
    group_rows = tok_rows * uly_size
    seq_rows = group_rows * blk_size
    span_size = group_rows // 2
    order_row = span_order[0]
    local_kv = KV // uly_size
    local_heads = H // uly_size
    group_size = H // KV
    ff_local = down_weight.shape[1]
    score_scale = HD ** (-0.5)
    token_start = (lax.axis_index("blk") * uly_size + lax.axis_index("uly")) * tok_rows
    token_pos = sequence_positions(
        token_start + jnp.arange(tok_rows, dtype=jnp.int32), span_size, order_row
    )
    token_angles = rope_angles(token_pos)
    query_pos = sequence_positions(
        lax.axis_index("blk") * group_rows + jnp.arange(group_rows, dtype=jnp.int32),
        span_size,
        order_row,
    )
    stream_in = layer_input.astype(jnp.float32)
    qkv_full, out_full, attn_gain_full, mlp_gain_full = (
        lax.all_gather(qkv_weight, ("dp", "blk", "uly"), axis=0, tiled=True),
        lax.all_gather(out_weight, ("dp", "blk", "uly"), axis=0, tiled=True),
        lax.all_gather(attn_gain, ("dp", "blk", "uly"), axis=0, tiled=True),
        lax.all_gather(mlp_gain, ("dp", "blk", "uly"), axis=0, tiled=True),
    )
    gate_up_cols, down_cols = (
        lax.all_gather(gate_up_weight, ("dp", "blk"), axis=0, tiled=True),
        lax.all_gather(down_weight, ("dp", "blk"), axis=0, tiled=True),
    )
    attn_gain_wide = attn_gain_full.astype(jnp.float32)
    mlp_gain_wide = mlp_gain_full.astype(jnp.float32)
    normed_attn = rms_scale(stream_in, attn_gain_wide).astype(jnp.bfloat16)
    qkv_all = jnp.dot(normed_attn, qkv_full, preferred_element_type=jnp.float32)
    query_tok = (
        rotate_pairs(qkv_all[:, : H * HD].reshape(tok_rows, H, HD), token_angles)
        .reshape(tok_rows, H * HD)
        .astype(jnp.bfloat16)
    )
    key_tok = (
        rotate_pairs(qkv_all[:, H * HD : (H + KV) * HD].reshape(tok_rows, KV, HD), token_angles)
        .reshape(tok_rows, KV * HD)
        .astype(jnp.bfloat16)
    )
    value_tok = qkv_all[:, (H + KV) * HD :].astype(jnp.bfloat16)
    query_grp, key_grp, value_grp = (
        lax.all_to_all(query_tok, "uly", split_axis=1, concat_axis=0, tiled=True),
        lax.all_to_all(key_tok, "uly", split_axis=1, concat_axis=0, tiled=True),
        lax.all_to_all(value_tok, "uly", split_axis=1, concat_axis=0, tiled=True),
    )
    query_four = query_grp.reshape(group_rows, local_kv, group_size, HD)
    key_whole, value_whole = (
        lax.all_gather(key_grp, "blk", axis=0, tiled=True),
        lax.all_gather(value_grp, "blk", axis=0, tiled=True),
    )
    block_count = seq_rows // group_rows

    def take_block(block_index):
        offset = block_index * group_rows
        key_block = lax.dynamic_slice_in_dim(key_whole, offset, group_rows, 0).reshape(
            group_rows, local_kv, HD
        )
        value_block = lax.dynamic_slice_in_dim(value_whole, offset, group_rows, 0).reshape(
            group_rows, local_kv, HD
        )
        key_pos = sequence_positions(
            offset + jnp.arange(group_rows, dtype=jnp.int32), span_size, order_row
        )
        return (offset, key_block, value_block, key_pos)

    def attend_step(block_index, running):
        top_run, total_run, acc_run = running
        offset, key_block, value_block, key_pos = take_block(block_index)
        scores = (
            jnp.einsum("rkgd,pkd->kgrp", query_four, key_block, preferred_element_type=jnp.float32)
            * score_scale
        )
        allowed = key_pos[None, :] <= query_pos[:, None]
        scores = jnp.where(allowed, scores, MASKED)
        top_new = jnp.maximum(top_run, jnp.max(scores, axis=-1))
        weights = jnp.where(allowed, jnp.exp(scores - top_new[..., None]), 0.0)
        shrink_factor = jnp.exp(top_run - top_new)
        total_new = total_run * shrink_factor + jnp.sum(weights, axis=-1)
        acc_new = acc_run * shrink_factor[..., None] + jnp.einsum(
            "kgrp,pkd->kgrd",
            weights.astype(jnp.bfloat16),
            value_block,
            preferred_element_type=jnp.float32,
        )
        return (top_new, total_new, acc_new)

    start_state = (
        jnp.full((local_kv, group_size, group_rows), MASKED, jnp.float32),
        jnp.zeros((local_kv, group_size, group_rows), jnp.float32),
        jnp.zeros((local_kv, group_size, group_rows, HD), jnp.float32),
    )
    top_end, total_end, acc_end = lax.fori_loop(0, block_count, attend_step, start_state)
    log_total = top_end + jnp.log(total_end)
    head_rows = jnp.transpose(acc_end / total_end[..., None], (2, 0, 1, 3))
    heads_group = head_rows.reshape(group_rows, local_heads * HD).astype(jnp.bfloat16)
    heads_tok = lax.all_to_all(heads_group, "uly", split_axis=0, concat_axis=1, tiled=True)
    attn_out = contract_cols(heads_tok, out_full)
    middle = stream_in + attn_out
    normed_mlp = rms_scale(middle, mlp_gain_wide).astype(jnp.bfloat16)
    normed_grp, cotangent_grp = (
        lax.all_gather(normed_mlp, "uly", axis=0, tiled=True),
        lax.all_gather(output_cotangent, "uly", axis=0, tiled=True),
    )
    gate_up = jnp.einsum(
        "rd,dcf->rcf", normed_grp, gate_up_cols, preferred_element_type=jnp.float32
    )
    gate_part = gate_up[:, 0, :]
    up_part = gate_up[:, 1, :]
    hidden = (jax.nn.silu(gate_part) * up_part).astype(jnp.bfloat16)
    mlp_part = contract_cols(hidden, down_cols)
    mlp_out = lax.psum_scatter(
        mlp_part.astype(jnp.bfloat16), "uly", scatter_dimension=0, tiled=True
    ).astype(jnp.float32)
    final_stream = middle + mlp_out
    local_squares = jnp.stack(
        [
            jnp.sum(stream_in * stream_in),
            jnp.sum(attn_out * attn_out),
            jnp.sum(middle * middle),
            jnp.sum(mlp_out * mlp_out),
            jnp.sum(final_stream * final_stream),
        ]
    )
    total_squares = lax.psum(local_squares, ("dp", "blk", "uly"))
    entry_count = tok_rows * lax.axis_size("dp") * blk_size * uly_size * D
    rms_values = jnp.sqrt(total_squares / entry_count)
    grad_hidden = jnp.dot(cotangent_grp, down_cols, preferred_element_type=jnp.float32)
    sigmoid_gate = jax.nn.sigmoid(gate_part)
    grad_gate = grad_hidden * up_part * sigmoid_gate * (1.0 + gate_part * (1.0 - sigmoid_gate))
    grad_up = grad_hidden * gate_part * sigmoid_gate
    grad_gate_up = jnp.stack([grad_gate, grad_up], axis=1).astype(jnp.bfloat16)
    grad_normed_part = jnp.einsum(
        "rcf,dcf->rd", grad_gate_up, gate_up_cols, preferred_element_type=jnp.float32
    )
    grad_normed_mlp = lax.psum_scatter(
        grad_normed_part.astype(jnp.bfloat16), "uly", scatter_dimension=0, tiled=True
    ).astype(jnp.float32)
    gate_term = jnp.einsum(
        "rd,rcf->dcf", normed_grp, grad_gate_up, preferred_element_type=jnp.float32
    ).reshape(lax.axis_size(("dp", "blk")) * gate_up_weight.shape[0], 2 * ff_local)
    mlp_grads = lax.psum_scatter(
        jnp.concatenate([gate_term, contract_rows(cotangent_grp, hidden)], axis=1).astype(
            jnp.bfloat16
        ),
        ("dp", "blk"),
        scatter_dimension=0,
        tiled=True,
    ).astype(jnp.float32)
    gate_up_grad = mlp_grads[:, : 2 * ff_local].reshape(mlp_grads.shape[0], 2, ff_local)
    down_grad = mlp_grads[:, 2 * ff_local :]
    mlp_value, mlp_pull = jax.vjp(rms_scale, middle, mlp_gain_wide)
    grad_middle_norm, mlp_gain_grad_full = mlp_pull(grad_normed_mlp)
    grad_middle = output_cotangent.astype(jnp.float32) + grad_middle_norm
    grad_attn_out = grad_middle.astype(jnp.bfloat16)
    grad_heads_tok = jnp.dot(grad_attn_out, out_full, preferred_element_type=jnp.float32).astype(
        jnp.bfloat16
    )
    out_weight_term = contract_rows(grad_attn_out, heads_tok)
    grad_heads = lax.all_to_all(grad_heads_tok, "uly", split_axis=1, concat_axis=0, tiled=True)
    grad_four = grad_heads.reshape(group_rows, local_kv, group_size, HD)
    row_delta = jnp.transpose(
        jnp.sum(grad_four.astype(jnp.float32) * head_rows, axis=-1), (1, 2, 0)
    )

    def backward_step(block_index, running):
        grad_query_run, grad_key_all, grad_value_all = running
        offset, key_block, value_block, key_pos = take_block(block_index)
        scores = (
            jnp.einsum("rkgd,pkd->kgrp", query_four, key_block, preferred_element_type=jnp.float32)
            * score_scale
        )
        allowed = key_pos[None, :] <= query_pos[:, None]
        soft_probs = jnp.where(
            allowed, jnp.exp(jnp.where(allowed, scores, MASKED) - log_total[..., None]), 0.0
        )
        grad_probs = jnp.einsum(
            "rkgd,pkd->kgrp", grad_four, value_block, preferred_element_type=jnp.float32
        )
        grad_scores = (soft_probs * (grad_probs - row_delta[..., None])).astype(jnp.bfloat16)
        grad_query_run = (
            grad_query_run
            + jnp.einsum(
                "kgrp,pkd->kgrd", grad_scores, key_block, preferred_element_type=jnp.float32
            )
            * score_scale
        )
        grad_key_block = (
            jnp.einsum(
                "kgrp,rkgd->pkd", grad_scores, query_four, preferred_element_type=jnp.float32
            )
            * score_scale
        ).reshape(group_rows, local_kv * HD)
        grad_value_block = jnp.einsum(
            "kgrp,rkgd->pkd",
            soft_probs.astype(jnp.bfloat16),
            grad_four,
            preferred_element_type=jnp.float32,
        ).reshape(group_rows, local_kv * HD)
        grad_key_all = lax.dynamic_update_slice_in_dim(grad_key_all, grad_key_block, offset, 0)
        grad_value_all = lax.dynamic_update_slice_in_dim(
            grad_value_all, grad_value_block, offset, 0
        )
        return (grad_query_run, grad_key_all, grad_value_all)

    back_state = (
        jnp.zeros((local_kv, group_size, group_rows, HD), jnp.float32),
        jnp.zeros((seq_rows, local_kv * HD), jnp.float32),
        jnp.zeros((seq_rows, local_kv * HD), jnp.float32),
    )
    grad_query_end, grad_key_whole, grad_value_whole = lax.fori_loop(
        0, block_count, backward_step, back_state
    )
    grad_key_own, grad_value_own = (
        lax.psum_scatter(
            grad_key_whole.astype(jnp.bfloat16), "blk", scatter_dimension=0, tiled=True
        ).astype(jnp.float32),
        lax.psum_scatter(
            grad_value_whole.astype(jnp.bfloat16), "blk", scatter_dimension=0, tiled=True
        ).astype(jnp.float32),
    )
    grad_query_rows = (
        jnp.transpose(grad_query_end, (2, 0, 1, 3))
        .reshape(group_rows, local_heads * HD)
        .astype(jnp.bfloat16)
    )
    grad_query_tok, grad_key_tok, grad_value_tok = (
        lax.all_to_all(grad_query_rows, "uly", split_axis=0, concat_axis=1, tiled=True),
        lax.all_to_all(
            grad_key_own.astype(jnp.bfloat16), "uly", split_axis=0, concat_axis=1, tiled=True
        ),
        lax.all_to_all(
            grad_value_own.astype(jnp.bfloat16), "uly", split_axis=0, concat_axis=1, tiled=True
        ),
    )
    back_angles = rope_angles(-token_pos)
    grad_query_plain = rotate_pairs(
        grad_query_tok.astype(jnp.float32).reshape(tok_rows, H, HD), back_angles
    ).reshape(tok_rows, H * HD)
    grad_key_plain = rotate_pairs(
        grad_key_tok.astype(jnp.float32).reshape(tok_rows, KV, HD), back_angles
    ).reshape(tok_rows, KV * HD)
    grad_qkv = jnp.concatenate(
        [grad_query_plain, grad_key_plain, grad_value_tok.astype(jnp.float32)], axis=1
    ).astype(jnp.bfloat16)
    grad_normed_attn = contract_cols(grad_qkv, qkv_full)
    qkv_term = contract_rows(normed_attn, grad_qkv)
    attn_value, attn_pull = jax.vjp(rms_scale, stream_in, attn_gain_wide)
    grad_input_norm, attn_gain_grad_full = attn_pull(grad_normed_attn)
    input_grad = grad_middle + grad_input_norm
    qkv_grad, out_weight_grad, attn_gain_grad, mlp_gain_grad = (
        lax.psum_scatter(qkv_term, ("dp", "blk", "uly"), scatter_dimension=0, tiled=True),
        lax.psum_scatter(out_weight_term, ("dp", "blk", "uly"), scatter_dimension=0, tiled=True),
        lax.psum_scatter(
            attn_gain_grad_full, ("dp", "blk", "uly"), scatter_dimension=0, tiled=True
        ),
        lax.psum_scatter(mlp_gain_grad_full, ("dp", "blk", "uly"), scatter_dimension=0, tiled=True),
    )
    return (
        final_stream.astype(jnp.bfloat16),
        input_grad,
        qkv_grad,
        out_weight_grad,
        gate_up_grad,
        down_grad,
        attn_gain_grad,
        mlp_gain_grad,
        rms_values,
    )


ALL_AXES = ("dp", "yy", "cc", "uly")
SIDE_AXES = ("yy", "uly")
PLANE_AXES = ("yy", "cc", "uly")
GROUP_AXES = ("dp", "cc")
SWAP = [(0, 1), (1, 0)]
DIAGONAL = [(0, 3), (1, 2), (2, 1), (3, 0)]
VMEM_SPEC = pl.BlockSpec(memory_space=pltpu.VMEM)
SMEM_SPEC = pl.BlockSpec(memory_space=pltpu.SMEM)
KERNEL = dict(
    compiler_params=pltpu.CompilerParams(vmem_limit_bytes=58 * 1024 * 1024),
    cost_estimate=pl.CostEstimate(flops=1000, bytes_accessed=1000, transcendentals=0),
)
ROWS = 256
STRIPE = 1024
BY_ROWS = (((0,), (0,)), ((), ()))
BY_COLS = (((1,), (1,)), ((), ()))
PLAIN = (((1,), (0,)), ((), ()))


def wide(values):
    return values.astype(jnp.float32)


def low(values):
    return values.astype(jnp.bfloat16)


def dot32(left, right, dims=PLAIN):
    return lax.dot_general(left, right, dims, preferred_element_type=jnp.float32)


def low_shape(rows, cols):
    return jax.ShapeDtypeStruct((rows, cols), jnp.bfloat16)


def wide_shape(rows, cols):
    return jax.ShapeDtypeStruct((rows, cols), jnp.float32)


def once(shape):
    return pl.BlockSpec(shape, lambda *i: (0,) * len(shape), pipeline_mode=pl.Buffered(1))


def row_block(step):
    return pl.ds(pl.multiple_of(step * ROWS, ROWS), ROWS)


def head_cut(head):
    return slice(head * HD, (head + 1) * HD)


def join_rows(pieces, out):
    rows = pieces[0].shape[0]
    for number, piece in enumerate(pieces):
        out[number * rows : (number + 1) * rows, :] = piece[...]


def turn(values, cosine, sine):
    return values * cosine + pltpu.roll(values, HD // 2, 1) * sine


def softmax_rows(query, key, start):
    scores = dot32(query, key, BY_COLS) * HD ** (-0.5)
    row = lax.broadcasted_iota(jnp.int32, scores.shape, 0) + start
    scores = jnp.where(lax.broadcasted_iota(jnp.int32, scores.shape, 1) <= row, scores, MASKED)
    weights = jnp.exp(scores - jnp.max(scores, axis=1, keepdims=True))
    return weights * (1.0 / jnp.sum(weights, axis=1, keepdims=True))


def rows_at(block, size):
    return pl.ds(pl.multiple_of(block * size, size), size)


def attention_forward_body(group, place, weight, cosine, sine, *refs):
    pieces, (query_out, key_out, value_out, heads_out, normed) = refs[:-5], refs[-5:]
    join_rows(pieces, normed)
    size, rows = pieces[0].shape[0], normed.shape[0]

    def project(step, carry):
        at = rows_at(step, 2 * size)
        qkv = dot32(normed[at, :], weight[...])
        turned = [
            low(turn(qkv[:, head_cut(head)], cosine[at, :], sine[at, :]))
            for head in range(group + 1)
        ]
        value = low(qkv[:, head_cut(group + 1)])
        for part in (0, 1):
            own, to = slice(part * size, (part + 1) * size), rows_at(place[2 * step + part], size)
            for head in range(group):
                query_out[to, head_cut(head)] = turned[head][own]
            key_out[to, :] = turned[group][own]
            value_out[to, :] = value[own]
        return carry

    lax.fori_loop(0, rows // (2 * size), project, 0)
    blocks = rows // size
    for start in range(0, rows, ROWS):
        at, seen = slice(start, start + ROWS), slice(0, start + ROWS)
        for head in range(group):
            probs = softmax_rows(query_out[at, head_cut(head)], key_out[seen, :], start)
            result = low(dot32(low(probs), value_out[seen, :]))
            for part in range(ROWS // size):
                to = rows_at(place[blocks + start // size + part], size)
                own = slice(part * size, (part + 1) * size)
                heads_out[to, head_cut(head)] = result[own]


def attention_forward(pieces, weight, cosine, sine, place):
    rows, group = cosine.shape[0], weight.shape[1] // HD - 2
    return pl.pallas_call(
        functools.partial(attention_forward_body, group),
        out_shape=(
            low_shape(rows, group * HD),
            low_shape(rows, HD),
            low_shape(rows, HD),
            low_shape(rows, group * HD),
        ),
        in_specs=[SMEM_SPEC] + [VMEM_SPEC] * (3 + len(pieces)),
        out_specs=(VMEM_SPEC,) * 4,
        scratch_shapes=[pltpu.VMEM((rows, weight.shape[0]), jnp.bfloat16)],
        name="attention_forward",
        **KERNEL,
    )(place, weight, cosine, sine, *pieces)


def attention_backward_body(group, place, weight, query, key, value, cosine, sine, *refs):
    pieces, (grad_qkv, grad_out, key_sum, value_sum) = refs[:-4], refs[-4:]
    size, rows = pieces[0].shape[0], query.shape[0]
    blocks = rows // size
    for number, piece in enumerate(pieces):
        grad_out[rows_at(place[number], size), :] = piece[...]
    key_sum[...] = jnp.zeros_like(key_sum)
    value_sum[...] = jnp.zeros_like(value_sum)

    def store_turned(start, values, cut, back):
        for part in range(values.shape[0] // size):
            to = rows_at(place[blocks + start // size + part], size)
            own = values[part * size : (part + 1) * size]
            if back:
                own = low(turn(wide(own), cosine[to, :], -sine[to, :]))
            grad_qkv[to, cut] = own

    for start in range(0, rows, ROWS):
        at, seen = slice(start, start + ROWS), slice(0, start + ROWS)
        grad_heads = low(dot32(grad_out[at, :], weight[...]))
        for head in range(group):
            cut = head_cut(head)
            probs = softmax_rows(query[at, cut], key[seen, :], start)
            grad_probs = dot32(grad_heads[:, cut], value[seen, :], BY_COLS)
            delta = jnp.sum(probs * grad_probs, axis=1, keepdims=True)
            grad_scores = low(probs * (grad_probs - delta))
            store_turned(start, low(dot32(grad_scores, key[seen, :]) * HD ** (-0.5)), cut, True)
            key_sum[seen, :] += dot32(grad_scores, query[at, cut], BY_ROWS)
            value_sum[seen, :] += dot32(low(probs), grad_heads[:, cut], BY_ROWS)
    for start in range(0, rows, ROWS):
        at = slice(start, start + ROWS)
        store_turned(start, low(key_sum[at, :] * HD ** (-0.5)), head_cut(group), True)
        store_turned(start, low(value_sum[at, :]), head_cut(group + 1), False)


def attention_backward(pieces, weight, query, key, value, cosine, sine, place):
    rows, group = query.shape[0], query.shape[1] // HD
    return pl.pallas_call(
        functools.partial(attention_backward_body, group),
        out_shape=low_shape(rows, (group + 2) * HD),
        in_specs=[SMEM_SPEC] + [VMEM_SPEC] * (6 + len(pieces)),
        out_specs=VMEM_SPEC,
        scratch_shapes=[pltpu.VMEM((rows, weight.shape[0]), jnp.bfloat16)]
        + [pltpu.VMEM((rows, HD), jnp.float32)] * 2,
        name="attention_backward",
        **KERNEL,
    )(place, weight, query, key, value, cosine, sine, *pieces)


def stripes(weight, parts, number):
    depth = weight.shape[0] // parts**2 // STRIPE

    def place(x, step):
        at = jnp.clip(step - number, 0, parts * depth - 1)
        return ((at // depth * parts + x) * depth + at % depth, 0)

    shape = (STRIPE, weight.shape[1])
    return [pl.BlockSpec(shape, functools.partial(place, x)) for x in range(parts)]


def stripe_dot(rows, refs):
    weight = [ref[...] for ref in refs]
    weight = weight[0] if len(refs) == 1 else jnp.concatenate(weight, axis=1)
    return dot32(rows[...], weight, BY_COLS)


def store_rows(outs, values):
    rows = outs[0].shape[0]
    for number, out in enumerate(outs):
        out[...] = values[number * rows : (number + 1) * rows, :]


def by_cols_body(parts, rows, *refs):
    store_rows(refs[parts:], low(stripe_dot(rows, refs[:parts])))


def by_cols_pass(rows, weight, parts, blocks, name):
    width = weight.shape[0] // parts
    block = rows.shape[0] // blocks
    return pl.pallas_call(
        functools.partial(by_cols_body, parts),
        grid=(width // STRIPE,),
        out_shape=(low_shape(block, width),) * blocks,
        in_specs=[once(rows.shape), *stripes(weight, parts, 0)],
        out_specs=(pl.BlockSpec((block, STRIPE), lambda step: (0, step)),) * blocks,
        name=name,
        **KERNEL,
    )(rows, *[weight] * parts)


def by_halves(weight):
    return weight.reshape(2, 2, weight.shape[0] // 4, weight.shape[1])


def columns_of(weight):
    def place(step):
        at = jnp.minimum(step, 3)
        return (0, at // 2, 0, at % 2)

    return pl.BlockSpec((2, 1, weight.shape[0] // 4, weight.shape[1] // 2), place)


def column_dot(rows, ref):
    return dot32(rows[...], ref[...].reshape(rows.shape[1], ref.shape[3]))


def hidden_body(gate_w, up_w, *refs):
    normed_p, (hidden_out, gate_slope, up_slope, normed) = refs[:-4], refs[-4:]

    @pl.when(pl.program_id(0) == 0)
    def _():
        join_rows(normed_p, normed)

    gate, up = column_dot(normed, gate_w), column_dot(normed, up_w)
    sig = jax.nn.sigmoid(gate)
    act = gate * sig
    hidden_out[...] = low(act * up)
    gate_slope[...] = low(up * (sig + act * (1.0 - sig)))
    up_slope[...] = low(act)


def hidden_pass(normed_p, gate_w, up_w):
    rows, width = len(normed_p) * normed_p[0].shape[0], normed_p[0].shape[1]
    units = 2 * gate_w.shape[1]
    return pl.pallas_call(
        hidden_body,
        grid=(4,),
        out_shape=(low_shape(rows, units),) * 3,
        in_specs=[columns_of(gate_w), columns_of(up_w)] + [once(v.shape) for v in normed_p],
        out_specs=(pl.BlockSpec((rows, units // 4), lambda step: (0, step)),) * 3,
        scratch_shapes=[pltpu.VMEM((rows, width), jnp.bfloat16)],
        name="hidden_pass",
        **KERNEL,
    )(by_halves(gate_w), by_halves(up_w), *normed_p)


def grad_hidden_body(down_w, gate_slope, up_slope, *refs):
    stripe_refs, refs = refs[:4], refs[4:]
    count = (len(refs) - 4) // 2
    cot_p, (grad_gate_out, grad_up_out, *outs) = refs[:count], refs[count:-2]
    cot, grads = refs[-2:]
    step, chunk = pl.program_id(0), grad_gate_out.shape[1]

    @pl.when(step == 0)
    def _():
        join_rows(cot_p, cot)

    for number in range(4):

        @pl.when(step == number)
        def _(number=number):
            grad_hidden = column_dot(cot, down_w)
            slopes = (gate_slope, up_slope), (grad_gate_out, grad_up_out)
            for part, (slope, out) in enumerate(zip(*slopes)):
                grad = low(grad_hidden * wide(slope[...]))
                out[...] = grad
                start = (4 * part + number) * chunk
                grads[:, start : start + chunk] = grad

    @pl.when(step >= 4)
    def _():
        weight = jnp.concatenate([ref[...] for ref in stripe_refs], axis=1)
        store_rows(outs, low(dot32(grads[...], weight, BY_COLS)))


def grad_hidden_pass(cot_p, gate_slope, up_slope, gate_w, up_w, down_w):
    rows, width = len(cot_p) * cot_p[0].shape[0], cot_p[0].shape[1]
    units = 2 * gate_w.shape[1]
    quarter = pl.BlockSpec((rows, units // 4), lambda step: (0, jnp.minimum(step, 3)))
    stripe = pl.BlockSpec((cot_p[0].shape[0], STRIPE), lambda step: (0, jnp.maximum(step - 4, 0)))
    return pl.pallas_call(
        grad_hidden_body,
        grid=(4 + width // STRIPE,),
        out_shape=(low_shape(rows, units),) * 2 + tuple(low_shape(*v.shape) for v in cot_p),
        in_specs=[columns_of(down_w)]
        + [quarter] * 2
        + stripes(gate_w, 2, 4)
        + stripes(up_w, 2, 4)
        + [once(v.shape) for v in cot_p],
        out_specs=(quarter,) * 2 + (stripe,) * len(cot_p),
        scratch_shapes=[pltpu.VMEM((rows, width), jnp.bfloat16)]
        + [pltpu.VMEM((rows, 2 * units), jnp.bfloat16)],
        name="grad_hidden_pass",
        **KERNEL,
    )(by_halves(down_w), gate_slope, up_slope, gate_w, gate_w, up_w, up_w, *cot_p)


def term_body(*refs):
    pieces, columns, out = refs[:-2], refs[-2], refs[-1]
    rows = jnp.concatenate([piece[...] for piece in pieces], axis=0)
    out[...] = low(dot32(rows, columns[...], BY_ROWS))


def term_half(pieces, columns, part):
    tokens, width = pieces[0].shape
    depth, chunk = width // 2, columns.shape[1] // 2
    return pl.pallas_call(
        term_body,
        grid=(2,),
        out_shape=low_shape(width, chunk),
        in_specs=[pl.BlockSpec((tokens, depth), lambda y: (0, y))] * len(pieces)
        + [pl.BlockSpec((columns.shape[0], chunk), lambda y: (0, part))],
        out_specs=pl.BlockSpec((depth, chunk), lambda y: (y, 0)),
        name="term_half",
        **KERNEL,
    )(*pieces, columns)


def term_pass(pieces, columns, row_parts, col_parts):
    tokens, width = pieces[0].shape
    depth, chunk = width // row_parts, columns.shape[1] // col_parts
    return pl.pallas_call(
        term_body,
        grid=(row_parts, col_parts),
        out_shape=low_shape(width * col_parts, chunk),
        in_specs=[pl.BlockSpec((tokens, depth), lambda y, x: (0, y))] * len(pieces)
        + [pl.BlockSpec((columns.shape[0], chunk), lambda y, x: (0, x))],
        out_specs=pl.BlockSpec((depth, chunk), lambda y, x: (y * col_parts + x, 0)),
        name="term_pass",
        **KERNEL,
    )(*pieces, columns)


def unit_scale(values):
    return lax.rsqrt(jnp.mean(values * values, axis=-1, keepdims=True) + EPSILON)


def norm_pull(values, grad_scaled):
    scale = unit_scale(values)
    mean = jnp.mean(grad_scaled * values, axis=-1, keepdims=True)
    return scale * grad_scaled - values * (scale * scale * scale) * mean


def pick(bit, near, far):
    return jnp.where(bit == 0, near, far)


def to_split(values):
    step = values.shape[1] // 8
    cuts = [values[:, at * step : (at + 1) * step] for at in range(8)]
    return jnp.concatenate(cuts[0::2] + cuts[1::2], axis=1)


def from_split(values):
    step = values.shape[1] // 8
    cuts = [values[:, at * step : (at + 1) * step] for at in range(8)]
    return jnp.concatenate([cut for pair in zip(cuts[:4], cuts[4:]) for cut in pair], axis=1)


def column_sums(*arrays):
    return jnp.concatenate([jnp.sum(v * v, axis=0, keepdims=True) for v in arrays], axis=0)


def summed(parts):
    total = wide(parts[0][...])
    for part in parts[1:]:
        total += wide(part[...])
    return total


def prepare_body(stream_in, cot, normed_out, cot_out):
    rows = wide(stream_in[...])
    normed_out[...] = low(rows * unit_scale(rows))
    cot_out[...] = to_split(cot[...])


def prepare_pass(stream_in, cot):
    return pl.pallas_call(
        prepare_body,
        out_shape=(low_shape(*stream_in.shape), low_shape(*cot.shape)),
        in_specs=[VMEM_SPEC] * 2,
        out_specs=(VMEM_SPEC,) * 2,
        name="prepare_pass",
        **KERNEL,
    )(stream_in, cot)


def middle_body(stream_in, *refs):
    parts, (middle_out, normed_out, squares_out) = refs[:-3], refs[-3:]
    attn_out, rows = summed(parts), wide(stream_in[...])
    middle = rows + attn_out
    middle_out[...] = middle
    normed_out[...] = to_split(low(middle * unit_scale(middle)))
    squares_out[...] = column_sums(rows, attn_out, middle)


def middle_pass(stream_in, parts):
    rows, width = stream_in.shape
    return pl.pallas_call(
        middle_body,
        out_shape=(wide_shape(rows, width), low_shape(rows, width), wide_shape(3, width)),
        in_specs=[VMEM_SPEC] * (1 + len(parts)),
        out_specs=(VMEM_SPEC,) * 3,
        name="middle_pass",
        **KERNEL,
    )(stream_in, *parts)


def final_body(middle, squares_a, *refs):
    parts, (layer_out, sums_out) = refs[:-2], refs[-2:]
    mlp_out = from_split(summed(parts))
    final = middle[...] + mlp_out
    layer_out[...] = low(final)
    squares = jnp.concatenate([squares_a[...], column_sums(mlp_out, final)], axis=0)
    sums = jnp.sum(squares, axis=1, keepdims=True)
    lane = lax.broadcasted_iota(jnp.int32, (1, sums_out.shape[1]), 1)
    total = jnp.zeros((1, sums_out.shape[1]), jnp.float32)
    for number in range(sums.shape[0]):
        total += jnp.where(lane == number, sums[number : number + 1, :], 0.0)
    sums_out[...] = jnp.broadcast_to(total, sums_out.shape)


def final_pass(middle, squares_a, parts, copies):
    rows, width = middle.shape
    return pl.pallas_call(
        final_body,
        out_shape=(low_shape(rows, width), wide_shape(copies, 128)),
        in_specs=[VMEM_SPEC] * (2 + len(parts)),
        out_specs=(VMEM_SPEC,) * 2,
        name="final_pass",
        **KERNEL,
    )(middle, squares_a, *parts)


def grad_middle_body(middle, cot, *refs):
    parts, (grad_out, low_out) = refs[:-2], refs[-2:]
    grad_normed = from_split(summed(parts))
    grad = wide(cot[...]) + norm_pull(middle[...], grad_normed)
    grad_out[...] = grad
    low_out[...] = low(grad)


def grad_middle_pass(middle, cot, parts):
    rows, width = middle.shape
    return pl.pallas_call(
        grad_middle_body,
        out_shape=(wide_shape(rows, width), low_shape(rows, width)),
        in_specs=[VMEM_SPEC] * (2 + len(parts)),
        out_specs=(VMEM_SPEC,) * 2,
        name="grad_middle_pass",
        **KERNEL,
    )(middle, cot, *parts)


def input_grad_body(stream_in, grad_middle, *refs):
    parts, out = refs[:-1], refs[-1]
    out[...] = grad_middle[...] + norm_pull(wide(stream_in[...]), summed(parts))


def input_grad_pass(stream_in, grad_middle, parts):
    return pl.pallas_call(
        input_grad_body,
        out_shape=wide_shape(*stream_in.shape),
        in_specs=[VMEM_SPEC] * (2 + len(parts)),
        out_specs=VMEM_SPEC,
        name="input_grad_pass",
        **KERNEL,
    )(stream_in, grad_middle, *parts)


def stack_groups(out, values):
    rows, chunk = values.shape[0], out.shape[1]
    for number in range(out.shape[0] // rows):
        out[number * rows : (number + 1) * rows, :] = values[:, number * chunk : (number + 1) * chunk]


def pack_body(gain, gate_up, out):
    stack_groups(out, low(wide(gate_up[:, 0, :]) * gain[...]))


def pack_more_body(gain, gate_up, down, up_out, down_out):
    stack_groups(up_out, low(wide(gate_up[:, 1, :]) * gain[...]))
    stack_groups(down_out, down[...])


def pack_pass(body, outs, groups, gain, gate_up, *down):
    rows, chunk = gate_up.shape[0], gate_up.shape[2] // groups
    steps = 2
    per_step = groups // steps
    return pl.pallas_call(
        body,
        grid=(steps,),
        out_shape=(low_shape(groups * rows, chunk),) * outs,
        in_specs=[
            pl.BlockSpec((rows, 1), lambda g: (0, 0)),
            pl.BlockSpec((rows, 2, per_step * chunk), lambda g: (0, 0, g)),
        ]
        + [pl.BlockSpec((rows, per_step * chunk), lambda g: (0, g))] * len(down),
        out_specs=(pl.BlockSpec((per_step * rows, chunk), lambda g: (g, 0)),) * outs,
        name="pack_pass",
        **KERNEL,
    )(gain, gate_up, *down)


def qkv_pack_body(gain, query, key, value, out):
    start = 0
    for part in (query, key, value):
        cut = slice(start, start + part.shape[1])
        rows = low(wide(part[...]) * gain[...])
        for plane in range(out.shape[0]):
            out[plane, 0, :, cut] = rows
        start += part.shape[1]


def qkv_pack_pass(gain, weight, planes, groups):
    rows = weight.shape[0]
    query, rest = H * HD // groups, KV * HD // groups
    first = H * HD // rest
    block = (planes, 1, rows, query + 2 * rest)
    out = pl.pallas_call(
        qkv_pack_body,
        grid=(groups,),
        out_shape=jax.ShapeDtypeStruct((planes, groups, *block[2:]), jnp.bfloat16),
        in_specs=[
            pl.BlockSpec((rows, 1), lambda g: (0, 0)),
            pl.BlockSpec((rows, query), lambda g: (0, g)),
            pl.BlockSpec((rows, rest), lambda g: (0, first + g)),
            pl.BlockSpec((rows, rest), lambda g: (0, first + groups + g)),
        ],
        out_specs=pl.BlockSpec(block, lambda g: (0, g, 0, 0)),
        name="qkv_pack_pass",
        **KERNEL,
    )(gain, weight, weight, weight)
    return out.reshape(-1, block[3])


def unpack_body(gain, weight, gate, up, out, gain_sum):
    gate_term, up_term = wide(gate[...]), wide(up[...])
    out[:, 0, :] = gate_term * gain[...]
    out[:, 1, :] = up_term * gain[...]
    products = gate_term * wide(weight[:, 0, :]) + up_term * wide(weight[:, 1, :])
    total = jnp.sum(products, axis=1, keepdims=True)

    @pl.when(pl.program_id(0) == 0)
    def _():
        gain_sum[...] = total

    @pl.when(pl.program_id(0) > 0)
    def _():
        gain_sum[...] += total


def unpack_pass(gain, weight, gate, up, groups):
    rows, chunk = weight.shape[0], weight.shape[2] // groups
    column = pl.BlockSpec((rows, 1), lambda g: (0, 0))
    pair = pl.BlockSpec((rows, 2, chunk), lambda g: (0, 0, g))
    by_group = pl.BlockSpec((rows, chunk), lambda g: (g, 0))
    return pl.pallas_call(
        unpack_body,
        grid=(groups,),
        out_shape=(jax.ShapeDtypeStruct(weight.shape, jnp.float32), wide_shape(rows, 1)),
        in_specs=[column, pair, by_group, by_group],
        out_specs=(pair, column),
        name="unpack_pass",
        **KERNEL,
    )(gain, weight, gate, up)


def side_by_side_body(part, out):
    out[...] = wide(part[...])


def side_by_side(values, groups):
    rows, cols = values.shape[0] // groups, values.shape[1]
    return pl.pallas_call(
        side_by_side_body,
        grid=(groups,),
        out_shape=wide_shape(rows, groups * cols),
        in_specs=[pl.BlockSpec((rows, cols), lambda g: (g, 0))],
        out_specs=pl.BlockSpec((rows, cols), lambda g: (0, g)),
        name="side_by_side",
        **KERNEL,
    )(values)


def exchange(values, axes):
    return lax.all_to_all(values, axes, split_axis=0, concat_axis=0, tiled=True)


def after(values, *earlier):
    return lax.optimization_barrier((values, *earlier))[0]


def together(*values):
    return lax.optimization_barrier(values)


def swap(values, *axes):
    pairs = SWAP if len(axes) == 1 else DIAGONAL
    return lax.ppermute(values, axes if len(axes) > 1 else axes[0], pairs)


def plane_hop(rows):
    return (rows, swap(rows, "uly"), swap(rows, "yy"), swap(rows, "yy", "uly"))


def plane_back(parts):
    return (parts[0], swap(parts[1], "uly"), swap(parts[2], "yy"), swap(parts[3], "yy", "uly"))


def shift(values, by):
    count = lax.axis_size("dp")
    return lax.ppermute(values, "dp", [(i, (i + by) % count) for i in range(count)])


def column_hop(rows):
    return (rows, *(shift(rows, by) for by in range(1, lax.axis_size("dp"))))


def column_back(parts):
    return (parts[0], *(shift(v, -by) for by, v in enumerate(parts[1:], 1)))


def core_hop(pieces):
    return (*pieces, *(swap(v, "cc") for v in pieces))


def add_body(*refs):
    count = len(refs) // 3
    for left, right, out in zip(refs[:count], refs[count : 2 * count], refs[2 * count :]):
        out[...] = low(wide(left[...]) + wide(right[...]))


def core_back(blocks):
    half = len(blocks) // 2
    arrived = [swap(v, "cc") for v in blocks[half:]]
    return pl.pallas_call(
        add_body,
        out_shape=tuple(low_shape(*v.shape) for v in arrived),
        in_specs=[VMEM_SPEC] * (2 * half),
        out_specs=(VMEM_SPEC,) * half,
        name="add_pass",
        **KERNEL,
    )(*blocks[:half], *arrived)


def plane_plan(
    layer_input,
    span_order,
    qkv_weight,
    out_weight,
    gate_up_weight,
    down_weight,
    attn_gain,
    mlp_gain,
    output_cotangent,
):
    tok = layer_input.shape[0]
    nz = lax.axis_size("dp")
    ndev = lax.axis_size(ALL_AXES)
    plane = ndev // nz
    span_size = tok * plane // span_order.shape[1]
    y_at, c_at, x_at = lax.axis_index("yy"), lax.axis_index("cc"), lax.axis_index("uly")
    q_cols, kv_cols = H * HD // plane, KV * HD // plane
    own_cols = q_cols + 2 * kv_cols
    d_rows = qkv_weight.shape[0]
    mlp_rows, ff_local = down_weight.shape
    hgroups = lax.axis_size(GROUP_AXES)
    hchunk = ff_local // hgroups

    gain_peer = swap(mlp_gain[None, :], "uly")
    gain_own, gain_peer = wide(mlp_gain)[None, :], wide(gain_peer)
    gain_m = pick(
        x_at,
        jnp.concatenate([gain_own, gain_peer], axis=1),
        jnp.concatenate([gain_peer, gain_own], axis=1),
    ).reshape(mlp_rows, 1)
    (gate_rows,) = pack_pass(pack_body, 1, hgroups, gain_m, gate_up_weight)
    out_rows = out_weight.reshape(d_rows, plane, q_cols).transpose(1, 0, 2).reshape(-1, q_cols)
    out_here = exchange(out_rows, PLANE_AXES)
    normed, cot_split = prepare_pass(layer_input, output_cotangent)
    gate_rows, gain_m, out_here, normed, cot_split, qkv_weight, down_weight = together(
        gate_rows, gain_m, out_here, normed, cot_split, qkv_weight, down_weight
    )

    def spread(here):
        return lax.all_gather(here, SIDE_AXES, axis=0, tiled=True)

    wo = lax.all_gather(out_here, "dp", axis=0, tiled=True)
    gate_here = exchange(gate_rows, GROUP_AXES)
    normed_p = plane_hop(normed)
    gain_a = wide(attn_gain)[:, None]
    qkv_rows = qkv_pack_pass(gain_a, qkv_weight, nz, plane)
    up_rows, down_rows = pack_pass(
        pack_more_body, 2, hgroups, gain_m, gate_up_weight, down_weight
    )
    gate_here, normed_p, qkv_rows, up_rows, down_rows, cot_split = together(
        gate_here, normed_p, qkv_rows, up_rows, down_rows, cot_split
    )

    block = jnp.arange(plane, dtype=jnp.int32)
    core_of, y_of, x_of = (block // 4) ^ c_at, (block // 2) % 2 ^ y_at, block % 2 ^ x_at
    stored = (y_of * 2 + core_of) * 2 + x_of
    row_at = (stored[:, None] * tok + jnp.arange(tok, dtype=jnp.int32)[None, :]).reshape(-1)
    positions = sequence_positions(row_at, span_size, span_order[0])
    angles = rope_angles(positions)
    cosine = jnp.concatenate([jnp.cos(angles)] * 2, axis=1)
    sine = jnp.concatenate([-jnp.sin(angles), jnp.sin(angles)], axis=1)
    gate_w = spread(gate_here)
    wq = exchange(qkv_rows, ALL_AXES)
    normed_p = core_hop(normed_p)
    place = positions[::tok] // span_size
    ordered = place[None, :] == block[:, None]
    place = jnp.concatenate([place, jnp.sum(jnp.where(ordered, block[None, :], 0), axis=1)])
    rows_info = (cosine, sine, place)
    wq, normed_p, up_rows, rows_info = together(wq, normed_p, up_rows, rows_info)

    up_here = exchange(up_rows, GROUP_AXES)
    query, key, value, heads = attention_forward(normed_p, wq, *rows_info)
    attn_parts = core_back(by_cols_pass(heads, wo, 1, plane, "out_pass"))
    up_here, attn_parts, down_rows, cot_split = together(
        up_here, attn_parts, down_rows, cot_split
    )

    up_w = spread(up_here)
    down_here = exchange(down_rows, GROUP_AXES)
    attn_parts = plane_back(attn_parts)
    cot_3 = shift(cot_split, 3)
    attn_parts, down_here, cot_3, cot_split = together(attn_parts, down_here, cot_3, cot_split)

    middle, zhat, squares_a = middle_pass(layer_input, attn_parts)
    zhat, down_here = together(zhat, down_here)
    down_w = spread(down_here)
    zhat_p = core_hop(column_hop(zhat))
    zhat_p, gate_w, up_w, cot_split = together(zhat_p, gate_w, up_w, cot_split)

    cot_2 = shift(cot_split, 2)
    hidden, gate_slope, up_slope = hidden_pass(zhat_p, gate_w, up_w)
    hidden, cot_2, cot_split, gate_slope, down_w = together(
        hidden, cot_2, cot_split, gate_slope, down_w
    )

    cot_p = core_hop((cot_split, shift(cot_split, 1), cot_2, cot_3))
    mlp_parts = core_back(by_cols_pass(hidden, down_w, 2, 2 * nz, "down_pass"))
    cot_p, mlp_parts = together(cot_p, mlp_parts)
    mlp_1 = shift(mlp_parts[1], -1)
    down_t = term_pass(cot_p, hidden, 2, 2)
    mlp_1, mlp_parts, down_t = together(mlp_1, mlp_parts, down_t)

    def side_sum(term):
        return lax.psum_scatter(term, SIDE_AXES, scatter_dimension=0, tiled=True)

    down_t = side_sum(down_t)
    mlp_2 = shift(mlp_parts[2], -2)
    grad_gate, grad_up, *gz_parts = grad_hidden_pass(
        cot_p, gate_slope, up_slope, gate_w, up_w, down_w
    )
    gz_parts, grad_gate, mlp_2, mlp_parts = together(gz_parts, grad_gate, mlp_2, mlp_parts)

    gz_parts = core_back(gz_parts)
    mlp_3 = shift(mlp_parts[3], -3)
    gate_t = term_pass(zhat_p, grad_gate, 2, 2)
    gz_parts, gate_t, mlp_3, mlp_parts = together(gz_parts, gate_t, mlp_3, mlp_parts)

    gate_t = side_sum(gate_t)
    gz_parts = column_back(gz_parts)
    up_t = term_pass(zhat_p, grad_up, 2, 2)
    mlp_parts = (mlp_parts[0], mlp_1, mlp_2, mlp_3)
    layer_output, lanes = final_pass(middle, squares_a, mlp_parts, ndev)
    gathered = exchange(lanes, ALL_AXES)
    gz_parts, up_t, down_t, gathered = together(gz_parts, up_t, down_t, gathered)

    down_back = exchange(down_t, GROUP_AXES)
    grad_middle, grad_out = grad_middle_pass(middle, output_cotangent, gz_parts)
    grad_out_p = plane_hop(grad_out)
    grad_out_p, gate_t, down_back, up_t = together(grad_out_p, gate_t, down_back, up_t)
    grad_out_p, gate_t, up_t = together(core_hop(grad_out_p), gate_t, up_t)

    up_t = side_sum(up_t)
    gate_back = exchange(gate_t, GROUP_AXES)
    grad_qkv = attention_backward(grad_out_p, wo, query, key, value, *rows_info)
    gx_parts = core_back(by_cols_pass(grad_qkv, wq, 1, plane, "qkv_back_pass"))
    query_term = term_half(normed_p, grad_qkv, 0)
    gx_parts, query_term, grad_qkv, gate_back, down_back, heads = together(
        gx_parts, query_term, grad_qkv, gate_back, down_back, heads
    )

    query_sum = exchange(query_term, ALL_AXES)
    rest_term = term_half(normed_p, grad_qkv, 1)
    out_term = term_pass(grad_out_p, heads, 2, 1)
    down_grad = side_by_side(down_back, hgroups)
    query_sum, up_t, out_term, down_grad, rest_term, gx_parts = together(
        query_sum, up_t, out_term, down_grad, rest_term, gx_parts
    )

    out_term = lax.psum_scatter(out_term, "dp", scatter_dimension=0, tiled=True)
    up_back = exchange(up_t, GROUP_AXES)
    gx_parts = plane_back(gx_parts)

    def plane_sum(arrived):
        parts = wide(arrived.reshape(nz, plane, d_rows, arrived.shape[1]))
        return jnp.sum(parts, axis=0).transpose(1, 0, 2)

    query_sum = plane_sum(query_sum).reshape(d_rows, -1)
    up_back, gx_parts, rest_term, query_sum = together(up_back, gx_parts, rest_term, query_sum)

    rest_sum = exchange(rest_term, ALL_AXES)
    input_grad = input_grad_pass(layer_input, grad_middle, gx_parts)
    gate_up_grad, gain_sum = unpack_pass(gain_m, gate_up_weight, gate_back, up_back, hgroups)
    rest_sum, input_grad, gate_up_grad, gain_sum, out_term = together(
        rest_sum, input_grad, gate_up_grad, gain_sum, out_term
    )
    out_sum = exchange(out_term, PLANE_AXES)

    rest_sum = plane_sum(rest_sum)
    qkv_sum = jnp.concatenate(
        [
            query_sum,
            rest_sum[:, :, :kv_cols].reshape(d_rows, -1),
            rest_sum[:, :, kv_cols:].reshape(d_rows, -1),
        ],
        axis=1,
    )
    qkv_grad = qkv_sum * gain_a
    attn_gain_grad = jnp.sum(qkv_sum * wide(qkv_weight), axis=1)
    gain_halves = gain_sum.reshape(2, -1)
    gain_keep = jnp.where(x_at == 0, gain_halves[0], gain_halves[1])
    gain_send = jnp.where(x_at == 0, gain_halves[1], gain_halves[0])
    mlp_gain_grad = gain_keep + swap(gain_send[None, :], "uly")[0]

    out_sum = wide(out_sum).reshape(plane, d_rows, q_cols).transpose(1, 0, 2)
    out_weight_grad = out_sum.reshape(d_rows, -1)
    rms_values = jnp.sqrt(jnp.sum(gathered, axis=0)[:5] / (tok * ndev * D))
    return (
        layer_output,
        input_grad,
        qkv_grad,
        out_weight_grad,
        gate_up_grad,
        down_grad,
        attn_gain_grad,
        mlp_gain_grad,
        rms_values,
    )


def solution(mesh):
    sizes = dict(mesh.shape)
    if sizes["blk"] == 4 and sizes["uly"] == 2:
        mesh = Mesh(mesh.devices.reshape(sizes["dp"], 2, 2, 2), ALL_AXES)
        body, blk = plane_plan, ("yy", "cc")
    else:
        body, blk = general_plan, ("blk",)
    every = ("dp", *blk, "uly")
    rows = ("dp", *blk)
    return jax.shard_map(
        body,
        mesh=mesh,
        in_specs=(
            P(every, None),
            P("dp", None),
            P(every, None),
            P(every, None),
            P(rows, None, "uly"),
            P(rows, "uly"),
            P(every),
            P(every),
            P(every, None),
        ),
        out_specs=(
            P(every, None),
            P(every, None),
            P(every, None),
            P(every, None),
            P(rows, None, "uly"),
            P(rows, "uly"),
            P(every),
            P(every),
            P(),
        ),
        check_vma=False,
    )
```
